32 devices in a mesh: dp: 8 (over y, x, core), mp: 4 (over z).
Axes of the slice: x: 2, y: 2, z: 4, core: 2. Of those that a mesh axis runs over, the one named last changes fastest.
Arguments:
- tokens: bfloat16 [8, 1536, 768], P('dp'), may hold values from -6 to 6
- lengths: int32 [8, 8], P('dp'), may hold values from 1 to 512, 1536 in all within a row
- query_weight: float32 [768, 768], P('dp', 'mp'), may hold values from -0.3125 to 0.3125
- key_weight: float32 [768, 768], P('dp', 'mp'), may hold values from -0.3125 to 0.3125
- value_weight: float32 [768, 768], P('dp', 'mp'), may hold values from -0.21875 to 0.21875
- out_weight: float32 [768, 768], P('mp', 'dp'), may hold values from -0.875 to 0.875
- attn_gain: float32 [768], P('dp'), may hold values from 0.1 to 1.9
- gate_weight: float32 [768, 2048], P('dp', 'mp'), may hold values from -0.21875 to 0.21875
- up_weight: float32 [768, 2048], P('dp', 'mp'), may hold values from -0.21875 to 0.21875
- down_weight: float32 [2048, 768], P('mp', 'dp'), may hold values from -0.1875 to 0.1875
- ffn_gain: float32 [768], P('dp'), may hold values from 0.1 to 1.9
- cotangent: bfloat16 [8, 1536, 768], P('dp'), may hold values from -6 to 6
Outputs:
- output: bfloat16 [8, 1536, 768], P('dp')
- grad_tokens: float32 [8, 1536, 768], P('dp')
- grad_query: float32 [768, 768], P('dp', 'mp')
- grad_key: float32 [768, 768], P('dp', 'mp')
- grad_value: float32 [768, 768], P('dp', 'mp')
- grad_out: float32 [768, 768], P('mp', 'dp')
- grad_attn_gain: float32 [768], P('dp')
- grad_gate: float32 [768, 2048], P('dp', 'mp')
- grad_up: float32 [768, 2048], P('dp', 'mp')
- grad_down: float32 [2048, 768], P('mp', 'dp')
- grad_ffn_gain: float32 [768], P('dp')
The draws below stay inside these ranges and needn't reach their ends.
Inputs may be any that keep to these rules, and one draw needn't show every extreme that they name: Each row's lengths add up to 1536; the longest segment of a row has 512 positions.
All inputs are finite; a program needn't handle non-finite values.
Results may differ from the reference program's by a relative error of at most 0.014.
The reference program's roundings to bfloat16 on the way count: a program that leaves them out, or rounds other values in their place, can miss the bound.
Values may be sent and summed in bfloat16 or wider, within the bound.
A program may use at most 192 MiB of HBM per device.

```python
import math
import jax
import jax.numpy as jnp
import numpy as np
from jax import lax

D = 768
HD = 64
FF = 2048
SEQ = 1536
NSEG = 8
MOST = 512
ROWS = 8


def with_spikes(array, rng, source, target, parts, factor):
    owner, partner = [(jnp.arange(array.shape[axis_at]) // (array.shape[axis_at] // parts)).reshape([-1 if axis == axis_at else 1 for axis in range(array.ndim)]) for axis_at in (source, target)]
    chosen = jax.random.permutation(rng, parts)[partner]
    strong = (owner == chosen) | (owner == (partner + parts // 2) % parts)
    return jnp.where(strong, factor * array, array)


def shard_levels(stream_key, dims, shards, smallest, largest):
    loudness = 1.0
    for axis_at, shards_of in shards:
        heights = jax.random.uniform(jax.random.fold_in(jax.random.fold_in(stream_key, 6), axis_at), (shards_of,), jnp.float32, smallest / len(shards), largest / len(shards))
        loudness = loudness * jnp.repeat(jnp.exp(heights), dims[axis_at] // shards_of).reshape((-1,) + (1,) * (len(dims) - 1 - axis_at))
    return loudness


def split_up(amount, total, most, slope):
    portions = [(1 << 20) // math.isqrt(standing ** slope) + 1 for standing in range(2, amount + 1)]
    spare, holding = total - most - (amount - 1), [1] * (amount - 1)
    while spare > 0:
        movable = [i for i in range(amount - 1) if holding[i] < most]
        whole, budget = sum([portions[i] for i in movable]), spare
        for i in movable:
            more = min(most - holding[i], max(1, budget * portions[i] // whole), spare)
            holding[i] = holding[i] + more
            spare = spare - more
    return np.array([most] + holding)


def uneven(stream_key, count, total, most, lean):
    if count == 2:
        one = jax.random.randint(stream_key, (), max(1, total - most), min(most, total - 1) + 1)
        return jnp.stack([one, total - one])
    sizes = jnp.asarray(split_up(count, total, most, lean), jnp.int32)
    twos = (count - 1) // 2
    giver, sink = sizes[1:1 + 2 * twos:2], sizes[2:2 + 2 * twos:2]
    margin = jnp.minimum(giver - 1, most - sink)
    passed = jax.random.randint(jax.random.fold_in(stream_key, 1), (twos,), 0, 1 << 20) % (margin + 1)
    sizes = sizes.at[1:1 + 2 * twos:2].set(giver - passed).at[2:2 + 2 * twos:2].set(sink + passed)
    return sizes[jax.random.permutation(jax.random.fold_in(stream_key, 2), count)]


def normal_values(rng, extent, scale, limit, pieces=(), kind=jnp.bfloat16):
    drawn = jax.random.normal(rng, extent, jnp.float32) * scale
    if len(pieces) > 0:
        drawn = shard_levels(rng, extent, pieces, -0.22, 0.18) * drawn
    return jnp.clip(drawn, min=-limit, max=limit).astype(kind)


def noise_with(key, shape, width, bound, split, heavy, kind=jnp.bfloat16):
    values = width * jax.random.normal(key, shape, jnp.float32)
    if split:
        values = values * shard_levels(key, shape, split, -0.22, 0.18)
    return jnp.clip(with_spikes(values, jax.random.fold_in(key, 3), *heavy), -bound, bound).astype(kind)


def setup_inputs(seed: int = 0) -> dict:
    arg_keys = jax.random.split(jax.random.key(seed), 13)
    return {
        "tokens": noise_with(arg_keys[0], (ROWS, SEQ, D), 1.0, 6.0, ((0, 8),), (0, 2, 8, 2.0)),
        "lengths": jax.vmap(lambda own: uneven(own, NSEG, SEQ, MOST, 2))(jax.random.split(arg_keys[1], ROWS)).reshape((ROWS, NSEG)).astype(jnp.int32),
        "query_weight": normal_values(arg_keys[2], (D, D), (D // 2) ** -0.5, 0.3125, ((0, 8), (1, 4)), jnp.float32),
        "key_weight": normal_values(arg_keys[3], (D, D), (D // 2) ** -0.5, 0.3125, ((0, 8), (1, 4)), jnp.float32),
        "value_weight": normal_values(arg_keys[4], (D, D), D ** -0.5, 0.21875, ((0, 8), (1, 4)), jnp.float32),
        "out_weight": normal_values(arg_keys[5], (D, D), (D // 16) ** -0.5, 0.875, ((0, 4), (1, 8)), jnp.float32),
        "attn_gain": jnp.clip(1.0 + 0.18 * jax.random.normal(arg_keys[6], (D,), jnp.float32), 0.1, 1.9),
        "gate_weight": normal_values(arg_keys[7], (D, FF), D ** -0.5, 0.21875, ((0, 8), (1, 4)), jnp.float32),
        "up_weight": normal_values(arg_keys[8], (D, FF), D ** -0.5, 0.21875, ((0, 8), (1, 4)), jnp.float32),
        "down_weight": normal_values(arg_keys[9], (FF, D), (FF // 2) ** -0.5, 0.1875, ((0, 4), (1, 8)), jnp.float32),
        "ffn_gain": jnp.clip(1.0 + 0.18 * jax.random.normal(arg_keys[10], (D,), jnp.float32), 0.1, 1.9),
        "cotangent": noise_with(arg_keys[11], (ROWS, SEQ, D), 1.0, 6.0, ((0, 8),), (0, 2, 8, 2.0)),
    }


EPSILON = 1e-06
GELU_COEF = 0.7978845608028654
HIGHEST = lax.Precision.HIGHEST

@jax.custom_vjp
def low(v):
    return lax.optimization_barrier(v.astype(jnp.bfloat16)).astype(jnp.float32)

@jax.custom_vjp
def low_back(v):
    return v

def low_keep(v):
    return (low(v), None)

def low_pass(kept, grad):
    return (grad,)

def back_keep(v):
    return (v, None)

def back_low(kept, grad):
    return (low(grad),)
low.defvjp(low_keep, low_pass)
low_back.defvjp(back_keep, back_low)

def rms_scale(values, gain):
    return values * lax.rsqrt(lax.optimization_barrier(jnp.mean(values * values, axis=-1, keepdims=True)) + EPSILON) * gain

def gelu_tanh(values):
    return 0.5 * values * (1.0 + jnp.tanh(GELU_COEF * (values + 0.044715 * values * values * values)))

def matmul(left, right):
    return jnp.dot(left, right, precision=HIGHEST)

def segment_numbers(lengths):
    ends = jnp.cumsum(lengths, axis=1)
    places = jnp.arange(SEQ, dtype=jnp.int32)
    return lax.optimization_barrier(jnp.sum((ends[:, None, :] <= places[None, :, None]).astype(jnp.int32), axis=2))

def row_layer(params, row_input, segment_row):
    full_query, full_key, full_value, full_out, gain_attn, full_gate, full_up, full_down, gain_ffn = params
    normed = low(rms_scale(row_input, gain_attn))
    query = low(low_back(matmul(normed, full_query)))
    keys = low(low_back(matmul(normed, full_key)))
    values = low(low_back(matmul(normed, full_value)))
    heads = D // HD
    query4 = query.reshape(SEQ, heads, HD)
    keys4 = keys.reshape(SEQ, heads, HD)
    values4 = values.reshape(SEQ, heads, HD)
    block = min(512, SEQ)
    scale = HD ** (-0.5)

    def attend(index):
        begin = index * block
        query_block = lax.dynamic_slice_in_dim(query4, begin, block, 0)
        segment_block = lax.dynamic_slice_in_dim(segment_row, begin, block, 0)
        scores = low_back(jnp.einsum('qhd,khd->hqk', query_block, keys4, precision=HIGHEST) * scale)
        same = segment_block[:, None] == segment_row[None, :]
        scores = jnp.where(same[None], scores, -1e+30)
        totals = jax.nn.logsumexp(scores, axis=-1, keepdims=True)
        attention = low(jnp.exp(scores - totals))
        return jnp.einsum('hqk,khd->qhd', attention, values4, precision=HIGHEST)
    mixed = lax.map(jax.checkpoint(attend), jnp.arange(SEQ // block, dtype=jnp.int32))
    attended = low(low_back(mixed.reshape(SEQ, D)))
    hidden = row_input + low_back(matmul(attended, full_out))
    normed_ffn = low(rms_scale(hidden, gain_ffn))
    gate = low_back(matmul(normed_ffn, full_gate))
    upward = low_back(matmul(normed_ffn, full_up))
    inner = low(gelu_tanh(gate) * upward)
    return hidden + low_back(matmul(inner, full_down))

def reference(tokens, lengths, query_weight, key_weight, value_weight, out_weight, attn_gain, gate_weight, up_weight, down_weight, ffn_gain, cotangent):
    inputs = tokens.astype(jnp.float32)
    upstream = cotangent.astype(jnp.float32)
    segment = segment_numbers(lengths)

    def forward(inputs, query_weight, key_weight, value_weight, out_weight, attn_gain, gate_weight, up_weight, down_weight, ffn_gain):
        params = tuple((low(weight) for weight in (query_weight, key_weight, value_weight, out_weight, attn_gain, gate_weight, up_weight, down_weight, ffn_gain)))
        layer = jax.checkpoint(row_layer)

        def step(carry, item):
            return (carry, layer(params, item[0], item[1]))
        _, outputs = lax.scan(step, None, (inputs, segment))
        return outputs
    outputs, pullback = jax.vjp(forward, inputs, query_weight, key_weight, value_weight, out_weight, attn_gain, gate_weight, up_weight, down_weight, ffn_gain)
    grads = pullback(upstream)
    return (outputs.astype(jnp.bfloat16), grads[0], grads[1], grads[2], grads[3], grads[4], grads[5], grads[6], grads[7], grads[8], grads[9])
```

```python
import functools
import jax
import jax.numpy as jnp
from jax import lax
from jax.experimental import pallas as pl
from jax.experimental.pallas import tpu as pltpu
from jax.sharding import PartitionSpec as P

EPSILON = 1e-06
GELU_COEF = 0.7978845608028654
GELU_CUBE = 0.044715
CAP = 512
NEG = -1e30
F32 = jnp.float32
BF16 = jnp.bfloat16


def nn(a, b):
    return lax.dot_general(a, b, (((1,), (0,)), ((), ())), preferred_element_type=F32)


def nt(a, b):
    return lax.dot_general(a, b, (((1,), (1,)), ((), ())), preferred_element_type=F32)


def tn(a, b):
    return lax.dot_general(a, b, (((0,), (0,)), ((), ())), preferred_element_type=F32)


def placement(len_ref, bins):
    count = len_ref.shape[1]
    sizes = [len_ref[0, i] for i in range(count)]
    starts = [jnp.int32(0)]
    for i in range(count - 1):
        starts.append(starts[-1] + sizes[i])
    ranks = []
    for i in range(count):
        rank = jnp.int32(0)
        for j in range(count):
            if j < i:
                rank = rank + jnp.where(sizes[j] >= sizes[i], 1, 0)
            elif j > i:
                rank = rank + jnp.where(sizes[j] > sizes[i], 1, 0)
        ranks.append(rank)
    fills = [jnp.int32(0)] * (bins - 1)
    spots = [jnp.int32(0)] * count
    for k in range(count):
        size = jnp.int32(0)
        for i in range(count):
            size = size + jnp.where(ranks[i] == k, sizes[i], 0)
        if k == 0:
            spot = jnp.int32((bins - 1) * CAP)
        else:
            free = jnp.int32(1)
            spot = jnp.int32(0)
            for b in range(bins - 1):
                fits = jnp.where(fills[b] + size <= CAP, free, 0) if b < bins - 2 else free
                spot = spot + fits * (b * CAP + fills[b])
                fills[b] = fills[b] + fits * size
                free = free - fits
        for i in range(count):
            spots[i] = spots[i] + jnp.where(ranks[i] == k, spot, 0)
    return starts, sizes, spots


def packed_source(place, first, shape, axis):
    spot = lax.broadcasted_iota(jnp.int32, shape, axis) + first
    source = jnp.full(shape, -1, jnp.int32)
    segment = jnp.full(shape, -1, jnp.int32)
    for i, (start, size, at) in enumerate(zip(*place)):
        here = (spot >= at) & (spot < at + size)
        source = jnp.where(here, spot + (start - at), source)
        segment = jnp.where(here, i, segment)
    return source, segment


def low_lanes():
    return lax.broadcasted_iota(jnp.int32, (1, 128), 1) < 64


def half(tile, low):
    lanes = low_lanes()
    return jnp.where(lanes if low else jnp.logical_not(lanes), tile, jnp.zeros_like(tile))


HEADS = ((0, 2, 4, True), (0, 2, 4, False), (1, 3, 5, True))


def tile_of(ref, m, t, rows=slice(None)):
    return ref[m, rows, 128 * t : 128 * (t + 1)]


def attend_group(qkv, m, bias, o_ref, at, lse_ref=None, qb=256):
    def rows_body(i, carry):
        rows = pl.ds(pl.multiple_of(i * qb, qb), qb)
        sums = [None, None]
        for head, (tq, tk, tv, low) in enumerate(HEADS):
            q = half(qkv[m, rows, 128 * tq : 128 * (tq + 1)], low) * jnp.asarray(0.125, BF16)
            s = nt(q, tile_of(qkv, m, tk)) + bias[rows, :]
            top = jnp.max(s, axis=1, keepdims=True)
            e = jnp.exp(s - top)
            total = jnp.sum(e, axis=1, keepdims=True)
            p = (e * (1.0 / total)).astype(BF16)
            o = nn(p, half(tile_of(qkv, m, tv), low))
            j = 0 if head < 2 else 1
            sums[j] = o if sums[j] is None else sums[j] + o
            if lse_ref is not None:
                lane = lax.broadcasted_iota(jnp.int32, (1, 128), 1)
                lse_ref[rows, :] = jnp.where(lane == 3 * m + head, top + jnp.log(total), lse_ref[rows, :])
        o_ref[at, rows, 0:128] = sums[0].astype(BF16)
        o_ref[at, rows, 128:256] = sums[1].astype(BF16)
        return carry

    lax.fori_loop(0, CAP // qb, rows_body, 0)


def attend_group_back(qkv, m, bias, lse_t, do_ref, dqkv, qb=256):
    dk = [None, None]
    dv = [None, None]
    dq = [[None] * (CAP // qb), [None] * (CAP // qb)]
    for head, (tq, tk, tv, low) in enumerate(HEADS):
        j = 0 if head < 2 else 1
        k = half(tile_of(qkv, m, tk), low) * jnp.asarray(0.125, BF16)
        v = half(tile_of(qkv, m, tv), low)
        lse = lse_t[pl.ds(3 * m + head, 1), :]
        for i in range(CAP // qb):
            rows = slice(i * qb, (i + 1) * qb)
            q = tile_of(qkv, m, tq, rows)
            do = do_ref[m, rows, 128 * j : 128 * (j + 1)]
            p = jnp.exp(nt(k, q) + bias[:, rows] - lse[:, rows])
            dp = nt(v, do)
            delta = jnp.sum(p * dp, axis=0, keepdims=True)
            ds = (p * (dp - delta)).astype(BF16)
            dv_part = nn(p.astype(BF16), half(do, low))
            dk_part = nn(ds, half(q, low) * jnp.asarray(0.125, BF16))
            dq_part = tn(ds, k)
            dv[j] = dv_part if dv[j] is None else dv[j] + dv_part
            dk[j] = dk_part if dk[j] is None else dk[j] + dk_part
            dq[j][i] = dq_part if dq[j][i] is None else dq[j][i] + dq_part
    for j in range(2):
        for i in range(CAP // qb):
            dqkv[m, i * qb : (i + 1) * qb, 128 * j : 128 * (j + 1)] = dq[j][i].astype(BF16)
        dqkv[m, :, 128 * (2 + j) : 128 * (3 + j)] = dk[j].astype(BF16)
        dqkv[m, :, 128 * (4 + j) : 128 * (5 + j)] = dv[j].astype(BF16)


def out_weight_tiles(w, m):
    lanes = low_lanes()
    t1 = tile_of(w, m, 1).astype(F32)
    t3 = tile_of(w, m, 3).astype(F32)
    t5 = tile_of(w, m, 5).astype(F32)
    first = jnp.where(lanes, pltpu.roll(t1, 64, 1), t3)
    second = jnp.where(lanes, pltpu.roll(t5, 64, 1), 0.0)
    return first.astype(BF16), second.astype(BF16)


def gelu_parts(a):
    inner = GELU_COEF * (a + GELU_CUBE * a * a * a)
    t = jnp.tanh(inner)
    return t


def rms_rows(values):
    return lax.rsqrt(jnp.mean(values * values, axis=1, keepdims=True) + EPSILON)


def layer_kernel(
    len_ref, x_ref, dy_ref, w_ref, gain_ref, which_ref,
    out_ref, gt_ref, g_ref, gg_ref,
    bias, xp, dyp, n1, n1t, n2, n2t, dypt, dhbt, qkv, o_all, wo, lse, lse_t, do, dqkv, h, acc,
):
    bins = w_ref.shape[0]
    seq = x_ref.shape[0]
    place = placement(len_ref, bins)
    me = which_ref[0]
    g1 = gain_ref[0:1, :]
    g2 = gain_ref[1:2, :]

    def wo_body(m, c):
        first, second = out_weight_tiles(w_ref, m)
        wo[m, :, 0:128] = first
        wo[m, :, 128:256] = second
        return c

    lax.fori_loop(0, bins, wo_body, 0)
    lse[...] = jnp.zeros_like(lse)

    def forward(b):
        source, segment = packed_source(place, b * CAP, (CAP, 1), 0)
        _, segment_row = packed_source(place, b * CAP, (1, CAP), 1)
        bias[...] = jnp.where(segment == segment_row, 0.0, NEG)
        pick = (source == lax.broadcasted_iota(jnp.int32, (CAP, seq), 1)).astype(BF16)
        xb = nn(pick, x_ref[...])
        xp[...] = xb.astype(BF16)
        dyp[...] = nn(pick, dy_ref[...]).astype(BF16)
        n1[...] = (xb * rms_rows(xb) * g1).astype(BF16)
        h[...] = xb

        def m_body(m, c):
            qkv[m] = nn(n1[...], w_ref[m, :, 0:768]).astype(BF16)
            attend_group(qkv, m, bias, o_all, m, lse)
            h[...] += nt(o_all[m], wo[m])
            return c

        lax.fori_loop(0, bins, m_body, 0)
        hb = h[...]
        n2[...] = (hb * rms_rows(hb) * g2).astype(BF16)

    def ffn_out(b):
        acc[...] = h[...]

        def m_body(m, c):
            a = nn(n2[...], w_ref[m, :, 768:1280])
            up = nn(n2[...], w_ref[m, :, 1280:1792])
            u = (0.5 * a * (1.0 + gelu_parts(a)) * up).astype(BF16)
            acc[...] += nt(u, w_ref[m, :, 1792:2304])
            return c

        lax.fori_loop(0, bins, m_body, 0)
        source, _ = packed_source(place, b * CAP, (1, CAP), 1)
        drop = (lax.broadcasted_iota(jnp.int32, (seq, CAP), 0) == source).astype(BF16)
        out_ref[...] = (out_ref[...].astype(F32) + nn(drop, acc[...].astype(BF16))).astype(BF16)

    out_ref[...] = jnp.zeros_like(out_ref)

    def others(i, c):
        b = lax.rem(me + 1 + i, bins)
        forward(b)
        ffn_out(b)
        return c

    lax.fori_loop(0, bins, others, 0)

    n1t[...] = n1[...].T
    n2t[...] = n2[...].T
    dypt[...] = dyp[...].T
    lse_t[...] = lse[...].T
    acc[...] = jnp.zeros_like(acc)

    def ffn_back(m, c):
        a = nn(n2[...], w_ref[m, :, 768:1280])
        up = nn(n2[...], w_ref[m, :, 1280:1792])
        t = gelu_parts(a)
        gel = 0.5 * a * (1.0 + t)
        u = (gel * up).astype(BF16)
        du = nn(dyp[...], w_ref[m, :, 1792:2304])
        slope = 0.5 * (1.0 + t) + 0.5 * a * (1.0 - t * t) * (GELU_COEF * (1.0 + 3.0 * GELU_CUBE * a * a))
        da = (du * up * slope).astype(BF16)
        db = (du * gel).astype(BF16)
        g_ref[m, :, 1792:2304] = nn(dypt[...], u).astype(BF16)
        g_ref[m, :, 768:1280] = nn(n2t[...], da).astype(BF16)
        g_ref[m, :, 1280:1792] = nn(n2t[...], db).astype(BF16)
        acc[...] += nt(da, w_ref[m, :, 768:1280]) + nt(db, w_ref[m, :, 1280:1792])
        return c

    lax.fori_loop(0, bins, ffn_back, 0)
    hb = h[...]
    r2 = rms_rows(hb)
    dn2 = acc[...]
    gg_ffn = jnp.sum(dn2 * hb * r2, axis=0, keepdims=True)
    wg = dn2 * g2
    dh = dyp[...].astype(F32) + r2 * wg - hb * (r2 * r2 * r2) * jnp.mean(wg * hb, axis=1, keepdims=True)
    h[...] = dh
    dhb = dh.astype(BF16)
    dhbt[...] = dhb.T
    n2[...] = dhb
    acc[...] = jnp.zeros_like(acc)

    def attn_back(m, c):
        do[m] = nn(n2[...], wo[m]).astype(BF16)
        attend_group_back(qkv, m, bias, lse_t, do, dqkv)
        acc[...] += nt(dqkv[m], w_ref[m, :, 0:768])
        grad = nn(n1t[...], dqkv[m])
        go = nn(dhbt[...], o_all[m])
        lanes = low_lanes()
        for t in range(6):
            g = grad[:, 128 * t : 128 * (t + 1)]
            if t == 1:
                g = jnp.where(lanes, g, pltpu.roll(go[:, 0:128], 64, 1))
            elif t == 3:
                g = jnp.where(lanes, g, go[:, 0:128])
            elif t == 5:
                g = jnp.where(lanes, g, pltpu.roll(go[:, 128:256], 64, 1))
            g_ref[m, :, 128 * t : 128 * (t + 1)] = g.astype(BF16)
        return c

    lax.fori_loop(0, bins, attn_back, 0)
    xb = xp[...].astype(F32)
    r1 = rms_rows(xb)
    dn1 = acc[...]
    gg_attn = jnp.sum(dn1 * xb * r1, axis=0, keepdims=True)
    wa = dn1 * g1
    gt = h[...] + r1 * wa - xb * (r1 * r1 * r1) * jnp.mean(wa * xb, axis=1, keepdims=True)
    gt_ref[...] = gt.astype(BF16)
    gg_ref[0:1, :] = gg_attn
    gg_ref[1:2, :] = gg_ffn


def unpack_kernel(len_ref, gt_ref, out_ref):
    bins = gt_ref.shape[0]
    seq = out_ref.shape[0]
    place = placement(len_ref, bins)
    total = jnp.zeros(out_ref.shape, F32)
    for b in range(bins):
        source, _ = packed_source(place, b * CAP, (1, CAP), 1)
        drop = (lax.broadcasted_iota(jnp.int32, (seq, CAP), 0) == source).astype(BF16)
        total = total + nn(drop, gt_ref[b])
    out_ref[...] = total


def per_device(
    tokens, lengths, query_weight, key_weight, value_weight, out_weight, attn_gain, gate_weight, up_weight, down_weight,
    ffn_gain, cotangent,
):
    rows, seq, width = tokens.shape
    bins = lax.axis_size("mp")
    q, k, v, o = (w.astype(BF16) for w in (query_weight, key_weight, value_weight, out_weight.T))
    package = jnp.concatenate(
        [q, o[:, 0:64], k, o[:, 64:128], v, o[:, 128:192], gate_weight.astype(BF16), up_weight.astype(BF16),
         down_weight.T.astype(BF16)], axis=1)
    w = lax.all_gather(lax.all_gather(package, "dp", axis=0, tiled=True), "mp", axis=0)
    gains = jnp.stack([attn_gain, ffn_gain]).astype(BF16)
    gains = lax.all_gather(gains, "dp", axis=1, tiled=True).astype(F32)
    gains = jnp.concatenate([gains, jnp.zeros((6, width), F32)], axis=0)
    which = lax.axis_index("mp").astype(jnp.int32).reshape(1)
    vmem = pl.BlockSpec(memory_space=pltpu.VMEM)
    smem = pl.BlockSpec(memory_space=pltpu.SMEM)
    group = w.shape[2]
    x = tokens.reshape(seq, width)
    dy = cotangent.reshape(seq, width)
    out, gt, g, gg = pl.pallas_call(
        layer_kernel,
        out_shape=(
            jax.ShapeDtypeStruct((seq, width), BF16),
            jax.ShapeDtypeStruct((CAP, width), BF16),
            jax.ShapeDtypeStruct((bins, width, group), BF16),
            jax.ShapeDtypeStruct((8, width), F32),
        ),
        in_specs=[smem, vmem, vmem, vmem, vmem, smem],
        out_specs=[vmem] * 4,
        scratch_shapes=[
            pltpu.VMEM((CAP, CAP), F32),
            pltpu.VMEM((CAP, width), BF16),
            pltpu.VMEM((CAP, width), BF16),
            pltpu.VMEM((CAP, width), BF16),
            pltpu.VMEM((width, CAP), BF16),
            pltpu.VMEM((CAP, width), BF16),
            pltpu.VMEM((width, CAP), BF16),
            pltpu.VMEM((width, CAP), BF16),
            pltpu.VMEM((width, CAP), BF16),
            pltpu.VMEM((bins, CAP, width), BF16),
            pltpu.VMEM((bins, CAP, 256), BF16),
            pltpu.VMEM((bins, width, 256), BF16),
            pltpu.VMEM((CAP, 128), F32),
            pltpu.VMEM((128, CAP), F32),
            pltpu.VMEM((bins, CAP, 256), BF16),
            pltpu.VMEM((bins, CAP, width), BF16),
            pltpu.VMEM((CAP, width), F32),
            pltpu.VMEM((CAP, width), F32),
        ],
        compiler_params=pltpu.CompilerParams(vmem_limit_bytes=63 * 2**20+900000),
        name="layer",
    )(lengths, x, dy, w, gains, which)
    gt_all = lax.all_gather(gt, "mp", axis=0)
    grad_tokens = pl.pallas_call(
        unpack_kernel,
        out_shape=jax.ShapeDtypeStruct((seq, width), F32),
        in_specs=[smem, vmem],
        out_specs=vmem,
        compiler_params=pltpu.CompilerParams(vmem_limit_bytes=60 * 2**20),
        name="unpack",
    )(lengths, gt_all)
    g = lax.psum_scatter(g, "mp", scatter_dimension=0, tiled=False)
    g = lax.psum_scatter(g, "dp", scatter_dimension=0, tiled=True).astype(F32)
    gg = lax.psum_scatter(lax.psum(gg[0:2], "mp"), "dp", scatter_dimension=1, tiled=True)
    go = jnp.concatenate([g[:, 192:256], g[:, 448:512], g[:, 704:768]], axis=1).T
    return (
        out.reshape(rows, seq, width),
        grad_tokens.reshape(rows, seq, width),
        g[:, 0:192],
        g[:, 256:448],
        g[:, 512:704],
        go,
        gg[0],
        g[:, 768:1280],
        g[:, 1280:1792],
        g[:, 1792:2304].T,
        gg[1],
    )


def solution(mesh):
    return jax.shard_map(
        per_device,
        mesh=mesh,
        in_specs=(
            P("dp", None, None), P("dp", None), P("dp", "mp"), P("dp", "mp"), P("dp", "mp"), P("mp", "dp"), P("dp"),
            P("dp", "mp"), P("dp", "mp"), P("mp", "dp"), P("dp"), P("dp", None, None),
        ),
        out_specs=(
            P("dp", None, None), P("dp", None, None), P("dp", "mp"), P("dp", "mp"), P("dp", "mp"), P("mp", "dp"),
            P("dp"), P("dp", "mp"), P("dp", "mp"), P("mp", "dp"), P("dp"),
        ),
        check_vma=False,
    )
```

```python
import functools
import jax
import jax.numpy as jnp
from jax import lax
from jax.experimental import pallas as pl
from jax.experimental.pallas import tpu as pltpu
from jax.sharding import PartitionSpec as P

EPSILON = 1e-06
GELU_COEF = 0.7978845608028654
GELU_CUBE = 0.044715
CAP = 512
NEG = -1e30
F32 = jnp.float32
BF16 = jnp.bfloat16


def nn(a, b):
    return lax.dot_general(a, b, (((1,), (0,)), ((), ())), preferred_element_type=F32)


def nt(a, b):
    return lax.dot_general(a, b, (((1,), (1,)), ((), ())), preferred_element_type=F32)


def tn(a, b):
    return lax.dot_general(a, b, (((0,), (0,)), ((), ())), preferred_element_type=F32)


def placement(len_ref, bins):
    count = len_ref.shape[1]
    sizes = [len_ref[0, i] for i in range(count)]
    starts = [jnp.int32(0)]
    for i in range(count - 1):
        starts.append(starts[-1] + sizes[i])
    ranks = []
    for i in range(count):
        rank = jnp.int32(0)
        for j in range(count):
            if j < i:
                rank = rank + jnp.where(sizes[j] >= sizes[i], 1, 0)
            elif j > i:
                rank = rank + jnp.where(sizes[j] > sizes[i], 1, 0)
        ranks.append(rank)
    fills = [jnp.int32(0)] * (bins - 1)
    spots = [jnp.int32(0)] * count
    for k in range(count):
        size = jnp.int32(0)
        for i in range(count):
            size = size + jnp.where(ranks[i] == k, sizes[i], 0)
        if k == 0:
            spot = jnp.int32((bins - 1) * CAP)
        else:
            free = jnp.int32(1)
            spot = jnp.int32(0)
            for b in range(bins - 1):
                fits = jnp.where(fills[b] + size <= CAP, free, 0) if b < bins - 2 else free
                spot = spot + fits * (b * CAP + fills[b])
                fills[b] = fills[b] + fits * size
                free = free - fits
        for i in range(count):
            spots[i] = spots[i] + jnp.where(ranks[i] == k, spot, 0)
    return starts, sizes, spots


def packed_source(place, first, shape, axis):
    spot = lax.broadcasted_iota(jnp.int32, shape, axis) + first
    source = jnp.full(shape, -1, jnp.int32)
    segment = jnp.full(shape, -1, jnp.int32)
    for i, (start, size, at) in enumerate(zip(*place)):
        here = (spot >= at) & (spot < at + size)
        source = jnp.where(here, spot + (start - at), source)
        segment = jnp.where(here, i, segment)
    return source, segment


def low_lanes():
    return lax.broadcasted_iota(jnp.int32, (1, 128), 1) < 64


def half(tile, low):
    lanes = low_lanes()
    return jnp.where(lanes if low else jnp.logical_not(lanes), tile, jnp.zeros_like(tile))


HEADS = ((0, 2, 4, True), (0, 2, 4, False), (1, 3, 5, True))


def tile_of(ref, m, t, rows=slice(None)):
    return ref[m, rows, 128 * t : 128 * (t + 1)]


def attend_group(qkv, m, bias, o_ref, at, lse_ref=None, qb=256):
    def rows_body(i, carry):
        rows = pl.ds(pl.multiple_of(i * qb, qb), qb)
        sums = [None, None]
        for head, (tq, tk, tv, low) in enumerate(HEADS):
            q = half(qkv[m, rows, 128 * tq : 128 * (tq + 1)], low) * jnp.asarray(0.125, BF16)
            s = nt(q, tile_of(qkv, m, tk)) + bias[rows, :]
            top = jnp.max(s, axis=1, keepdims=True)
            e = jnp.exp(s - top)
            total = jnp.sum(e, axis=1, keepdims=True)
            p = (e * (1.0 / total)).astype(BF16)
            o = nn(p, half(tile_of(qkv, m, tv), low))
            j = 0 if head < 2 else 1
            sums[j] = o if sums[j] is None else sums[j] + o
            if lse_ref is not None:
                lane = lax.broadcasted_iota(jnp.int32, (1, 128), 1)
                lse_ref[rows, :] = jnp.where(lane == 3 * m + head, top + jnp.log(total), lse_ref[rows, :])
        o_ref[at, rows, 0:128] = sums[0].astype(BF16)
        o_ref[at, rows, 128:256] = sums[1].astype(BF16)
        return carry

    lax.fori_loop(0, CAP // qb, rows_body, 0)


def attend_group_back(qkv, m, bias, lse_t, do_ref, at, dqkv, qb=256):
    dk = [None, None]
    dv = [None, None]
    dq = [[None] * (CAP // qb), [None] * (CAP // qb)]
    for head, (tq, tk, tv, low) in enumerate(HEADS):
        j = 0 if head < 2 else 1
        k = half(tile_of(qkv, m, tk), low) * jnp.asarray(0.125, BF16)
        v = half(tile_of(qkv, m, tv), low)
        lse = lse_t[pl.ds(3 * m + head, 1), :]
        for i in range(CAP // qb):
            rows = slice(i * qb, (i + 1) * qb)
            q = tile_of(qkv, m, tq, rows)
            do = do_ref[at, rows, 128 * j : 128 * (j + 1)]
            p = jnp.exp(nt(k, q) + bias[:, rows] - lse[:, rows])
            dp = nt(v, do)
            delta = jnp.sum(p * dp, axis=0, keepdims=True)
            ds = (p * (dp - delta)).astype(BF16)
            dv_part = nn(p.astype(BF16), half(do, low))
            dk_part = nn(ds, half(q, low) * jnp.asarray(0.125, BF16))
            dq_part = tn(ds, k)
            dv[j] = dv_part if dv[j] is None else dv[j] + dv_part
            dk[j] = dk_part if dk[j] is None else dk[j] + dk_part
            dq[j][i] = dq_part if dq[j][i] is None else dq[j][i] + dq_part
    for j in range(2):
        for i in range(CAP // qb):
            dqkv[m, i * qb : (i + 1) * qb, 128 * j : 128 * (j + 1)] = dq[j][i].astype(BF16)
        dqkv[m, :, 128 * (2 + j) : 128 * (3 + j)] = dk[j].astype(BF16)
        dqkv[m, :, 128 * (4 + j) : 128 * (5 + j)] = dv[j].astype(BF16)


def out_weight_tiles(w, m):
    lanes = low_lanes()
    t1 = tile_of(w, m, 1).astype(F32)
    t3 = tile_of(w, m, 3).astype(F32)
    t5 = tile_of(w, m, 5).astype(F32)
    first = jnp.where(lanes, pltpu.roll(t1, 64, 1), t3)
    second = jnp.where(lanes, pltpu.roll(t5, 64, 1), 0.0)
    return first.astype(BF16), second.astype(BF16)


def gelu_parts(a):
    inner = GELU_COEF * (a + GELU_CUBE * a * a * a)
    t = jnp.tanh(inner)
    return t


def rms_rows(values):
    return lax.rsqrt(jnp.mean(values * values, axis=1, keepdims=True) + EPSILON)


def layer_kernel(
    len_ref, x_ref, dy_ref, w_ref, gain_ref, which_ref,
    out_ref, gt_ref, g_ref, gg_ref,
    bias, xp, dyp, n1, n1t, n2, n2t, dypt, dhbt, qkv, o_all, wo, lse, lse_t, do, dqkv, h, acc,
):
    bins = w_ref.shape[0]
    seq = x_ref.shape[0]
    place = placement(len_ref, bins)
    me = which_ref[0]
    g1 = gain_ref[0:1, :]
    g2 = gain_ref[1:2, :]

    def wo_body(m, c):
        first, second = out_weight_tiles(w_ref, m)
        wo[m, :, 0:128] = first
        wo[m, :, 128:256] = second
        return c

    lax.fori_loop(0, bins, wo_body, 0)
    lse[...] = jnp.zeros_like(lse)

    def forward(b):
        source, segment = packed_source(place, b * CAP, (CAP, 1), 0)
        _, segment_row = packed_source(place, b * CAP, (1, CAP), 1)
        bias[...] = jnp.where(segment == segment_row, 0.0, NEG)
        pick = (source == lax.broadcasted_iota(jnp.int32, (CAP, seq), 1)).astype(BF16)
        xb = nn(pick, x_ref[...])
        xp[...] = xb.astype(BF16)
        dyp[...] = nn(pick, dy_ref[...]).astype(BF16)
        n1[...] = (xb * rms_rows(xb) * g1).astype(BF16)
        h[...] = xb

        def m_body(m, c):
            qkv[m] = nn(n1[...], w_ref[m, :, 0:768]).astype(BF16)
            attend_group(qkv, m, bias, o_all, m, lse)
            h[...] += nt(o_all[m], wo[m])
            return c

        lax.fori_loop(0, bins, m_body, 0)
        hb = h[...]
        n2[...] = (hb * rms_rows(hb) * g2).astype(BF16)

    def ffn_out(b):
        acc[...] = h[...]

        def m_body(m, c):
            a = nn(n2[...], w_ref[m, :, 768:1280])
            up = nn(n2[...], w_ref[m, :, 1280:1792])
            u = (0.5 * a * (1.0 + gelu_parts(a)) * up).astype(BF16)
            acc[...] += nt(u, w_ref[m, :, 1792:2304])
            return c

        lax.fori_loop(0, bins, m_body, 0)
        source, _ = packed_source(place, b * CAP, (1, CAP), 1)
        drop = (lax.broadcasted_iota(jnp.int32, (seq, CAP), 0) == source).astype(BF16)
        out_ref[...] = (out_ref[...].astype(F32) + nn(drop, acc[...].astype(BF16))).astype(BF16)

    out_ref[...] = jnp.zeros_like(out_ref)

    def others(i, c):
        b = lax.rem(me + 1 + i, bins)
        forward(b)
        ffn_out(b)
        return c

    lax.fori_loop(0, bins, others, 0)

    n1t[...] = n1[...].T
    n2t[...] = n2[...].T
    dypt[...] = dyp[...].T
    lse_t[...] = lse[...].T
    acc[...] = jnp.zeros_like(acc)

    def ffn_back(m, c):
        a = nn(n2[...], w_ref[m, :, 768:1280])
        up = nn(n2[...], w_ref[m, :, 1280:1792])
        t = gelu_parts(a)
        gel = 0.5 * a * (1.0 + t)
        u = (gel * up).astype(BF16)
        du = nn(dyp[...], w_ref[m, :, 1792:2304])
        slope = 0.5 * (1.0 + t) + 0.5 * a * (1.0 - t * t) * (GELU_COEF * (1.0 + 3.0 * GELU_CUBE * a * a))
        da = (du * up * slope).astype(BF16)
        db = (du * gel).astype(BF16)
        g_ref[m, :, 1792:2304] = nn(dypt[...], u).astype(BF16)
        g_ref[m, :, 768:1280] = nn(n2t[...], da).astype(BF16)
        g_ref[m, :, 1280:1792] = nn(n2t[...], db).astype(BF16)
        acc[...] += nt(da, w_ref[m, :, 768:1280]) + nt(db, w_ref[m, :, 1280:1792])
        return c

    lax.fori_loop(0, bins, ffn_back, 0)
    hb = h[...]
    r2 = rms_rows(hb)
    dn2 = acc[...]
    gg_ffn = jnp.sum(dn2 * hb * r2, axis=0, keepdims=True)
    wg = dn2 * g2
    dh = dyp[...].astype(F32) + r2 * wg - hb * (r2 * r2 * r2) * jnp.mean(wg * hb, axis=1, keepdims=True)
    h[...] = dh
    dhb = dh.astype(BF16)
    dhbt[...] = dhb.T
    n2[...] = dhb
    acc[...] = jnp.zeros_like(acc)

    def attn_back(m, c):
        do[m] = nn(n2[...], wo[m]).astype(BF16)
        attend_group_back(qkv, m, bias, lse_t, do, m, dqkv)
        acc[...] += nt(dqkv[m], w_ref[m, :, 0:768])
        grad = nn(n1t[...], dqkv[m])
        go = nn(dhbt[...], o_all[m])
        lanes = low_lanes()
        for t in range(6):
            g = grad[:, 128 * t : 128 * (t + 1)]
            if t == 1:
                g = jnp.where(lanes, g, pltpu.roll(go[:, 0:128], 64, 1))
            elif t == 3:
                g = jnp.where(lanes, g, go[:, 0:128])
            elif t == 5:
                g = jnp.where(lanes, g, pltpu.roll(go[:, 128:256], 64, 1))
            g_ref[m, :, 128 * t : 128 * (t + 1)] = g.astype(BF16)
        return c

    lax.fori_loop(0, bins, attn_back, 0)
    xb = xp[...].astype(F32)
    r1 = rms_rows(xb)
    dn1 = acc[...]
    gg_attn = jnp.sum(dn1 * xb * r1, axis=0, keepdims=True)
    wa = dn1 * g1
    gt = h[...] + r1 * wa - xb * (r1 * r1 * r1) * jnp.mean(wa * xb, axis=1, keepdims=True)
    gt_ref[...] = gt.astype(BF16)
    gg_ref[0:1, :] = gg_attn
    gg_ref[1:2, :] = gg_ffn


def unpack_kernel(len_ref, gt_ref, out_ref):
    bins = gt_ref.shape[0]
    seq = out_ref.shape[0]
    place = placement(len_ref, bins)
    total = jnp.zeros(out_ref.shape, F32)
    for b in range(bins):
        source, _ = packed_source(place, b * CAP, (1, CAP), 1)
        drop = (lax.broadcasted_iota(jnp.int32, (seq, CAP), 0) == source).astype(BF16)
        total = total + nn(drop, gt_ref[b])
    out_ref[...] = total


def per_device(
    tokens, lengths, query_weight, key_weight, value_weight, out_weight, attn_gain, gate_weight, up_weight, down_weight,
    ffn_gain, cotangent,
):
    rows, seq, width = tokens.shape
    bins = lax.axis_size("mp")
    q, k, v, o = (w.astype(BF16) for w in (query_weight, key_weight, value_weight, out_weight.T))
    package = jnp.concatenate(
        [q, o[:, 0:64], k, o[:, 64:128], v, o[:, 128:192], gate_weight.astype(BF16), up_weight.astype(BF16),
         down_weight.T.astype(BF16)], axis=1)
    w = lax.all_gather(lax.all_gather(package, "dp", axis=0, tiled=True), "mp", axis=0)
    gains = jnp.stack([attn_gain, ffn_gain]).astype(BF16)
    gains = lax.all_gather(gains, "dp", axis=1, tiled=True).astype(F32)
    gains = jnp.concatenate([gains, jnp.zeros((6, width), F32)], axis=0)
    which = lax.axis_index("mp").astype(jnp.int32).reshape(1)
    vmem = pl.BlockSpec(memory_space=pltpu.VMEM)
    smem = pl.BlockSpec(memory_space=pltpu.SMEM)
    group = w.shape[2]
    x = tokens.reshape(seq, width)
    dy = cotangent.reshape(seq, width)
    out, gt, g, gg = pl.pallas_call(
        layer_kernel,
        out_shape=(
            jax.ShapeDtypeStruct((seq, width), BF16),
            jax.ShapeDtypeStruct((CAP, width), BF16),
            jax.ShapeDtypeStruct((bins, width, group), BF16),
            jax.ShapeDtypeStruct((8, width), F32),
        ),
        in_specs=[smem, vmem, vmem, vmem, vmem, smem],
        out_specs=[vmem] * 4,
        scratch_shapes=[
            pltpu.VMEM((CAP, CAP), F32),
            pltpu.VMEM((CAP, width), BF16),
            pltpu.VMEM((CAP, width), BF16),
            pltpu.VMEM((CAP, width), BF16),
            pltpu.VMEM((width, CAP), BF16),
            pltpu.VMEM((CAP, width), BF16),
            pltpu.VMEM((width, CAP), BF16),
            pltpu.VMEM((width, CAP), BF16),
            pltpu.VMEM((width, CAP), BF16),
            pltpu.VMEM((bins, CAP, width), BF16),
            pltpu.VMEM((bins, CAP, 256), BF16),
            pltpu.VMEM((bins, width, 256), BF16),
            pltpu.VMEM((CAP, 128), F32),
            pltpu.VMEM((128, CAP), F32),
            pltpu.VMEM((bins, CAP, 256), BF16),
            pltpu.VMEM((bins, CAP, width), BF16),
            pltpu.VMEM((CAP, width), F32),
            pltpu.VMEM((CAP, width), F32),
        ],
        compiler_params=pltpu.CompilerParams(vmem_limit_bytes=63 * 2**20+900000),
        name="layer",
    )(lengths, x, dy, w, gains, which)
    gt_all = lax.all_gather(gt, "mp", axis=0)
    grad_tokens = pl.pallas_call(
        unpack_kernel,
        out_shape=jax.ShapeDtypeStruct((seq, width), F32),
        in_specs=[smem, vmem],
        out_specs=vmem,
        compiler_params=pltpu.CompilerParams(vmem_limit_bytes=60 * 2**20),
        name="unpack",
    )(lengths, gt_all)
    g = lax.psum_scatter(g, "mp", scatter_dimension=0, tiled=False)
    g = lax.psum_scatter(g, "dp", scatter_dimension=0, tiled=True).astype(F32)
    gg = lax.psum_scatter(lax.psum(gg[0:2], "mp"), "dp", scatter_dimension=1, tiled=True)
    go = jnp.concatenate([g[:, 192:256], g[:, 448:512], g[:, 704:768]], axis=1).T
    return (
        out.reshape(rows, seq, width),
        grad_tokens.reshape(rows, seq, width),
        g[:, 0:192],
        g[:, 256:448],
        g[:, 512:704],
        go,
        gg[0],
        g[:, 768:1280],
        g[:, 1280:1792],
        g[:, 1792:2304].T,
        gg[1],
    )


MESH = pl.DeviceIdType.MESH
PARTS = ((0, 768), (768, 2304))


class Net:
    def __init__(self):
        self.dp = lax.axis_index("dp")
        self.z = lax.axis_index("mp")
        self.core = lax.rem(self.dp, 2)
        self.chip = lax.div(self.dp, 2)
        self.chip_x = self.chip + 1 - 2 * lax.rem(self.chip, 2)
        self.chip_y = lax.rem(self.chip + 2, 4)
        self.chip_d = 3 - self.chip
        self.sibling = (2 * self.chip + 1 - self.core, self.z)
        self.x = (2 * self.chip_x + self.core, self.z)
        self.y = (2 * self.chip_y + self.core, self.z)

    def up(self, k):
        return (self.dp, lax.rem(self.z + k, 4))

    def group(self, i):
        z = self.z
        one = jnp.where(z == 0, 1, jnp.where(z == 1, 0, jnp.where(z == 2, 3, 2)))
        two = jnp.where(z < 2, 2, 1)
        return jnp.where(i == 0, z, jnp.where(i == 1, one, jnp.where(i == 2, two, 6 - z - one - two)))


class Gather:
    def __init__(self, net, w, send, send_z, recv):
        self.net, self.w, self.send, self.send_z, self.recv = net, w, send, send_z, recv

    def unit(self, part, m, chip, core):
        lo, hi = PARTS[part]
        return self.w.at[m, chip, core, :, lo:hi]

    def copy(self, part, m, chip, core, sem, to):
        ref = self.unit(part, m, chip, core)
        return pltpu.make_async_remote_copy(
            src_ref=ref, dst_ref=ref, send_sem=sem, recv_sem=self.recv.at[part, m, chip, core],
            device_id=to, device_id_type=MESH)

    def wait(self, part, m, chip, core):
        self.copy(part, m, chip, core, self.send.at[part, m, chip, 0], self.net.sibling).wait_recv()

    def along_z(self, part):
        net = self.net
        for k in range(1, 4):
            self.copy(part, net.z, net.chip, net.core, self.send_z.at[part, k - 1], net.up(k)).start()

    def spread(self, part, i):
        net = self.net
        m = net.group(i)
        if isinstance(i, int):
            if i > 0:
                self.wait(part, m, net.chip, net.core)
        else:
            @pl.when(i > 0)
            def _():
                self.wait(part, m, net.chip, net.core)
        for k, to in enumerate((net.x, net.y, net.sibling)):
            self.copy(part, m, net.chip, net.core, self.send.at[part, m, net.chip, k], to).start()

    def relay(self, part, i):
        net = self.net
        m = net.group(i)
        first = m < 2
        self.wait(part, m, net.chip_x, net.core)
        self.copy(part, m, net.chip_x, net.core, self.send.at[part, m, net.chip_x, 2], net.sibling).start()
        self.wait(part, m, net.chip_y, net.core)
        source = jnp.where(first, net.chip_x, net.chip_y)
        target = jnp.where(first, net.chip_y, net.chip_x)
        self.copy(part, m, source, net.core, self.send.at[part, m, source, 0], (2 * target + net.core, net.z)).start()
        self.copy(part, m, net.chip_y, net.core, self.send.at[part, m, net.chip_y, 2], net.sibling).start()

    def across(self, part, i):
        net = self.net
        m = net.group(i)
        self.wait(part, m, net.chip_d, net.core)
        self.copy(part, m, net.chip_d, net.core, self.send.at[part, m, net.chip_d, 2], net.sibling).start()

    def complete(self, part, i):
        net = self.net
        m = net.group(i)
        for chip in range(4):
            self.wait(part, m, chip, 1 - net.core)

    def drain(self):
        net = self.net

        def sent(part, m, chip, sem):
            self.copy(part, m, chip, net.core, sem, net.sibling).wait_send()

        for part in range(2):
            for k in range(3):
                sent(part, net.z, net.chip, self.send_z.at[part, k])

            def body(m, c, part=part):
                for k in range(3):
                    sent(part, m, net.chip, self.send.at[part, m, net.chip, k])
                for chip in (net.chip_x, net.chip_y, net.chip_d):
                    sent(part, m, chip, self.send.at[part, m, chip, 2])
                source = jnp.where(m < 2, net.chip_x, net.chip_y)
                sent(part, m, source, self.send.at[part, m, source, 0])
                return c

            lax.fori_loop(0, 4, body, 0)


def greet(net):
    barrier = pltpu.get_barrier_semaphore()
    for other in range(1, 8):
        pl.semaphore_signal(barrier, inc=1, device_id=(lax.rem(net.dp + other, 8), net.z), device_id_type=MESH)
    for k in range(1, 4):
        pl.semaphore_signal(barrier, inc=1, device_id=net.up(k), device_id_type=MESH)
    pl.semaphore_wait(barrier, 10)


def share_gains(net, parts, send, recv):
    copies = []
    for k in range(1, 8):
        copies.append(pltpu.make_async_remote_copy(
            src_ref=parts.at[net.dp], dst_ref=parts.at[net.dp], send_sem=send.at[k - 1], recv_sem=recv.at[net.dp],
            device_id=(lax.rem(net.dp + k, 8), net.z), device_id_type=MESH))
        copies[-1].start()
    return copies


def join_gains(net, parts, send, recv, gain):
    for k in range(1, 8):
        other = lax.rem(net.dp + k, 8)
        pltpu.make_async_remote_copy(
            src_ref=parts.at[other], dst_ref=parts.at[other], send_sem=send.at[k - 1], recv_sem=recv.at[other],
            device_id=net.sibling, device_id_type=MESH).wait_recv()
    total = jnp.zeros(gain.shape, F32)
    for d in range(8):
        piece = jnp.concatenate([parts[d], jnp.zeros((8, gain.shape[1] - 128), F32)], axis=1)
        total = total + pltpu.roll(piece, 96 * d, 1)
    gain[...] = total


def build_package(w, net, q_ref, k_ref, v_ref, o_ref, g_ref, u_ref, d_ref):
    lanes = low_lanes()
    ot = o_ref[...].T
    pad = jnp.zeros((96, 64), F32)
    at = (net.z, net.chip, net.core)

    def put(tile, value):
        w[at[0], at[1], at[2], :, 128 * tile : 128 * (tile + 1)] = value.astype(BF16)

    for j, ref in enumerate((q_ref, k_ref, v_ref)):
        put(2 * j, ref[:, 0:128])
        last = jnp.concatenate([ref[:, 128:192], pad], axis=1)
        extra = jnp.concatenate([ot[:, 64 * j : 64 * (j + 1)], pad], axis=1)
        put(2 * j + 1, jnp.where(lanes, last, pltpu.roll(extra, 64, 1)))
    w[at[0], at[1], at[2], :, 768:1280] = g_ref[...].astype(BF16)
    w[at[0], at[1], at[2], :, 1280:1792] = u_ref[...].astype(BF16)
    w[at[0], at[1], at[2], :, 1792:2304] = d_ref[...].T.astype(BF16)


def rows768(ref, m, lo, hi):
    return ref[m, :, :, :, lo:hi].reshape(768, hi - lo)


def put768(ref, m, lo, hi, value):
    ref[m, :, :, :, lo:hi] = value.reshape(4, 2, 96, hi - lo)


def mega_kernel(
    len_ref, x_ref, dy_ref, q_ref, k_ref, v_ref, o_ref, gate_ref, up_ref, down_ref, ga_ref, gf_ref,
    out_ref, gt_ref, g_ref, gg_ref,
    w, gain, gain_parts, bias, xp, dyp, n1, n1t, n2, n2t, dypt, dhbt, qkv, qkv_b, o_own, o_b, do, wo, lse, lse_t, h, acc, res,
    ag_send, ag_send_z, ag_recv, gn_send, gn_recv, in_sem,
):
    net = Net()
    bins = 4
    halves = [pltpu.make_async_copy(dy_ref.at[j], g_ref.at[0, :, :, :, 768 * j : 768 * (j + 1)], in_sem.at[j]) for j in (0, 1)]
    for copy in halves:
        copy.start()
    seq = x_ref.shape[0]
    me = net.z
    ag = Gather(net, w, ag_send, ag_send_z, ag_recv)
    build_package(w, net, q_ref, k_ref, v_ref, o_ref, gate_ref, up_ref, down_ref)
    pad = jnp.zeros((1, 32), F32)
    mine = jnp.concatenate([
        jnp.concatenate([ga_ref[...], pad], axis=1), jnp.concatenate([gf_ref[...], pad], axis=1),
        jnp.zeros((6, 128), F32)], axis=0)
    gain_parts[net.dp] = mine.astype(BF16).astype(F32)
    greet(net)
    gain_copies = share_gains(net, gain_parts, gn_send, gn_recv)
    ag.along_z(0)
    ag.spread(0, 0)

    place = placement(len_ref, bins)
    lse[...] = jnp.zeros_like(lse)

    def pack(b):
        source, segment = packed_source(place, b * CAP, (CAP, 1), 0)
        _, segment_row = packed_source(place, b * CAP, (1, CAP), 1)
        bias[...] = jnp.where(segment == segment_row, 0.0, NEG)
        return (source == lax.broadcasted_iota(jnp.int32, (CAP, seq), 1)).astype(BF16)

    def unpack(b, value):
        source, _ = packed_source(place, b * CAP, (1, CAP), 1)
        drop = (lax.broadcasted_iota(jnp.int32, (seq, CAP), 0) == source).astype(BF16)
        out_ref[...] = (out_ref[...].astype(F32) + nn(drop, value)).astype(BF16)

    pick = pack(me)
    xb = nn(pick, x_ref[...])
    xp[...] = xb.astype(BF16)
    for copy in halves:
        copy.wait()
    dyp[...] = (nn(pick[:, 0:768], rows768(g_ref, 0, 0, 768)) + nn(pick[:, 768:1536], rows768(g_ref, 0, 768, 1536))).astype(BF16)
    h[...] = xb
    dypt[...] = dyp[...].T
    ag.spread(0, 1)
    ag.relay(0, 0)
    join_gains(net, gain_parts, gn_send, gn_recv, gain)
    g1 = gain[0:1, :]
    g2 = gain[1:2, :]
    n1[...] = (xb * rms_rows(xb) * g1).astype(BF16)
    n1t[...] = n1[...].T
    ag.spread(0, 2)
    ag.across(0, 0)
    ag.relay(0, 1)
    ag.spread(0, 3)

    def own_forward(i, c):
        m = net.group(i)

        @pl.when(i == 0)
        def _():
            ag.across(0, 1)
            ag.relay(0, 2)

        @pl.when(i == 1)
        def _():
            ag.across(0, 2)
            ag.relay(0, 3)
            ag.along_z(1)
            ag.spread(1, 0)

        @pl.when(i == 2)
        def _():
            ag.across(0, 3)
            ag.spread(1, 1)

        @pl.when(i == 3)
        def _():
            ag.relay(1, 0)

        ag.complete(0, i)
        first, second = out_weight_tiles_at(w, m)
        wo[m, :, 0:128] = first
        wo[m, :, 128:256] = second
        qkv[m] = nn(n1[...], rows768(w, m, 0, 768)).astype(BF16)
        attend_group(qkv, m, bias, o_own, m, lse)
        h[...] += nt(o_own[m], wo[m])
        return c

    lax.fori_loop(0, 4, own_forward, 0)
    hb = h[...]
    n2[...] = (hb * rms_rows(hb) * g2).astype(BF16)
    n2t[...] = n2[...].T
    lse_t[...] = lse[...].T
    acc[...] = jnp.zeros_like(acc)
    res[...] = hb

    def ffn_back(i, c):
        m = net.group(i)
        ag.across(1, i)

        @pl.when(i < 3)
        def _():
            ag.relay(1, i + 1)

        @pl.when(i < 2)
        def _():
            ag.spread(1, i + 2)

        ag.complete(1, i)
        for lo in (0, 256):
            w_gate = rows768(w, m, 768 + lo, 1024 + lo)
            w_up = rows768(w, m, 1280 + lo, 1536 + lo)
            w_down = rows768(w, m, 1792 + lo, 2048 + lo)
            a = nn(n2[...], w_gate)
            up = nn(n2[...], w_up)
            t = gelu_parts(a)
            gel = 0.5 * a * (1.0 + t)
            u = (gel * up).astype(BF16)
            res[...] += nt(u, w_down)
            put768(g_ref, m, 1792 + lo, 2048 + lo, nn(dypt[...], u).astype(BF16))
            du = nn(dyp[...], w_down)
            slope = 0.5 * (1.0 + t) + 0.5 * a * (1.0 - t * t) * (GELU_COEF * (1.0 + 3.0 * GELU_CUBE * a * a))
            da = (du * up * slope).astype(BF16)
            db = (du * gel).astype(BF16)
            put768(g_ref, m, 768 + lo, 1024 + lo, nn(n2t[...], da).astype(BF16))
            put768(g_ref, m, 1280 + lo, 1536 + lo, nn(n2t[...], db).astype(BF16))
            acc[...] += nt(da, w_gate) + nt(db, w_up)
        return c

    lax.fori_loop(0, 4, ffn_back, 0)
    out_ref[...] = jnp.zeros_like(out_ref)
    unpack(me, res[...].astype(BF16))
    hb = h[...]
    r2 = rms_rows(hb)
    dn2 = acc[...]
    gg_ffn = jnp.sum(dn2 * hb * r2, axis=0, keepdims=True)
    wg = dn2 * g2
    dh = dyp[...].astype(F32) + r2 * wg - hb * (r2 * r2 * r2) * jnp.mean(wg * hb, axis=1, keepdims=True)
    h[...] = dh
    dhb = dh.astype(BF16)
    dhbt[...] = dhb.T
    n2[...] = dhb
    acc[...] = jnp.zeros_like(acc)

    def attn_back(m, c):
        do[0] = nn(n2[...], wo[m]).astype(BF16)
        attend_group_back(qkv, m, bias, lse_t, do, 0, qkv)
        acc[...] += nt(qkv[m], rows768(w, m, 0, 768))
        return c

    lax.fori_loop(0, 4, attn_back, 0)
    xb = xp[...].astype(F32)
    r1 = rms_rows(xb)
    dn1 = acc[...]
    gg_attn = jnp.sum(dn1 * xb * r1, axis=0, keepdims=True)
    wa = dn1 * g1
    gt = h[...] + r1 * wa - xb * (r1 * r1 * r1) * jnp.mean(wa * xb, axis=1, keepdims=True)
    gt_ref[...] = gt.astype(BF16)
    gg_ref[0:1, :] = gg_attn
    gg_ref[1:2, :] = gg_ffn

    def attn_grads(m, c):
        grad = nn(n1t[...], qkv[m])
        go = nn(dhbt[...], o_own[m])
        lanes = low_lanes()
        for t in range(6):
            g = grad[:, 128 * t : 128 * (t + 1)]
            if t == 1:
                g = jnp.where(lanes, g, pltpu.roll(go[:, 0:128], 64, 1))
            elif t == 3:
                g = jnp.where(lanes, g, go[:, 0:128])
            elif t == 5:
                g = jnp.where(lanes, g, pltpu.roll(go[:, 128:256], 64, 1))
            put768(g_ref, m, 128 * t, 128 * (t + 1), g.astype(BF16))
        return c

    lax.fori_loop(0, 4, attn_grads, 0)

    def others(k, c):
        b = lax.rem(me + 1 + k, bins)
        xo = nn(pack(b), x_ref[...])
        n1[...] = (xo * rms_rows(xo) * g1).astype(BF16)
        h[...] = xo

        def attend(m, c):
            qkv_b[0] = nn(n1[...], rows768(w, m, 0, 768)).astype(BF16)
            attend_group(qkv_b, 0, bias, o_b, 0)
            h[...] += nt(o_b[0], wo[m])
            return c

        lax.fori_loop(0, 4, attend, 0)
        ho = h[...]
        n2[...] = (ho * rms_rows(ho) * g2).astype(BF16)

        def ffn(m, c):
            a = nn(n2[...], rows768(w, m, 768, 1280))
            up = nn(n2[...], rows768(w, m, 1280, 1792))
            u = (0.5 * a * (1.0 + gelu_parts(a)) * up).astype(BF16)
            h[...] += nt(u, rows768(w, m, 1792, 2304))
            return c

        lax.fori_loop(0, 4, ffn, 0)
        unpack(b, h[...].astype(BF16))
        return c

    lax.fori_loop(0, 3, others, 0)
    for copy in gain_copies:
        copy.wait_send()
    ag.drain()


def out_weight_tiles_at(w, m):
    lanes = low_lanes()
    t1 = rows768(w, m, 128, 256).astype(F32)
    t3 = rows768(w, m, 384, 512).astype(F32)
    t5 = rows768(w, m, 640, 768).astype(F32)
    first = jnp.where(lanes, pltpu.roll(t1, 64, 1), t3)
    second = jnp.where(lanes, pltpu.roll(t5, 64, 1), 0.0)
    return first.astype(BF16), second.astype(BF16)


def on_this_slice(
    tokens, lengths, query_weight, key_weight, value_weight, out_weight, attn_gain, gate_weight, up_weight, down_weight,
    ffn_gain, cotangent,
):
    rows, seq, width = tokens.shape
    vmem = pl.BlockSpec(memory_space=pltpu.VMEM)
    smem = pl.BlockSpec(memory_space=pltpu.SMEM)
    dma = pltpu.SemaphoreType.DMA
    act = pltpu.VMEM((CAP, width), BF16)
    act_t = pltpu.VMEM((width, CAP), BF16)
    wide = pltpu.VMEM((CAP, width), F32)
    out, gt, g, gg = pl.pallas_call(
        mega_kernel,
        out_shape=(
            jax.ShapeDtypeStruct((seq, width), BF16),
            jax.ShapeDtypeStruct((CAP, width), BF16),
            jax.ShapeDtypeStruct((4, 4, 2, 96, 2304), BF16),
            jax.ShapeDtypeStruct((8, width), F32),
        ),
        in_specs=[smem, vmem, pl.BlockSpec(memory_space=pl.ANY)] + [vmem] * 9,
        out_specs=[vmem] * 4,
        scratch_shapes=[
            pltpu.VMEM((4, 4, 2, 96, 2304), BF16),
            pltpu.VMEM((8, width), F32),
            pltpu.VMEM((8, 8, 128), F32),
            pltpu.VMEM((CAP, CAP), F32),
            act, act, act, act_t, act, act_t, act_t, act_t,
            pltpu.VMEM((4, CAP, width), BF16),
            pltpu.VMEM((1, CAP, width), BF16),
            pltpu.VMEM((4, CAP, 256), BF16),
            pltpu.VMEM((1, CAP, 256), BF16),
            pltpu.VMEM((1, CAP, 256), BF16),
            pltpu.VMEM((4, width, 256), BF16),
            pltpu.VMEM((CAP, 128), F32),
            pltpu.VMEM((128, CAP), F32),
            wide, wide, wide,
            dma((2, 4, 4, 3)), dma((2, 3)), dma((2, 4, 4, 2)), dma((7,)), dma((8,)), dma((2,)),
        ],
        compiler_params=pltpu.CompilerParams(
            vmem_limit_bytes=60 * 2**20, collective_id=0, has_side_effects=True),
        name="layer",
    )(lengths, tokens.reshape(seq, width), cotangent.reshape(2, 4, 2, 96, width), query_weight, key_weight, value_weight, out_weight,
      gate_weight, up_weight, down_weight, attn_gain.reshape(1, 96), ffn_gain.reshape(1, 96))
    bins = 4
    gt_all = lax.all_gather(gt, "mp", axis=0)
    grad_tokens = pl.pallas_call(
        unpack_kernel,
        out_shape=jax.ShapeDtypeStruct((seq, width), F32),
        in_specs=[smem, vmem],
        out_specs=vmem,
        compiler_params=pltpu.CompilerParams(vmem_limit_bytes=60 * 2**20),
        name="unpack",
    )(lengths, gt_all)
    g = g.reshape(4, width, 2304)
    g = lax.psum_scatter(g, "mp", scatter_dimension=0, tiled=False)
    g = lax.psum_scatter(g, "dp", scatter_dimension=0, tiled=True).astype(F32)
    gg = lax.psum_scatter(lax.psum(gg[0:2], "mp"), "dp", scatter_dimension=1, tiled=True)
    go = jnp.concatenate([g[:, 192:256], g[:, 448:512], g[:, 704:768]], axis=1).T
    return (
        out.reshape(rows, seq, width),
        grad_tokens.reshape(rows, seq, width),
        g[:, 0:192],
        g[:, 256:448],
        g[:, 512:704],
        go,
        gg[0],
        g[:, 768:1280],
        g[:, 1280:1792],
        g[:, 1792:2304].T,
        gg[1],
    )
def solution(mesh):
    body = on_this_slice if dict(mesh.shape) == {"dp": 8, "mp": 4} else per_device
    return jax.shard_map(
        body,
        mesh=mesh,
        in_specs=(
            P("dp", None, None), P("dp", None), P("dp", "mp"), P("dp", "mp"), P("dp", "mp"), P("mp", "dp"), P("dp"),
            P("dp", "mp"), P("dp", "mp"), P("mp", "dp"), P("dp"), P("dp", None, None),
        ),
        out_specs=(
            P("dp", None, None), P("dp", None, None), P("dp", "mp"), P("dp", "mp"), P("dp", "mp"), P("mp", "dp"),
            P("dp"), P("dp", "mp"), P("dp", "mp"), P("mp", "dp"), P("dp"),
        ),
        check_vma=False,
    )
```

```python
import functools
import jax
import jax.numpy as jnp
from jax import lax
from jax.experimental import pallas as pl
from jax.experimental.pallas import tpu as pltpu
from jax.sharding import PartitionSpec as P

EPSILON = 1e-06
GELU_COEF = 0.7978845608028654
GELU_CUBE = 0.044715
CAP = 512
NEG = -1e30
F32 = jnp.float32
BF16 = jnp.bfloat16


def nn(a, b):
    return lax.dot_general(a, b, (((1,), (0,)), ((), ())), preferred_element_type=F32)


def nt(a, b):
    return lax.dot_general(a, b, (((1,), (1,)), ((), ())), preferred_element_type=F32)


def tn(a, b):
    return lax.dot_general(a, b, (((0,), (0,)), ((), ())), preferred_element_type=F32)


def placement(len_ref, bins):
    count = len_ref.shape[1]
    sizes = [len_ref[0, i] for i in range(count)]
    starts = [jnp.int32(0)]
    for i in range(count - 1):
        starts.append(starts[-1] + sizes[i])
    ranks = []
    for i in range(count):
        rank = jnp.int32(0)
        for j in range(count):
            if j < i:
                rank = rank + jnp.where(sizes[j] >= sizes[i], 1, 0)
            elif j > i:
                rank = rank + jnp.where(sizes[j] > sizes[i], 1, 0)
        ranks.append(rank)
    fills = [jnp.int32(0)] * (bins - 1)
    spots = [jnp.int32(0)] * count
    for k in range(count):
        size = jnp.int32(0)
        for i in range(count):
            size = size + jnp.where(ranks[i] == k, sizes[i], 0)
        if k == 0:
            spot = jnp.int32((bins - 1) * CAP)
        else:
            free = jnp.int32(1)
            spot = jnp.int32(0)
            for b in range(bins - 1):
                fits = jnp.where(fills[b] + size <= CAP, free, 0) if b < bins - 2 else free
                spot = spot + fits * (b * CAP + fills[b])
                fills[b] = fills[b] + fits * size
                free = free - fits
        for i in range(count):
            spots[i] = spots[i] + jnp.where(ranks[i] == k, spot, 0)
    return starts, sizes, spots


def packed_source(place, first, shape, axis):
    spot = lax.broadcasted_iota(jnp.int32, shape, axis) + first
    source = jnp.full(shape, -1, jnp.int32)
    segment = jnp.full(shape, -1, jnp.int32)
    for i, (start, size, at) in enumerate(zip(*place)):
        here = (spot >= at) & (spot < at + size)
        source = jnp.where(here, spot + (start - at), source)
        segment = jnp.where(here, i, segment)
    return source, segment


def low_lanes():
    return lax.broadcasted_iota(jnp.int32, (1, 128), 1) < 64


def half(tile, low):
    lanes = low_lanes()
    return jnp.where(lanes if low else jnp.logical_not(lanes), tile, jnp.zeros_like(tile))


HEADS = ((0, 2, 4, True), (0, 2, 4, False), (1, 3, 5, True))


def tile_of(ref, m, t, rows=slice(None)):
    return ref[m, rows, 128 * t : 128 * (t + 1)]


def attend_group(qkv, m, bias, o_ref, at, lse_ref=None, qb=256):
    def rows_body(i, carry):
        rows = pl.ds(pl.multiple_of(i * qb, qb), qb)
        sums = [None, None]
        for head, (tq, tk, tv, low) in enumerate(HEADS):
            q = half(qkv[m, rows, 128 * tq : 128 * (tq + 1)], low) * jnp.asarray(0.125, BF16)
            s = nt(q, tile_of(qkv, m, tk)) + bias[rows, :]
            top = jnp.max(s, axis=1, keepdims=True)
            e = jnp.exp(s - top)
            total = jnp.sum(e, axis=1, keepdims=True)
            p = (e * (1.0 / total)).astype(BF16)
            o = nn(p, half(tile_of(qkv, m, tv), low))
            j = 0 if head < 2 else 1
            sums[j] = o if sums[j] is None else sums[j] + o
            if lse_ref is not None:
                lane = lax.broadcasted_iota(jnp.int32, (1, 128), 1)
                lse_ref[rows, :] = jnp.where(lane == 3 * m + head, top + jnp.log(total), lse_ref[rows, :])
        o_ref[at, rows, 0:128] = sums[0].astype(BF16)
        o_ref[at, rows, 128:256] = sums[1].astype(BF16)
        return carry

    lax.fori_loop(0, CAP // qb, rows_body, 0)


def attend_group_back(qkv, m, bias, lse_t, do_ref, at, dqkv, qb=256):
    dk = [None, None]
    dv = [None, None]
    dq = [[None] * (CAP // qb), [None] * (CAP // qb)]
    for head, (tq, tk, tv, low) in enumerate(HEADS):
        j = 0 if head < 2 else 1
        k = half(tile_of(qkv, m, tk), low) * jnp.asarray(0.125, BF16)
        v = half(tile_of(qkv, m, tv), low)
        lse = lse_t[pl.ds(3 * m + head, 1), :]
        for i in range(CAP // qb):
            rows = slice(i * qb, (i + 1) * qb)
            q = tile_of(qkv, m, tq, rows)
            do = do_ref[at, rows, 128 * j : 128 * (j + 1)]
            p = jnp.exp(nt(k, q) + bias[:, rows] - lse[:, rows])
            dp = nt(v, do)
            delta = jnp.sum(p * dp, axis=0, keepdims=True)
            ds = (p * (dp - delta)).astype(BF16)
            dv_part = nn(p.astype(BF16), half(do, low))
            dk_part = nn(ds, half(q, low) * jnp.asarray(0.125, BF16))
            dq_part = tn(ds, k)
            dv[j] = dv_part if dv[j] is None else dv[j] + dv_part
            dk[j] = dk_part if dk[j] is None else dk[j] + dk_part
            dq[j][i] = dq_part if dq[j][i] is None else dq[j][i] + dq_part
    for j in range(2):
        for i in range(CAP // qb):
            dqkv[m, i * qb : (i + 1) * qb, 128 * j : 128 * (j + 1)] = dq[j][i].astype(BF16)
        dqkv[m, :, 128 * (2 + j) : 128 * (3 + j)] = dk[j].astype(BF16)
        dqkv[m, :, 128 * (4 + j) : 128 * (5 + j)] = dv[j].astype(BF16)


def out_weight_tiles(w, m):
    lanes = low_lanes()
    t1 = tile_of(w, m, 1).astype(F32)
    t3 = tile_of(w, m, 3).astype(F32)
    t5 = tile_of(w, m, 5).astype(F32)
    first = jnp.where(lanes, pltpu.roll(t1, 64, 1), t3)
    second = jnp.where(lanes, pltpu.roll(t5, 64, 1), 0.0)
    return first.astype(BF16), second.astype(BF16)


def gelu_parts(a):
    inner = GELU_COEF * (a + GELU_CUBE * a * a * a)
    t = jnp.tanh(inner)
    return t


def rms_rows(values):
    return lax.rsqrt(jnp.mean(values * values, axis=1, keepdims=True) + EPSILON)


def layer_kernel(
    len_ref, x_ref, dy_ref, w_ref, gain_ref, which_ref,
    out_ref, gt_ref, g_ref, gg_ref,
    bias, xp, dyp, n1, n1t, n2, n2t, dypt, dhbt, qkv, o_all, wo, lse, lse_t, do, dqkv, h, acc,
):
    bins = w_ref.shape[0]
    seq = x_ref.shape[0]
    place = placement(len_ref, bins)
    me = which_ref[0]
    g1 = gain_ref[0:1, :]
    g2 = gain_ref[1:2, :]

    def wo_body(m, c):
        first, second = out_weight_tiles(w_ref, m)
        wo[m, :, 0:128] = first
        wo[m, :, 128:256] = second
        return c

    lax.fori_loop(0, bins, wo_body, 0)
    lse[...] = jnp.zeros_like(lse)

    def forward(b):
        source, segment = packed_source(place, b * CAP, (CAP, 1), 0)
        _, segment_row = packed_source(place, b * CAP, (1, CAP), 1)
        bias[...] = jnp.where(segment == segment_row, 0.0, NEG)
        pick = (source == lax.broadcasted_iota(jnp.int32, (CAP, seq), 1)).astype(BF16)
        xb = nn(pick, x_ref[...])
        xp[...] = xb.astype(BF16)
        dyp[...] = nn(pick, dy_ref[...]).astype(BF16)
        n1[...] = (xb * rms_rows(xb) * g1).astype(BF16)
        h[...] = xb

        def m_body(m, c):
            qkv[m] = nn(n1[...], w_ref[m, :, 0:768]).astype(BF16)
            attend_group(qkv, m, bias, o_all, m, lse)
            h[...] += nt(o_all[m], wo[m])
            return c

        lax.fori_loop(0, bins, m_body, 0)
        hb = h[...]
        n2[...] = (hb * rms_rows(hb) * g2).astype(BF16)

    def ffn_out(b):
        acc[...] = h[...]

        def m_body(m, c):
            a = nn(n2[...], w_ref[m, :, 768:1280])
            up = nn(n2[...], w_ref[m, :, 1280:1792])
            u = (0.5 * a * (1.0 + gelu_parts(a)) * up).astype(BF16)
            acc[...] += nt(u, w_ref[m, :, 1792:2304])
            return c

        lax.fori_loop(0, bins, m_body, 0)
        source, _ = packed_source(place, b * CAP, (1, CAP), 1)
        drop = (lax.broadcasted_iota(jnp.int32, (seq, CAP), 0) == source).astype(BF16)
        out_ref[...] = (out_ref[...].astype(F32) + nn(drop, acc[...].astype(BF16))).astype(BF16)

    out_ref[...] = jnp.zeros_like(out_ref)

    def others(i, c):
        b = lax.rem(me + 1 + i, bins)
        forward(b)
        ffn_out(b)
        return c

    lax.fori_loop(0, bins, others, 0)

    n1t[...] = n1[...].T
    n2t[...] = n2[...].T
    dypt[...] = dyp[...].T
    lse_t[...] = lse[...].T
    acc[...] = jnp.zeros_like(acc)

    def ffn_back(m, c):
        a = nn(n2[...], w_ref[m, :, 768:1280])
        up = nn(n2[...], w_ref[m, :, 1280:1792])
        t = gelu_parts(a)
        gel = 0.5 * a * (1.0 + t)
        u = (gel * up).astype(BF16)
        du = nn(dyp[...], w_ref[m, :, 1792:2304])
        slope = 0.5 * (1.0 + t) + 0.5 * a * (1.0 - t * t) * (GELU_COEF * (1.0 + 3.0 * GELU_CUBE * a * a))
        da = (du * up * slope).astype(BF16)
        db = (du * gel).astype(BF16)
        g_ref[m, :, 1792:2304] = nn(dypt[...], u).astype(BF16)
        g_ref[m, :, 768:1280] = nn(n2t[...], da).astype(BF16)
        g_ref[m, :, 1280:1792] = nn(n2t[...], db).astype(BF16)
        acc[...] += nt(da, w_ref[m, :, 768:1280]) + nt(db, w_ref[m, :, 1280:1792])
        return c

    lax.fori_loop(0, bins, ffn_back, 0)
    hb = h[...]
    r2 = rms_rows(hb)
    dn2 = acc[...]
    gg_ffn = jnp.sum(dn2 * hb * r2, axis=0, keepdims=True)
    wg = dn2 * g2
    dh = dyp[...].astype(F32) + r2 * wg - hb * (r2 * r2 * r2) * jnp.mean(wg * hb, axis=1, keepdims=True)
    h[...] = dh
    dhb = dh.astype(BF16)
    dhbt[...] = dhb.T
    n2[...] = dhb
    acc[...] = jnp.zeros_like(acc)

    def attn_back(m, c):
        do[m] = nn(n2[...], wo[m]).astype(BF16)
        attend_group_back(qkv, m, bias, lse_t, do, m, dqkv)
        acc[...] += nt(dqkv[m], w_ref[m, :, 0:768])
        grad = nn(n1t[...], dqkv[m])
        go = nn(dhbt[...], o_all[m])
        lanes = low_lanes()
        for t in range(6):
            g = grad[:, 128 * t : 128 * (t + 1)]
            if t == 1:
                g = jnp.where(lanes, g, pltpu.roll(go[:, 0:128], 64, 1))
            elif t == 3:
                g = jnp.where(lanes, g, go[:, 0:128])
            elif t == 5:
                g = jnp.where(lanes, g, pltpu.roll(go[:, 128:256], 64, 1))
            g_ref[m, :, 128 * t : 128 * (t + 1)] = g.astype(BF16)
        return c

    lax.fori_loop(0, bins, attn_back, 0)
    xb = xp[...].astype(F32)
    r1 = rms_rows(xb)
    dn1 = acc[...]
    gg_attn = jnp.sum(dn1 * xb * r1, axis=0, keepdims=True)
    wa = dn1 * g1
    gt = h[...] + r1 * wa - xb * (r1 * r1 * r1) * jnp.mean(wa * xb, axis=1, keepdims=True)
    gt_ref[...] = gt.astype(BF16)
    gg_ref[0:1, :] = gg_attn
    gg_ref[1:2, :] = gg_ffn


def unpack_kernel(len_ref, gt_ref, out_ref):
    bins = gt_ref.shape[0]
    seq = out_ref.shape[0]
    place = placement(len_ref, bins)
    total = jnp.zeros(out_ref.shape, F32)
    for b in range(bins):
        source, _ = packed_source(place, b * CAP, (1, CAP), 1)
        drop = (lax.broadcasted_iota(jnp.int32, (seq, CAP), 0) == source).astype(BF16)
        total = total + nn(drop, gt_ref[b])
    out_ref[...] = total


def per_device(
    tokens, lengths, query_weight, key_weight, value_weight, out_weight, attn_gain, gate_weight, up_weight, down_weight,
    ffn_gain, cotangent,
):
    rows, seq, width = tokens.shape
    bins = lax.axis_size("mp")
    q, k, v, o = (w.astype(BF16) for w in (query_weight, key_weight, value_weight, out_weight.T))
    package = jnp.concatenate(
        [q, o[:, 0:64], k, o[:, 64:128], v, o[:, 128:192], gate_weight.astype(BF16), up_weight.astype(BF16),
         down_weight.T.astype(BF16)], axis=1)
    w = lax.all_gather(lax.all_gather(package, "dp", axis=0, tiled=True), "mp", axis=0)
    gains = jnp.stack([attn_gain, ffn_gain]).astype(BF16)
    gains = lax.all_gather(gains, "dp", axis=1, tiled=True).astype(F32)
    gains = jnp.concatenate([gains, jnp.zeros((6, width), F32)], axis=0)
    which = lax.axis_index("mp").astype(jnp.int32).reshape(1)
    vmem = pl.BlockSpec(memory_space=pltpu.VMEM)
    smem = pl.BlockSpec(memory_space=pltpu.SMEM)
    group = w.shape[2]
    x = tokens.reshape(seq, width)
    dy = cotangent.reshape(seq, width)
    out, gt, g, gg = pl.pallas_call(
        layer_kernel,
        out_shape=(
            jax.ShapeDtypeStruct((seq, width), BF16),
            jax.ShapeDtypeStruct((CAP, width), BF16),
            jax.ShapeDtypeStruct((bins, width, group), BF16),
            jax.ShapeDtypeStruct((8, width), F32),
        ),
        in_specs=[smem, vmem, vmem, vmem, vmem, smem],
        out_specs=[vmem] * 4,
        scratch_shapes=[
            pltpu.VMEM((CAP, CAP), F32),
            pltpu.VMEM((CAP, width), BF16),
            pltpu.VMEM((CAP, width), BF16),
            pltpu.VMEM((CAP, width), BF16),
            pltpu.VMEM((width, CAP), BF16),
            pltpu.VMEM((CAP, width), BF16),
            pltpu.VMEM((width, CAP), BF16),
            pltpu.VMEM((width, CAP), BF16),
            pltpu.VMEM((width, CAP), BF16),
            pltpu.VMEM((bins, CAP, width), BF16),
            pltpu.VMEM((bins, CAP, 256), BF16),
            pltpu.VMEM((bins, width, 256), BF16),
            pltpu.VMEM((CAP, 128), F32),
            pltpu.VMEM((128, CAP), F32),
            pltpu.VMEM((bins, CAP, 256), BF16),
            pltpu.VMEM((bins, CAP, width), BF16),
            pltpu.VMEM((CAP, width), F32),
            pltpu.VMEM((CAP, width), F32),
        ],
        compiler_params=pltpu.CompilerParams(vmem_limit_bytes=63 * 2**20+900000),
        name="layer",
    )(lengths, x, dy, w, gains, which)
    gt_all = lax.all_gather(gt, "mp", axis=0)
    grad_tokens = pl.pallas_call(
        unpack_kernel,
        out_shape=jax.ShapeDtypeStruct((seq, width), F32),
        in_specs=[smem, vmem],
        out_specs=vmem,
        compiler_params=pltpu.CompilerParams(vmem_limit_bytes=60 * 2**20),
        name="unpack",
    )(lengths, gt_all)
    g = lax.psum_scatter(g, "mp", scatter_dimension=0, tiled=False)
    g = lax.psum_scatter(g, "dp", scatter_dimension=0, tiled=True).astype(F32)
    gg = lax.psum_scatter(lax.psum(gg[0:2], "mp"), "dp", scatter_dimension=1, tiled=True)
    go = jnp.concatenate([g[:, 192:256], g[:, 448:512], g[:, 704:768]], axis=1).T
    return (
        out.reshape(rows, seq, width),
        grad_tokens.reshape(rows, seq, width),
        g[:, 0:192],
        g[:, 256:448],
        g[:, 512:704],
        go,
        gg[0],
        g[:, 768:1280],
        g[:, 1280:1792],
        g[:, 1792:2304].T,
        gg[1],
    )


MESH = pl.DeviceIdType.MESH
PARTS = ((0, 768), (768, 2304))


class Net:
    def __init__(self):
        self.dp = lax.axis_index("dp")
        self.z = lax.axis_index("mp")
        self.core = lax.rem(self.dp, 2)
        self.chip = lax.div(self.dp, 2)
        self.chip_x = self.chip + 1 - 2 * lax.rem(self.chip, 2)
        self.chip_y = lax.rem(self.chip + 2, 4)
        self.chip_d = 3 - self.chip
        self.sibling = (2 * self.chip + 1 - self.core, self.z)
        self.x = (2 * self.chip_x + self.core, self.z)
        self.y = (2 * self.chip_y + self.core, self.z)

    def up(self, k):
        return (self.dp, lax.rem(self.z + k, 4))

    def group(self, i):
        z = self.z
        one = jnp.where(z == 0, 1, jnp.where(z == 1, 0, jnp.where(z == 2, 3, 2)))
        two = jnp.where(z < 2, 2, 1)
        return jnp.where(i == 0, z, jnp.where(i == 1, one, jnp.where(i == 2, two, 6 - z - one - two)))


class Gather:
    def __init__(self, net, w, send, send_z, recv):
        self.net, self.w, self.send, self.send_z, self.recv = net, w, send, send_z, recv

    def unit(self, part, m, chip, core):
        lo, hi = PARTS[part]
        return self.w.at[m, chip, core, :, lo:hi]

    def copy(self, part, m, chip, core, sem, to):
        ref = self.unit(part, m, chip, core)
        return pltpu.make_async_remote_copy(
            src_ref=ref, dst_ref=ref, send_sem=sem, recv_sem=self.recv.at[part, m, chip, core],
            device_id=to, device_id_type=MESH)

    def wait(self, part, m, chip, core):
        self.copy(part, m, chip, core, self.send.at[part, m, chip, 0], self.net.sibling).wait_recv()

    def along_z(self, part):
        net = self.net
        for k in range(1, 4):
            self.copy(part, net.z, net.chip, net.core, self.send_z.at[part, k - 1], net.up(k)).start()

    def spread(self, part, i):
        net = self.net
        m = net.group(i)
        if isinstance(i, int):
            if i > 0:
                self.wait(part, m, net.chip, net.core)
        else:
            @pl.when(i > 0)
            def _():
                self.wait(part, m, net.chip, net.core)
        for k, to in enumerate((net.x, net.y, net.sibling)):
            self.copy(part, m, net.chip, net.core, self.send.at[part, m, net.chip, k], to).start()

    def relay(self, part, i):
        net = self.net
        m = net.group(i)
        first = m < 2
        self.wait(part, m, net.chip_x, net.core)
        self.copy(part, m, net.chip_x, net.core, self.send.at[part, m, net.chip_x, 2], net.sibling).start()
        self.wait(part, m, net.chip_y, net.core)
        source = jnp.where(first, net.chip_x, net.chip_y)
        target = jnp.where(first, net.chip_y, net.chip_x)
        self.copy(part, m, source, net.core, self.send.at[part, m, source, 0], (2 * target + net.core, net.z)).start()
        self.copy(part, m, net.chip_y, net.core, self.send.at[part, m, net.chip_y, 2], net.sibling).start()

    def across(self, part, i):
        net = self.net
        m = net.group(i)
        self.wait(part, m, net.chip_d, net.core)
        self.copy(part, m, net.chip_d, net.core, self.send.at[part, m, net.chip_d, 2], net.sibling).start()

    def complete(self, part, i):
        net = self.net
        m = net.group(i)
        for chip in range(4):
            self.wait(part, m, chip, 1 - net.core)

    def drain(self):
        net = self.net

        def sent(part, m, chip, sem):
            self.copy(part, m, chip, net.core, sem, net.sibling).wait_send()

        for part in range(2):
            for k in range(3):
                sent(part, net.z, net.chip, self.send_z.at[part, k])

            def body(m, c, part=part):
                for k in range(3):
                    sent(part, m, net.chip, self.send.at[part, m, net.chip, k])
                for chip in (net.chip_x, net.chip_y, net.chip_d):
                    sent(part, m, chip, self.send.at[part, m, chip, 2])
                source = jnp.where(m < 2, net.chip_x, net.chip_y)
                sent(part, m, source, self.send.at[part, m, source, 0])
                return c

            lax.fori_loop(0, 4, body, 0)


class Reduce:
    def __init__(self, net, g, slots, sems, ok):
        self.net, self.g, self.slots, self.sems, self.ok = net, g, slots, sems, ok

    def lanes(self, part):
        return slice(*PARTS[part])

    def unit(self, part, m, chip, core, rows=slice(0, 96)):
        return self.g.at[m, chip, core, rows, self.lanes(part)]

    def copy(self, kind, part, key, src, dst, to):
        return pltpu.make_async_remote_copy(
            src_ref=src, dst_ref=dst, send_sem=self.sems.at[0, kind, part, key], recv_sem=self.sems.at[1, kind, part, key],
            device_id=to, device_id_type=MESH)

    def core_copy(self, part, i):
        m = self.net.group(i)
        lo, hi = PARTS[part]
        return self.copy(
            0, part, m, self.g.at[m, :, 1 - self.net.core, :, lo:hi],
            self.slots.at[lax.rem(i, 2), :, :, 0 : hi - lo], self.net.sibling)

    def to_core(self, part, i, credit):
        if credit:
            pl.semaphore_wait(self.ok.at[3, part, self.net.group(i)], 1)
        self.core_copy(part, i).start()

    def from_core(self, part, i, credit):
        net = self.net
        m = net.group(i)
        lo, hi = PARTS[part]
        copy = self.core_copy(part, i)
        copy.wait_recv()
        slot = lax.rem(i, 2)
        for chip in range(4):
            mine = self.g[m, chip, net.core, :, lo:hi].astype(F32)
            theirs = self.slots[slot, chip, :, 0 : hi - lo].astype(F32)
            self.g[m, chip, net.core, :, lo:hi] = (mine + theirs).astype(BF16)
        if credit is not None:
            p, j = credit
            pl.semaphore_signal(self.ok.at[3, p, net.group(j)], inc=1, device_id=net.sibling, device_id_type=MESH)
        copy.wait_send()
        pl.semaphore_signal(self.ok.at[0, part, m], inc=1, device_id=net.x, device_id_type=MESH)
        pl.semaphore_signal(self.ok.at[1, part, m], inc=1, device_id=net.y, device_id_type=MESH)

        @pl.when(m != net.z)
        def _():
            pl.semaphore_signal(self.ok.at[2, part, net.z], inc=1, device_id=(net.dp, m), device_id_type=MESH)

    def across_copies(self, part, m):
        net = self.net
        out = []
        for kind, rows, to in ((1, slice(0, 48), net.y), (2, slice(48, 96), net.x)):
            out.append(self.copy(
                kind, part, m, self.unit(part, m, net.chip_d, net.core, rows),
                self.unit(part, m, 0, 1 - net.core, rows), to))
        return out

    def side_copies(self, part, m):
        net = self.net
        return [
            self.copy(kind, part, m, self.unit(part, m, chip, net.core), self.unit(part, m, slot, 1 - net.core), to)
            for kind, chip, slot, to in ((3, net.chip_x, 1, net.x), (4, net.chip_y, 2, net.y))]

    def z_copy(self, part, m):
        net = self.net
        return pltpu.make_async_remote_copy(
            src_ref=self.unit(part, m, net.chip, net.core), dst_ref=self.unit(part, net.z, 3, 1 - net.core),
            send_sem=self.sems.at[0, 5, part, m], recv_sem=self.sems.at[1, 5, part, net.z],
            device_id=(net.dp, m), device_id_type=MESH)

    def add(self, part, m, chip, slot, rows=slice(0, 96)):
        net = self.net
        lanes = self.lanes(part)
        mine = self.g[m, chip, net.core, rows, lanes].astype(F32)
        theirs = self.g[m, slot, 1 - net.core, rows, lanes].astype(F32)
        self.g[m, chip, net.core, rows, lanes] = (mine + theirs).astype(BF16)

    def start_across(self, part, i):
        m = self.net.group(i)
        pl.semaphore_wait(self.ok.at[0, part, m], 1)
        pl.semaphore_wait(self.ok.at[1, part, m], 1)
        for copy in self.across_copies(part, m):
            copy.start()

    def start_sides(self, part, i):
        net = self.net
        m = net.group(i)
        by_y, by_x = self.across_copies(part, m)
        by_y.wait_recv()
        self.add(part, m, net.chip_x, 0, slice(0, 48))
        by_x.wait_recv()
        self.add(part, m, net.chip_y, 0, slice(48, 96))
        for copy in self.side_copies(part, m):
            copy.start()

    def start_z(self, part, i):
        net = self.net
        m = net.group(i)
        for slot, copy in zip((1, 2), self.side_copies(part, m)):
            copy.wait_recv()
            self.add(part, m, net.chip, slot)

        @pl.when(m != net.z)
        def _():
            pl.semaphore_wait(self.ok.at[2, part, m], 1)
            self.z_copy(part, m).start()

    def total(self, part):
        net = self.net
        value = self.g[net.z, net.chip, net.core, :, self.lanes(part)].astype(F32)
        for k in range(1, 4):
            other = lax.rem(net.z + k, 4)
            ref = self.unit(part, other, 3, 1 - net.core)
            pltpu.make_async_remote_copy(
                src_ref=ref, dst_ref=ref, send_sem=self.sems.at[0, 5, part, other],
                recv_sem=self.sems.at[1, 5, part, other], device_id=(net.dp, other), device_id_type=MESH).wait_recv()
            value = value + self.g[other, 3, 1 - net.core, :, self.lanes(part)].astype(F32)
        return value

    def drain(self):
        net = self.net
        for part in range(2):

            def body(m, c, part=part):
                for copy in self.across_copies(part, m) + self.side_copies(part, m):
                    copy.wait_send()

                @pl.when(m != net.z)
                def _():
                    self.z_copy(part, m).wait_send()

                return c

            lax.fori_loop(0, 4, body, 0)


def greet(net):
    barrier = pltpu.get_barrier_semaphore()
    for other in range(1, 8):
        pl.semaphore_signal(barrier, inc=1, device_id=(lax.rem(net.dp + other, 8), net.z), device_id_type=MESH)
    for k in range(1, 4):
        pl.semaphore_signal(barrier, inc=1, device_id=net.up(k), device_id_type=MESH)
    pl.semaphore_wait(barrier, 10)


def share_gains(net, parts, send, recv):
    copies = []
    for k in range(1, 8):
        copies.append(pltpu.make_async_remote_copy(
            src_ref=parts.at[net.dp], dst_ref=parts.at[net.dp], send_sem=send.at[k - 1], recv_sem=recv.at[net.dp],
            device_id=(lax.rem(net.dp + k, 8), net.z), device_id_type=MESH))
        copies[-1].start()
    return copies


def join_gains(net, parts, send, recv, gain):
    for k in range(1, 8):
        other = lax.rem(net.dp + k, 8)
        pltpu.make_async_remote_copy(
            src_ref=parts.at[other], dst_ref=parts.at[other], send_sem=send.at[k - 1], recv_sem=recv.at[other],
            device_id=net.sibling, device_id_type=MESH).wait_recv()
    total = jnp.zeros(gain.shape, F32)
    for d in range(8):
        piece = jnp.concatenate([parts[d], jnp.zeros((8, gain.shape[1] - 128), F32)], axis=1)
        total = total + pltpu.roll(piece, 96 * d, 1)
    gain[...] = total


def build_package(w, net, q_ref, k_ref, v_ref, o_ref, g_ref, u_ref, d_ref):
    lanes = low_lanes()
    ot = o_ref[...].T
    pad = jnp.zeros((96, 64), F32)
    at = (net.z, net.chip, net.core)

    def put(tile, value):
        w[at[0], at[1], at[2], :, 128 * tile : 128 * (tile + 1)] = value.astype(BF16)

    for j, ref in enumerate((q_ref, k_ref, v_ref)):
        put(2 * j, ref[:, 0:128])
        last = jnp.concatenate([ref[:, 128:192], pad], axis=1)
        extra = jnp.concatenate([ot[:, 64 * j : 64 * (j + 1)], pad], axis=1)
        put(2 * j + 1, jnp.where(lanes, last, pltpu.roll(extra, 64, 1)))
    w[at[0], at[1], at[2], :, 768:1280] = g_ref[...].astype(BF16)
    w[at[0], at[1], at[2], :, 1280:1792] = u_ref[...].astype(BF16)
    w[at[0], at[1], at[2], :, 1792:2304] = d_ref[...].T.astype(BF16)


def rows768(ref, m, lo, hi):
    return ref[m, :, :, :, lo:hi].reshape(768, hi - lo)


def put768(ref, m, lo, hi, value):
    ref[m, :, :, :, lo:hi] = value.reshape(4, 2, 96, hi - lo)


def mega_kernel(
    len_ref, x_ref, dy_ref, q_ref, k_ref, v_ref, o_ref, gate_ref, up_ref, down_ref, ga_ref, gf_ref,
    out_ref, gt_ref, gq_ref, gk_ref, gv_ref, go_ref, gate_grad_ref, up_grad_ref, down_grad_ref, gga_ref, ggf_ref, bins_ref,
    w, g, slots, pool, gain, gain_parts, gg_out, gg_in, gg_z, bias, n1t, n2t, dypt, n_b, qkv, qkv_b, o_own, o_b, do, wo, lse, lse_t,
    h, acc, res,
    ag_send, ag_send_z, ag_recv, gn_send, gn_recv, in_sem, rs_sems, ok, gt_send, gt_recv, gt_ok, bin_sem, out_sem, gs_send,
    gs_recv, gz_send, gz_recv,
):
    net = Net()
    bins = 4
    seq = 1536
    me = net.z
    xp, dyp, n1, n2 = (pool.at[j] for j in range(4))
    halves = []
    for t, ref in enumerate((x_ref, dy_ref)):
        for j in range(2):
            halves.append(pltpu.make_async_copy(
                ref.at[j], g.at[t, :, :, :, 768 * j : 768 * (j + 1)], in_sem.at[2 * t + j]))
    for copy in halves:
        copy.start()
    ag = Gather(net, w, ag_send, ag_send_z, ag_recv)
    rs = Reduce(net, g, slots, rs_sems, ok)
    build_package(w, net, q_ref, k_ref, v_ref, o_ref, gate_ref, up_ref, down_ref)
    pad = jnp.zeros((1, 32), F32)
    mine = jnp.concatenate([
        jnp.concatenate([ga_ref[...], pad], axis=1), jnp.concatenate([gf_ref[...], pad], axis=1),
        jnp.zeros((6, 128), F32)], axis=0)
    gain_parts[net.dp] = mine.astype(BF16).astype(F32)
    greet(net)
    gain_copies = share_gains(net, gain_parts, gn_send, gn_recv)
    ag.along_z(0)
    ag.spread(0, 0)

    place = placement(len_ref, bins)
    lse[...] = jnp.zeros_like(lse)

    def set_bias(b):
        _, segment = packed_source(place, b * CAP, (CAP, 1), 0)
        _, segment_row = packed_source(place, b * CAP, (1, CAP), 1)
        bias[...] = jnp.where(segment == segment_row, 0.0, NEG)

    def picks(b):
        source, _ = packed_source(place, b * CAP, (CAP, 1), 0)
        return (source == lax.broadcasted_iota(jnp.int32, (CAP, seq), 1)).astype(BF16)

    def packed(pick, t):
        return nn(pick[:, 0:768], rows768(g, t, 0, 768)) + nn(pick[:, 768:1536], rows768(g, t, 768, 1536))

    def drops(b, first, count):
        source, _ = packed_source(place, b * CAP, (1, CAP), 1)
        return (lax.broadcasted_iota(jnp.int32, (count, CAP), 0) + first == source).astype(BF16)

    def unpack(b, value):
        def body(j, c):
            at = pl.ds(pl.multiple_of(j * 256, 256), 256)
            out_ref[at, :] = (out_ref[at, :].astype(F32) + nn(drops(b, j * 256, 256), value)).astype(BF16)
            return c

        lax.fori_loop(0, seq // 256, body, 0)

    for copy in halves:
        copy.wait()
    pick = picks(me)
    xb = packed(pick, 0)
    xp[...] = xb.astype(BF16)
    h[...] = xb
    dyp[...] = packed(pick, 1).astype(BF16)
    set_bias(me)
    dypt[...] = dyp[...].T
    ag.spread(0, 1)
    ag.relay(0, 0)
    join_gains(net, gain_parts, gn_send, gn_recv, gain)
    g1 = gain[0:1, :]
    g2 = gain[1:2, :]
    xb = h[...]
    n1[...] = (xb * rms_rows(xb) * g1).astype(BF16)
    n1t[...] = n1[...].T
    ag.spread(0, 2)
    ag.across(0, 0)
    ag.relay(0, 1)
    ag.spread(0, 3)

    def bin_copy(k, up):
        there = bins_ref.at[k]
        return pltpu.make_async_copy(qkv_b.at[0], there, bin_sem) if up else pltpu.make_async_copy(there, qkv_b.at[0], bin_sem)

    def pack_others(k, c):
        b = lax.rem(me + 1 + k, bins)
        qkv_b[0] = packed(picks(b), 0).astype(BF16)
        copy = bin_copy(k, True)
        copy.start()
        copy.wait()
        return c

    lax.fori_loop(0, 3, pack_others, 0)

    def own_forward(i, c):
        m = net.group(i)

        @pl.when(i == 0)
        def _():
            ag.across(0, 1)
            ag.relay(0, 2)

        @pl.when(i == 1)
        def _():
            ag.across(0, 2)
            ag.relay(0, 3)
            ag.along_z(1)
            ag.spread(1, 0)

        @pl.when(i == 2)
        def _():
            ag.across(0, 3)
            ag.spread(1, 1)

        @pl.when(i == 3)
        def _():
            ag.relay(1, 0)

        ag.complete(0, i)
        first, second = out_weight_tiles_at(w, m)
        wo[m, :, 0:128] = first
        wo[m, :, 128:256] = second
        qkv[m] = nn(n1[...], rows768(w, m, 0, 768)).astype(BF16)
        attend_group(qkv, m, bias, o_own, m, lse)
        h[...] += nt(o_own[m], wo[m])
        return c

    lax.fori_loop(0, 4, own_forward, 0)
    def norm(dst, gain_row):
        def body(j, c):
            at = pl.ds(pl.multiple_of(j * 128, 128), 128)
            rows = h[at, :]
            dst[at, :] = (rows * rms_rows(rows) * gain_row).astype(BF16)
            return c

        lax.fori_loop(0, CAP // 128, body, 0)

    norm(n2, g2)
    n2t[...] = n2[...].T
    lse_t[...] = lse[...].T
    acc[...] = jnp.zeros_like(acc)
    res[...] = h[...]

    def ffn_back(i, c):
        m = net.group(i)
        ag.across(1, i)

        @pl.when(i < 3)
        def _():
            ag.relay(1, i + 1)

        @pl.when(i < 2)
        def _():
            ag.spread(1, i + 2)

        ag.complete(1, i)
        for lo in (0, 256):
            w_gate = rows768(w, m, 768 + lo, 1024 + lo)
            w_up = rows768(w, m, 1280 + lo, 1536 + lo)
            w_down = rows768(w, m, 1792 + lo, 2048 + lo)
            a = nn(n2[...], w_gate)
            up = nn(n2[...], w_up)
            t = gelu_parts(a)
            gel = 0.5 * a * (1.0 + t)
            u = (gel * up).astype(BF16)
            res[...] += nt(u, w_down)
            put768(g, m, 1792 + lo, 2048 + lo, nn(dypt[...], u).astype(BF16))
            du = nn(dyp[...], w_down)
            slope = 0.5 * (1.0 + t) + 0.5 * a * (1.0 - t * t) * (GELU_COEF * (1.0 + 3.0 * GELU_CUBE * a * a))
            da = (du * up * slope).astype(BF16)
            db = (du * gel).astype(BF16)
            put768(g, m, 768 + lo, 1024 + lo, nn(n2t[...], da).astype(BF16))
            put768(g, m, 1280 + lo, 1536 + lo, nn(n2t[...], db).astype(BF16))
            acc[...] += nt(da, w_gate) + nt(db, w_up)

        @pl.when(i < 2)
        def _():
            rs.to_core(1, i, False)

        @pl.when(i >= 2)
        def _():
            rs.to_core(1, i, True)

        @pl.when(jnp.logical_and(i >= 1, i < 3))
        def _():
            rs.from_core(1, i - 1, (1, i + 1))

        @pl.when(i == 3)
        def _():
            rs.from_core(1, 2, (0, 0))

        return c

    lax.fori_loop(0, 4, ffn_back, 0)
    out_ref[...] = jnp.zeros_like(out_ref)
    unpack(me, res[...].astype(BF16))
    def hidden_back(j, total):
        at = pl.ds(pl.multiple_of(j * 128, 128), 128)
        hb = h[at, :]
        r2 = rms_rows(hb)
        dn2 = acc[at, :]
        wg = dn2 * g2
        dh = dyp[at, :].astype(F32) + r2 * wg - hb * (r2 * r2 * r2) * jnp.mean(wg * hb, axis=1, keepdims=True)
        h[at, :] = dh
        n2[at, :] = dh.astype(BF16)
        acc[at, :] = jnp.zeros_like(dh)
        return total + jnp.sum(dn2 * hb * r2, axis=0, keepdims=True)

    gg_ffn = lax.fori_loop(0, CAP // 128, hidden_back, jnp.zeros((1, 768), F32))
    n2t[...] = n2[...].T
    rs.from_core(1, 3, (0, 1))
    rs.start_across(1, 0)

    def attn_back(i, c):
        m = net.group(i)
        do[0] = nn(n2[...], wo[m]).astype(BF16)
        attend_group_back(qkv, m, bias, lse_t, do, 0, qkv)
        acc[...] += nt(qkv[m], rows768(w, m, 0, 768))

        rs.start_sides(1, i)

        @pl.when(i < 3)
        def _():
            rs.start_across(1, i + 1)

        return c

    lax.fori_loop(0, 4, attn_back, 0)
    def input_back(j, total):
        at = pl.ds(pl.multiple_of(j * 128, 128), 128)
        xb = xp[at, :].astype(F32)
        r1 = rms_rows(xb)
        dn1 = acc[at, :]
        wa = dn1 * g1
        gt = h[at, :] + r1 * wa - xb * (r1 * r1 * r1) * jnp.mean(wa * xb, axis=1, keepdims=True)
        n_b[at, :] = gt.astype(BF16)
        return total + jnp.sum(dn1 * xb * r1, axis=0, keepdims=True)

    gg_attn = lax.fori_loop(0, CAP // 128, input_back, jnp.zeros((1, 768), F32))
    pool[me] = n_b[...]
    for k in range(1, 4):
        pl.semaphore_signal(gt_ok.at[me], inc=1, device_id=net.up(k), device_id_type=MESH)
    gt_copies = []
    for k in range(1, 4):
        pl.semaphore_wait(gt_ok.at[lax.rem(me + k, 4)], 1)
        gt_copies.append(pltpu.make_async_remote_copy(
            src_ref=pool.at[me], dst_ref=pool.at[me], send_sem=gt_send.at[k - 1], recv_sem=gt_recv.at[me],
            device_id=net.up(k), device_id_type=MESH))
        gt_copies[-1].start()
    gg = jnp.concatenate([gg_attn, gg_ffn, jnp.zeros((6, 768), F32)], axis=0)
    for d in range(8):
        gg_out[d] = pltpu.roll(gg, (768 - 96 * d) % 768, 1)[:, 0:128] if d else gg[:, 0:128]

    def gg_copy(k):
        to = lax.rem(net.dp + k, 8)
        return pltpu.make_async_remote_copy(
            src_ref=gg_out.at[to], dst_ref=gg_in.at[net.dp], send_sem=gs_send.at[k - 1], recv_sem=gs_recv.at[net.dp],
            device_id=(to, net.z), device_id_type=MESH)

    for k in range(1, 8):
        gg_copy(k).start()

    def attn_grads(i, c):
        m = net.group(i)
        go = nn(n2t[...], o_own[m])
        lanes = low_lanes()
        for j in range(3):
            grad = nn(n1t[...], qkv[m, :, 256 * j : 256 * (j + 1)])
            put768(g, m, 256 * j, 256 * j + 128, grad[:, 0:128].astype(BF16))
            if j == 1:
                extra = go[:, 0:128]
            else:
                extra = pltpu.roll(go[:, 64 * j : 64 * j + 128], 64, 1)
            put768(g, m, 256 * j + 128, 256 * (j + 1), jnp.where(lanes, grad[:, 128:256], extra).astype(BF16))

        rs.to_core(0, i, True)

        @pl.when(jnp.logical_and(i >= 1, i < 3))
        def _():
            rs.from_core(0, i - 1, (0, i + 1))

        @pl.when(i == 3)
        def _():
            rs.from_core(0, 2, None)

        return c

    lax.fori_loop(0, 4, attn_grads, 0)
    rs.from_core(0, 3, None)

    part = gg_out[net.dp]
    for k in range(1, 8):
        other = lax.rem(net.dp + k, 8)
        pltpu.make_async_remote_copy(
            src_ref=gg_out.at[other], dst_ref=gg_in.at[other], send_sem=gs_send.at[k - 1], recv_sem=gs_recv.at[other],
            device_id=net.sibling, device_id_type=MESH).wait_recv()
        part = part + gg_in[other]
    gg_z[me] = part
    gz_copies = [pltpu.make_async_remote_copy(
        src_ref=gg_z.at[me], dst_ref=gg_z.at[me], send_sem=gz_send.at[k - 1], recv_sem=gz_recv.at[me],
        device_id=net.up(k), device_id_type=MESH) for k in range(1, 4)]
    for copy in gz_copies:
        copy.start()

    def others(k, c):
        b = lax.rem(me + 1 + k, bins)
        copy = bin_copy(k, False)
        copy.start()
        set_bias(b)
        copy.wait()
        h[...] = qkv_b[0].astype(F32)
        norm(n_b, g1)

        def attend(m, c):
            qkv_b[0] = nn(n_b[...], rows768(w, m, 0, 768)).astype(BF16)
            attend_group(qkv_b, 0, bias, o_b, 0)
            h[...] += nt(o_b[0], wo[m])

            @pl.when(jnp.logical_and(k == 0, m == 0))
            def _():
                rs.start_z(1, 0)

            @pl.when(jnp.logical_and(k == 0, m == 1))
            def _():
                rs.start_z(1, 1)

            @pl.when(jnp.logical_and(k == 0, m == 2))
            def _():
                rs.start_across(0, 0)
                rs.start_across(0, 1)
                rs.start_z(1, 2)

            @pl.when(jnp.logical_and(k == 0, m == 3))
            def _():
                rs.start_sides(0, 0)
                rs.start_sides(0, 1)
                rs.start_z(1, 3)

            @pl.when(jnp.logical_and(k == 1, m == 0))
            def _():
                rs.start_across(0, 2)
                rs.start_across(0, 3)
                rs.start_z(0, 0)

            @pl.when(jnp.logical_and(k == 1, m == 1))
            def _():
                rs.start_sides(0, 2)
                rs.start_sides(0, 3)
                rs.start_z(0, 1)

            @pl.when(jnp.logical_and(k == 1, m == 3))
            def _():
                rs.start_z(0, 2)
                rs.start_z(0, 3)

            return c

        lax.fori_loop(0, 4, attend, 0)
        norm(n_b, g2)

        def ffn(m, c):
            a = nn(n_b[...], rows768(w, m, 768, 1280))
            up = nn(n_b[...], rows768(w, m, 1280, 1792))
            u = (0.5 * a * (1.0 + gelu_parts(a)) * up).astype(BF16)
            h[...] += nt(u, rows768(w, m, 1792, 2304))
            return c

        lax.fori_loop(0, 4, ffn, 0)
        unpack(b, h[...].astype(BF16))
        return c

    lax.fori_loop(0, 3, others, 0)

    rows = (h, acc, res)
    for j in range(3):
        rows[j][...] = nn(drops(me, CAP * j, CAP), pool[me])
    for k in (1, 3, 2):
        other = lax.rem(me + k, 4)
        pltpu.make_async_remote_copy(
            src_ref=pool.at[other], dst_ref=pool.at[other], send_sem=gt_send.at[k - 1], recv_sem=gt_recv.at[other],
            device_id=net.up(k), device_id_type=MESH).wait_recv()
        for j in range(3):
            rows[j][...] += nn(drops(other, CAP * j, CAP), pool[other])
    outs = [pltpu.make_async_copy(rows[j], gt_ref.at[j], out_sem.at[j]) for j in range(3)]
    for copy in outs:
        copy.start()

    for k in range(1, 4):
        other = lax.rem(me + k, 4)
        pltpu.make_async_remote_copy(
            src_ref=gg_z.at[other], dst_ref=gg_z.at[other], send_sem=gz_send.at[k - 1], recv_sem=gz_recv.at[other],
            device_id=net.up(k), device_id_type=MESH).wait_recv()
        part = part + gg_z[other]
    gga_ref[...] = part[0:1, 0:96]
    ggf_ref[...] = part[1:2, 0:96]
    ffn_sum = rs.total(1)
    gate_grad_ref[...] = ffn_sum[:, 0:512]
    up_grad_ref[...] = ffn_sum[:, 512:1024]
    down_grad_ref[...] = ffn_sum[:, 1024:1536].T
    attn_sum = rs.total(0)
    gq_ref[...] = attn_sum[:, 0:192]
    gk_ref[...] = attn_sum[:, 256:448]
    gv_ref[...] = attn_sum[:, 512:704]
    go_ref[...] = jnp.concatenate([attn_sum[:, 192:256], attn_sum[:, 448:512], attn_sum[:, 704:768]], axis=1).T
    for copy in outs:
        copy.wait()
    for copy in gain_copies + gt_copies + gz_copies:
        copy.wait_send()
    for k in range(1, 8):
        gg_copy(k).wait_send()
    rs.drain()
    ag.drain()


def out_weight_tiles_at(w, m):
    lanes = low_lanes()
    t1 = rows768(w, m, 128, 256).astype(F32)
    t3 = rows768(w, m, 384, 512).astype(F32)
    t5 = rows768(w, m, 640, 768).astype(F32)
    first = jnp.where(lanes, pltpu.roll(t1, 64, 1), t3)
    second = jnp.where(lanes, pltpu.roll(t5, 64, 1), 0.0)
    return first.astype(BF16), second.astype(BF16)


def on_this_slice(
    tokens, lengths, query_weight, key_weight, value_weight, out_weight, attn_gain, gate_weight, up_weight, down_weight,
    ffn_gain, cotangent,
):
    rows, seq, width = tokens.shape
    vmem = pl.BlockSpec(memory_space=pltpu.VMEM)
    smem = pl.BlockSpec(memory_space=pltpu.SMEM)
    dma = pltpu.SemaphoreType.DMA
    act = pltpu.VMEM((CAP, width), BF16)
    act_t = pltpu.VMEM((width, CAP), BF16)
    wide = pltpu.VMEM((CAP, width), F32)
    hbm = pl.BlockSpec(memory_space=pl.ANY)

    def f32(*shape):
        return jax.ShapeDtypeStruct(shape, F32)

    out, gt, gq, gk, gv, go, gate, up, down, gain_a, gain_f, _ = pl.pallas_call(
        mega_kernel,
        out_shape=(
            jax.ShapeDtypeStruct((seq, width), BF16), f32(3, CAP, width), f32(96, 192), f32(96, 192), f32(96, 192), f32(192, 96),
            f32(96, 512), f32(96, 512), f32(512, 96), f32(1, 96), f32(1, 96), jax.ShapeDtypeStruct((3, CAP, width), BF16),
        ),
        in_specs=[smem, hbm, hbm] + [vmem] * 9,
        out_specs=[vmem, hbm] + [vmem] * 9 + [hbm],
        scratch_shapes=[
            pltpu.VMEM((4, 4, 2, 96, 2304), BF16),
            pltpu.VMEM((4, 4, 2, 96, 2304), BF16),
            pltpu.VMEM((2, 4, 96, 1536), BF16),
            pltpu.VMEM((4, CAP, width), BF16),
            pltpu.VMEM((8, width), F32),
            pltpu.VMEM((8, 8, 128), F32), pltpu.VMEM((8, 8, 128), F32), pltpu.VMEM((8, 8, 128), F32),
            pltpu.VMEM((4, 8, 128), F32),
            pltpu.VMEM((CAP, CAP), F32),
            act_t, act_t, act_t, act,
            pltpu.VMEM((4, CAP, width), BF16),
            pltpu.VMEM((1, CAP, width), BF16),
            pltpu.VMEM((4, CAP, 256), BF16),
            pltpu.VMEM((1, CAP, 256), BF16),
            pltpu.VMEM((1, CAP, 256), BF16),
            pltpu.VMEM((4, width, 256), BF16),
            pltpu.VMEM((CAP, 128), F32),
            pltpu.VMEM((128, CAP), F32),
            wide, wide, wide,
            dma((2, 4, 4, 3)), dma((2, 3)), dma((2, 4, 4, 2)), dma((7,)), dma((8,)), dma((4,)),
            dma((2, 6, 2, 4)), pltpu.SemaphoreType.REGULAR((4, 2, 4)),
            dma((3,)), dma((4,)), pltpu.SemaphoreType.REGULAR((4,)), dma, dma((3,)), dma((7,)), dma((8,)), dma((3,)), dma((4,)),
        ],
        compiler_params=pltpu.CompilerParams(
            vmem_limit_bytes=60 * 2**20, collective_id=0, has_side_effects=True),
        name="layer",
    )(lengths, tokens.reshape(2, 4, 2, 96, width), cotangent.reshape(2, 4, 2, 96, width), query_weight, key_weight,
      value_weight, out_weight, gate_weight, up_weight, down_weight, attn_gain.reshape(1, 96), ffn_gain.reshape(1, 96))
    return (
        out.reshape(rows, seq, width), gt.reshape(rows, seq, width), gq, gk, gv, go, gain_a.reshape(96), gate, up, down,
        gain_f.reshape(96),
    )
def solution(mesh):
    body = on_this_slice if dict(mesh.shape) == {"dp": 8, "mp": 4} else per_device
    return jax.shard_map(
        body,
        mesh=mesh,
        in_specs=(
            P("dp", None, None), P("dp", None), P("dp", "mp"), P("dp", "mp"), P("dp", "mp"), P("mp", "dp"), P("dp"),
            P("dp", "mp"), P("dp", "mp"), P("mp", "dp"), P("dp"), P("dp", None, None),
        ),
        out_specs=(
            P("dp", None, None), P("dp", None, None), P("dp", "mp"), P("dp", "mp"), P("dp", "mp"), P("mp", "dp"),
            P("dp"), P("dp", "mp"), P("dp", "mp"), P("mp", "dp"), P("dp"),
        ),
        check_vma=False,
    )
```

```python
import functools
import jax
import jax.numpy as jnp
from jax import lax
from jax.experimental import pallas as pl
from jax.experimental.pallas import tpu as pltpu
from jax.sharding import PartitionSpec as P

EPSILON = 1e-06
GELU_COEF = 0.7978845608028654
GELU_CUBE = 0.044715
CAP = 512
NEG = -1e30
F32 = jnp.float32
BF16 = jnp.bfloat16


def nn(a, b):
    return lax.dot_general(a, b, (((1,), (0,)), ((), ())), preferred_element_type=F32)


def nt(a, b):
    return lax.dot_general(a, b, (((1,), (1,)), ((), ())), preferred_element_type=F32)


def tn(a, b):
    return lax.dot_general(a, b, (((0,), (0,)), ((), ())), preferred_element_type=F32)


def placement(len_ref, bins):
    count = len_ref.shape[1]
    sizes = [len_ref[0, i] for i in range(count)]
    starts = [jnp.int32(0)]
    for i in range(count - 1):
        starts.append(starts[-1] + sizes[i])
    ranks = []
    for i in range(count):
        rank = jnp.int32(0)
        for j in range(count):
            if j < i:
                rank = rank + jnp.where(sizes[j] >= sizes[i], 1, 0)
            elif j > i:
                rank = rank + jnp.where(sizes[j] > sizes[i], 1, 0)
        ranks.append(rank)
    fills = [jnp.int32(0)] * (bins - 1)
    spots = [jnp.int32(0)] * count
    for k in range(count):
        size = jnp.int32(0)
        for i in range(count):
            size = size + jnp.where(ranks[i] == k, sizes[i], 0)
        if k == 0:
            spot = jnp.int32((bins - 1) * CAP)
        else:
            free = jnp.int32(1)
            spot = jnp.int32(0)
            for b in range(bins - 1):
                fits = jnp.where(fills[b] + size <= CAP, free, 0) if b < bins - 2 else free
                spot = spot + fits * (b * CAP + fills[b])
                fills[b] = fills[b] + fits * size
                free = free - fits
        for i in range(count):
            spots[i] = spots[i] + jnp.where(ranks[i] == k, spot, 0)
    return starts, sizes, spots


def packed_source(place, first, shape, axis):
    spot = lax.broadcasted_iota(jnp.int32, shape, axis) + first
    source = jnp.full(shape, -1, jnp.int32)
    segment = jnp.full(shape, -1, jnp.int32)
    for i, (start, size, at) in enumerate(zip(*place)):
        here = (spot >= at) & (spot < at + size)
        source = jnp.where(here, spot + (start - at), source)
        segment = jnp.where(here, i, segment)
    return source, segment


def low_lanes():
    return lax.broadcasted_iota(jnp.int32, (1, 128), 1) < 64


def half(tile, low):
    lanes = low_lanes()
    return jnp.where(lanes if low else jnp.logical_not(lanes), tile, jnp.zeros_like(tile))


HEADS = ((0, 2, 4, True), (0, 2, 4, False), (1, 3, 5, True))


def tile_of(ref, m, t, rows=slice(None)):
    return ref[m, rows, 128 * t : 128 * (t + 1)]


def attend_group(qkv, m, bias, o_ref, at, lse_ref=None, qb=256):
    for i in range(CAP // qb):
        rows = slice(i * qb, (i + 1) * qb)
        scores = []
        for tq, tk, tv, low in HEADS:
            q = half(tile_of(qkv, m, tq, rows), low) * jnp.asarray(0.125, BF16)
            scores.append(nt(q, tile_of(qkv, m, tk)))
        shares, totals = [], []
        for head, s in enumerate(scores):
            s = s + bias[rows, :]
            top = jnp.max(s, axis=1, keepdims=True)
            e = jnp.exp(s - top)
            total = jnp.sum(e, axis=1, keepdims=True)
            shares.append(e.astype(BF16))
            totals.append(total)
            if lse_ref is not None:
                lane = lax.broadcasted_iota(jnp.int32, (1, 128), 1)
                lse_ref[rows, :] = jnp.where(lane == 3 * m + head, top + jnp.log(total), lse_ref[rows, :])
        parts = []
        for (tq, tk, tv, low), e, total in zip(HEADS, shares, totals):
            parts.append(nn(e, half(tile_of(qkv, m, tv), low)) * (1.0 / total))
        o_ref[at, rows, 0:128] = (parts[0] + parts[1]).astype(BF16)
        o_ref[at, rows, 128:256] = parts[2].astype(BF16)


def attend_group_back(qkv, m, bias, lse_t, do_ref, at, dqkv):
    dk = [None, None]
    dv = [None, None]
    dq = [None, None]
    scale = jnp.asarray(0.125, BF16)
    for head, (tq, tk, tv, low) in enumerate(HEADS):
        j = 0 if head < 2 else 1
        k = half(tile_of(qkv, m, tk), low) * scale
        s = nt(k, tile_of(qkv, m, tq))
        do = do_ref[at, :, 128 * j : 128 * (j + 1)]
        dp = nt(half(tile_of(qkv, m, tv), low), do)
        p = jnp.exp(s + bias[...] - lse_t[pl.ds(3 * m + head, 1), :])
        delta = jnp.sum(p * dp, axis=0, keepdims=True)
        ds = (p * (dp - delta)).astype(BF16)
        parts = (
            nn(p.astype(BF16), half(do, low)), nn(ds, half(tile_of(qkv, m, tq), low) * scale), tn(ds, k))
        for total, part in zip((dv, dk, dq), parts):
            total[j] = part if total[j] is None else total[j] + part
    for j in range(2):
        for t, total in ((0, dq), (2, dk), (4, dv)):
            dqkv[m, :, 128 * (t + j) : 128 * (t + j + 1)] = total[j].astype(BF16)


def out_weight_tiles(w, m):
    lanes = low_lanes()
    t1 = tile_of(w, m, 1).astype(F32)
    t3 = tile_of(w, m, 3).astype(F32)
    t5 = tile_of(w, m, 5).astype(F32)
    first = jnp.where(lanes, pltpu.roll(t1, 64, 1), t3)
    second = jnp.where(lanes, pltpu.roll(t5, 64, 1), 0.0)
    return first.astype(BF16), second.astype(BF16)


def gelu_parts(a):
    inner = GELU_COEF * (a + GELU_CUBE * a * a * a)
    t = jnp.tanh(inner)
    return t


def rms_rows(values):
    return lax.rsqrt(jnp.mean(values * values, axis=1, keepdims=True) + EPSILON)


def layer_kernel(
    len_ref, x_ref, dy_ref, w_ref, gain_ref, which_ref,
    out_ref, gt_ref, g_ref, gg_ref,
    bias, xp, dyp, n1, n1t, n2, n2t, dypt, dhbt, qkv, o_all, wo, lse, lse_t, do, dqkv, h, acc,
):
    bins = w_ref.shape[0]
    seq = x_ref.shape[0]
    place = placement(len_ref, bins)
    me = which_ref[0]
    g1 = gain_ref[0:1, :]
    g2 = gain_ref[1:2, :]

    def wo_body(m, c):
        first, second = out_weight_tiles(w_ref, m)
        wo[m, :, 0:128] = first
        wo[m, :, 128:256] = second
        return c

    lax.fori_loop(0, bins, wo_body, 0)
    lse[...] = jnp.zeros_like(lse)

    def forward(b):
        source, segment = packed_source(place, b * CAP, (CAP, 1), 0)
        _, segment_row = packed_source(place, b * CAP, (1, CAP), 1)
        bias[...] = jnp.where(segment == segment_row, 0.0, NEG)
        pick = (source == lax.broadcasted_iota(jnp.int32, (CAP, seq), 1)).astype(BF16)
        xb = nn(pick, x_ref[...])
        xp[...] = xb.astype(BF16)
        dyp[...] = nn(pick, dy_ref[...]).astype(BF16)
        n1[...] = (xb * rms_rows(xb) * g1).astype(BF16)
        h[...] = xb

        def m_body(m, c):
            qkv[m] = nn(n1[...], w_ref[m, :, 0:768]).astype(BF16)
            attend_group(qkv, m, bias, o_all, m, lse)
            h[...] += nt(o_all[m], wo[m])
            return c

        lax.fori_loop(0, bins, m_body, 0)
        hb = h[...]
        n2[...] = (hb * rms_rows(hb) * g2).astype(BF16)

    def ffn_out(b):
        acc[...] = h[...]

        def m_body(m, c):
            a = nn(n2[...], w_ref[m, :, 768:1280])
            up = nn(n2[...], w_ref[m, :, 1280:1792])
            u = (0.5 * a * (1.0 + gelu_parts(a)) * up).astype(BF16)
            acc[...] += nt(u, w_ref[m, :, 1792:2304])
            return c

        lax.fori_loop(0, bins, m_body, 0)
        source, _ = packed_source(place, b * CAP, (1, CAP), 1)
        drop = (lax.broadcasted_iota(jnp.int32, (seq, CAP), 0) == source).astype(BF16)
        out_ref[...] = (out_ref[...].astype(F32) + nn(drop, acc[...].astype(BF16))).astype(BF16)

    out_ref[...] = jnp.zeros_like(out_ref)

    def others(i, c):
        b = lax.rem(me + 1 + i, bins)
        forward(b)
        ffn_out(b)
        return c

    lax.fori_loop(0, bins, others, 0)

    n1t[...] = n1[...].T
    n2t[...] = n2[...].T
    dypt[...] = dyp[...].T
    lse_t[...] = lse[...].T
    acc[...] = jnp.zeros_like(acc)

    def ffn_back(m, c):
        a = nn(n2[...], w_ref[m, :, 768:1280])
        up = nn(n2[...], w_ref[m, :, 1280:1792])
        t = gelu_parts(a)
        gel = 0.5 * a * (1.0 + t)
        u = (gel * up).astype(BF16)
        du = nn(dyp[...], w_ref[m, :, 1792:2304])
        slope = 0.5 * (1.0 + t) + 0.5 * a * (1.0 - t * t) * (GELU_COEF * (1.0 + 3.0 * GELU_CUBE * a * a))
        da = (du * up * slope).astype(BF16)
        db = (du * gel).astype(BF16)
        g_ref[m, :, 1792:2304] = nn(dypt[...], u).astype(BF16)
        g_ref[m, :, 768:1280] = nn(n2t[...], da).astype(BF16)
        g_ref[m, :, 1280:1792] = nn(n2t[...], db).astype(BF16)
        acc[...] += nt(da, w_ref[m, :, 768:1280]) + nt(db, w_ref[m, :, 1280:1792])
        return c

    lax.fori_loop(0, bins, ffn_back, 0)
    hb = h[...]
    r2 = rms_rows(hb)
    dn2 = acc[...]
    gg_ffn = jnp.sum(dn2 * hb * r2, axis=0, keepdims=True)
    wg = dn2 * g2
    dh = dyp[...].astype(F32) + r2 * wg - hb * (r2 * r2 * r2) * jnp.mean(wg * hb, axis=1, keepdims=True)
    h[...] = dh
    dhb = dh.astype(BF16)
    dhbt[...] = dhb.T
    n2[...] = dhb
    acc[...] = jnp.zeros_like(acc)

    def attn_back(m, c):
        do[m] = nn(n2[...], wo[m]).astype(BF16)
        attend_group_back(qkv, m, bias, lse_t, do, m, dqkv)
        acc[...] += nt(dqkv[m], w_ref[m, :, 0:768])
        grad = nn(n1t[...], dqkv[m])
        go = nn(dhbt[...], o_all[m])
        lanes = low_lanes()
        for t in range(6):
            g = grad[:, 128 * t : 128 * (t + 1)]
            if t == 1:
                g = jnp.where(lanes, g, pltpu.roll(go[:, 0:128], 64, 1))
            elif t == 3:
                g = jnp.where(lanes, g, go[:, 0:128])
            elif t == 5:
                g = jnp.where(lanes, g, pltpu.roll(go[:, 128:256], 64, 1))
            g_ref[m, :, 128 * t : 128 * (t + 1)] = g.astype(BF16)
        return c

    lax.fori_loop(0, bins, attn_back, 0)
    xb = xp[...].astype(F32)
    r1 = rms_rows(xb)
    dn1 = acc[...]
    gg_attn = jnp.sum(dn1 * xb * r1, axis=0, keepdims=True)
    wa = dn1 * g1
    gt = h[...] + r1 * wa - xb * (r1 * r1 * r1) * jnp.mean(wa * xb, axis=1, keepdims=True)
    gt_ref[...] = gt.astype(BF16)
    gg_ref[0:1, :] = gg_attn
    gg_ref[1:2, :] = gg_ffn


def unpack_kernel(len_ref, gt_ref, out_ref):
    bins = gt_ref.shape[0]
    seq = out_ref.shape[0]
    place = placement(len_ref, bins)
    total = jnp.zeros(out_ref.shape, F32)
    for b in range(bins):
        source, _ = packed_source(place, b * CAP, (1, CAP), 1)
        drop = (lax.broadcasted_iota(jnp.int32, (seq, CAP), 0) == source).astype(BF16)
        total = total + nn(drop, gt_ref[b])
    out_ref[...] = total


def per_device(
    tokens, lengths, query_weight, key_weight, value_weight, out_weight, attn_gain, gate_weight, up_weight, down_weight,
    ffn_gain, cotangent,
):
    rows, seq, width = tokens.shape
    bins = lax.axis_size("mp")
    q, k, v, o = (w.astype(BF16) for w in (query_weight, key_weight, value_weight, out_weight.T))
    package = jnp.concatenate(
        [q, o[:, 0:64], k, o[:, 64:128], v, o[:, 128:192], gate_weight.astype(BF16), up_weight.astype(BF16),
         down_weight.T.astype(BF16)], axis=1)
    w = lax.all_gather(lax.all_gather(package, "dp", axis=0, tiled=True), "mp", axis=0)
    gains = jnp.stack([attn_gain, ffn_gain]).astype(BF16)
    gains = lax.all_gather(gains, "dp", axis=1, tiled=True).astype(F32)
    gains = jnp.concatenate([gains, jnp.zeros((6, width), F32)], axis=0)
    which = lax.axis_index("mp").astype(jnp.int32).reshape(1)
    vmem = pl.BlockSpec(memory_space=pltpu.VMEM)
    smem = pl.BlockSpec(memory_space=pltpu.SMEM)
    group = w.shape[2]
    x = tokens.reshape(seq, width)
    dy = cotangent.reshape(seq, width)
    out, gt, g, gg = pl.pallas_call(
        layer_kernel,
        out_shape=(
            jax.ShapeDtypeStruct((seq, width), BF16),
            jax.ShapeDtypeStruct((CAP, width), BF16),
            jax.ShapeDtypeStruct((bins, width, group), BF16),
            jax.ShapeDtypeStruct((8, width), F32),
        ),
        in_specs=[smem, vmem, vmem, vmem, vmem, smem],
        out_specs=[vmem] * 4,
        scratch_shapes=[
            pltpu.VMEM((CAP, CAP), F32),
            pltpu.VMEM((CAP, width), BF16),
            pltpu.VMEM((CAP, width), BF16),
            pltpu.VMEM((CAP, width), BF16),
            pltpu.VMEM((width, CAP), BF16),
            pltpu.VMEM((CAP, width), BF16),
            pltpu.VMEM((width, CAP), BF16),
            pltpu.VMEM((width, CAP), BF16),
            pltpu.VMEM((width, CAP), BF16),
            pltpu.VMEM((bins, CAP, width), BF16),
            pltpu.VMEM((bins, CAP, 256), BF16),
            pltpu.VMEM((bins, width, 256), BF16),
            pltpu.VMEM((CAP, 128), F32),
            pltpu.VMEM((128, CAP), F32),
            pltpu.VMEM((bins, CAP, 256), BF16),
            pltpu.VMEM((bins, CAP, width), BF16),
            pltpu.VMEM((CAP, width), F32),
            pltpu.VMEM((CAP, width), F32),
        ],
        compiler_params=pltpu.CompilerParams(vmem_limit_bytes=63 * 2**20+900000),
        name="layer",
    )(lengths, x, dy, w, gains, which)
    gt_all = lax.all_gather(gt, "mp", axis=0)
    grad_tokens = pl.pallas_call(
        unpack_kernel,
        out_shape=jax.ShapeDtypeStruct((seq, width), F32),
        in_specs=[smem, vmem],
        out_specs=vmem,
        compiler_params=pltpu.CompilerParams(vmem_limit_bytes=60 * 2**20),
        name="unpack",
    )(lengths, gt_all)
    g = lax.psum_scatter(g, "mp", scatter_dimension=0, tiled=False)
    g = lax.psum_scatter(g, "dp", scatter_dimension=0, tiled=True).astype(F32)
    gg = lax.psum_scatter(lax.psum(gg[0:2], "mp"), "dp", scatter_dimension=1, tiled=True)
    go = jnp.concatenate([g[:, 192:256], g[:, 448:512], g[:, 704:768]], axis=1).T
    return (
        out.reshape(rows, seq, width),
        grad_tokens.reshape(rows, seq, width),
        g[:, 0:192],
        g[:, 256:448],
        g[:, 512:704],
        go,
        gg[0],
        g[:, 768:1280],
        g[:, 1280:1792],
        g[:, 1792:2304].T,
        gg[1],
    )


MESH = pl.DeviceIdType.MESH
PARTS = ((0, 768), (768, 2304))


class Net:
    def __init__(self):
        self.dp = lax.axis_index("dp")
        self.z = lax.axis_index("mp")
        self.core = lax.rem(self.dp, 2)
        self.chip = lax.div(self.dp, 2)
        self.chip_x = self.chip + 1 - 2 * lax.rem(self.chip, 2)
        self.chip_y = lax.rem(self.chip + 2, 4)
        self.chip_d = 3 - self.chip
        self.sibling = (2 * self.chip + 1 - self.core, self.z)
        self.x = (2 * self.chip_x + self.core, self.z)
        self.y = (2 * self.chip_y + self.core, self.z)

    def up(self, k):
        return (self.dp, lax.rem(self.z + k, 4))

    def along(self, step):
        return (self.dp, lax.rem(self.z + 4 + step, 4))

    def group(self, i):
        z = self.z
        one = jnp.where(z == 0, 1, jnp.where(z == 1, 0, jnp.where(z == 2, 3, 2)))
        two = jnp.where(z < 2, 2, 1)
        return jnp.where(i == 0, z, jnp.where(i == 1, one, jnp.where(i == 2, two, 6 - z - one - two)))


class Gather:
    def __init__(self, net, w, send, recv):
        self.net, self.w, self.send, self.recv = net, w, send, recv

    def copy(self, part, m, chip, core, kind, to, rows=None):
        lo, hi = PARTS[part]
        first, last, mark = (0, 96, 0) if rows is None else (48 * rows, 48 * (rows + 1), 1 + rows)
        ref = self.w.at[m, chip, core, first:last, lo:hi]
        return pltpu.make_async_remote_copy(
            src_ref=ref, dst_ref=ref, send_sem=self.send.at[part, m, chip, kind],
            recv_sem=self.recv.at[part, m, chip, core, mark], device_id=to, device_id_type=MESH)

    def wait(self, part, m, chip, core, rows=None):
        self.copy(part, m, chip, core, 0, self.net.sibling, rows).wait_recv()

    def each_along_z(self, part, m, act):
        net = self.net

        @pl.when(jnp.logical_and(m <= net.z, net.z < 3))
        def _():
            act(self.copy(part, m, net.chip, net.core, 3, net.along(1)))

        @pl.when(jnp.logical_and(m >= net.z, net.z > 0))
        def _():
            act(self.copy(part, m, net.chip, net.core, 4, net.along(-1)))

    def own_copies(self, part, m):
        net = self.net
        return [self.copy(part, m, net.chip, net.core, k, to) for k, to in enumerate((net.x, net.y, net.sibling))]

    def relay_copies(self, part, m):
        net = self.net
        return [
            self.copy(part, m, net.chip_x, net.core, 0, net.y, 0), self.copy(part, m, net.chip_x, net.core, 2, net.sibling),
            self.copy(part, m, net.chip_y, net.core, 1, net.x, 1), self.copy(part, m, net.chip_y, net.core, 2, net.sibling)]

    def spread(self, part, i):
        net = self.net
        m = net.group(i)
        if not isinstance(i, int) or i > 0:
            self.wait(part, m, net.chip, net.core)
        self.each_along_z(part, m, lambda copy: copy.start())
        for copy in self.own_copies(part, m):
            copy.start()

    def relay(self, part, i):
        net = self.net
        m = net.group(i)
        copies = self.relay_copies(part, m)
        for j, chip in enumerate((net.chip_x, net.chip_y)):
            self.wait(part, m, chip, net.core)
            copies[2 * j].start()
            copies[2 * j + 1].start()

    def across(self, part, i):
        net = self.net
        m = net.group(i)
        self.wait(part, m, net.chip_d, net.core, 0)
        self.wait(part, m, net.chip_d, net.core, 1)
        self.copy(part, m, net.chip_d, net.core, 2, net.sibling).start()

    def complete(self, part, i):
        net = self.net
        m = net.group(i)
        for chip in range(4):
            self.wait(part, m, chip, 1 - net.core)

    def drain(self):
        net = self.net
        for part in range(2):

            def body(m, c, part=part):
                self.each_along_z(part, m, lambda copy: copy.wait_send())
                for copy in self.own_copies(part, m) + self.relay_copies(part, m):
                    copy.wait_send()
                self.copy(part, m, net.chip_d, net.core, 2, net.sibling).wait_send()
                return c

            lax.fori_loop(0, 4, body, 0)


class Reduce:
    def __init__(self, net, g, slots, zbuf, sems, ok):
        self.net, self.g, self.slots, self.zbuf, self.sems, self.ok = net, g, slots, zbuf, sems, ok

    def lanes(self, part):
        return slice(*PARTS[part])

    def unit(self, part, m, chip, core, rows=slice(0, 96)):
        return self.g.at[m, chip, core, rows, self.lanes(part)]

    def copy(self, kind, part, key, src, dst, to):
        return pltpu.make_async_remote_copy(
            src_ref=src, dst_ref=dst, send_sem=self.sems.at[0, kind, part, key], recv_sem=self.sems.at[1, kind, part, key],
            device_id=to, device_id_type=MESH)

    def core_copy(self, part, i):
        m = self.net.group(i)
        lo, hi = PARTS[part]
        return self.copy(
            0, part, m, self.g.at[m, :, 1 - self.net.core, :, lo:hi],
            self.slots.at[lax.rem(i, 2), :, :, 0 : hi - lo], self.net.sibling)

    def to_core(self, part, i, credit):
        if credit:
            pl.semaphore_wait(self.ok.at[3, part, self.net.group(i)], 1)
        self.core_copy(part, i).start()

    def from_core(self, part, i, credit):
        net = self.net
        m = net.group(i)
        lo, hi = PARTS[part]
        copy = self.core_copy(part, i)
        copy.wait_recv()
        slot = lax.rem(i, 2)
        for chip in range(4):
            self.g[m, chip, net.core, :, lo:hi] = self.g[m, chip, net.core, :, lo:hi] + self.slots[slot, chip, :, 0 : hi - lo]
        if credit is not None:
            p, j = credit
            pl.semaphore_signal(self.ok.at[3, p, net.group(j)], inc=1, device_id=net.sibling, device_id_type=MESH)
        copy.wait_send()
        pl.semaphore_signal(self.ok.at[0, part, m], inc=1, device_id=net.x, device_id_type=MESH)
        pl.semaphore_signal(self.ok.at[1, part, m], inc=1, device_id=net.y, device_id_type=MESH)

        @pl.when(jnp.logical_and(m >= net.z, net.z > 0))
        def _():
            pl.semaphore_signal(self.ok.at[2, part, m], inc=1, device_id=net.along(-1), device_id_type=MESH)

        @pl.when(jnp.logical_and(m <= net.z, net.z < 3))
        def _():
            pl.semaphore_signal(self.ok.at[2, part, m], inc=1, device_id=net.along(1), device_id_type=MESH)

    def across_copies(self, part, m):
        net = self.net
        out = []
        for kind, rows, to in ((1, slice(0, 48), net.y), (2, slice(48, 96), net.x)):
            out.append(self.copy(
                kind, part, m, self.unit(part, m, net.chip_d, net.core, rows),
                self.unit(part, m, 0, 1 - net.core, rows), to))
        return out

    def side_copies(self, part, m):
        net = self.net
        return [
            self.copy(kind, part, m, self.unit(part, m, chip, net.core), self.unit(part, m, slot, 1 - net.core), to)
            for kind, chip, slot, to in ((3, net.chip_x, 1, net.x), (4, net.chip_y, 2, net.y))]

    def each_z(self, part, m, act):
        net = self.net
        z = net.z
        src = self.unit(part, m, net.chip, net.core)
        far = self.unit(part, m, 3, 1 - net.core)
        lo, hi = PARTS[part]
        near = self.zbuf.at[:, lo:hi]

        def copy(dst, kind, step):
            return pltpu.make_async_remote_copy(
                src_ref=src, dst_ref=dst, send_sem=self.sems.at[0, 5, part, m], recv_sem=self.sems.at[1, kind, part, m],
                device_id=net.along(step), device_id_type=MESH)

        for test, dst, kind, step in ((m > z, far, 5, 1), (m < z - 1, far, 5, -1), (m == z - 1, near, 6, -1)):

            @pl.when(test)
            def _(dst=dst, kind=kind, step=step):
                act(copy(dst, kind, step))

    def z_arrived(self, part, m, near):
        net = self.net
        lo, hi = PARTS[part]
        ref = self.zbuf.at[:, lo:hi] if near else self.unit(part, m, 3, 1 - net.core)
        pltpu.make_async_remote_copy(
            src_ref=ref, dst_ref=ref, send_sem=self.sems.at[0, 5, part, m],
            recv_sem=self.sems.at[1, 6 if near else 5, part, m], device_id=net.sibling, device_id_type=MESH).wait_recv()
        if near:
            mine = self.g[m, net.chip, net.core, :, lo:hi]
            self.g[m, net.chip, net.core, :, lo:hi] = mine + self.zbuf[:, lo:hi]
        else:
            self.add(part, m, net.chip, 3)

    def add(self, part, m, chip, slot, rows=slice(0, 96)):
        net = self.net
        lanes = self.lanes(part)
        self.g[m, chip, net.core, rows, lanes] = self.g[m, chip, net.core, rows, lanes] + self.g[m, slot, 1 - net.core, rows, lanes]

    def start_across(self, part, i):
        m = self.net.group(i)
        pl.semaphore_wait(self.ok.at[0, part, m], 1)
        pl.semaphore_wait(self.ok.at[1, part, m], 1)
        for copy in self.across_copies(part, m):
            copy.start()

    def start_sides(self, part, i):
        net = self.net
        m = net.group(i)
        by_y, by_x = self.across_copies(part, m)
        by_y.wait_recv()
        self.add(part, m, net.chip_x, 0, slice(0, 48))
        by_x.wait_recv()
        self.add(part, m, net.chip_y, 0, slice(48, 96))
        for copy in self.side_copies(part, m):
            copy.start()

    def gather_sides(self, part, i):
        net = self.net
        m = net.group(i)
        for slot, copy in zip((1, 2), self.side_copies(part, m)):
            copy.wait_recv()
            self.add(part, m, net.chip, slot)

    def start_z(self, part, m):
        net = self.net
        z = net.z

        @pl.when(jnp.logical_or(jnp.logical_and(m > z, z > 0), jnp.logical_and(m < z, z < 3)))
        def _():
            self.z_arrived(part, m, False)

        @pl.when(m != z)
        def _():
            pl.semaphore_wait(self.ok.at[2, part, m], 1)

        self.each_z(part, m, lambda copy: copy.start())

    def total(self, part):
        net = self.net

        @pl.when(net.z > 0)
        def _():
            self.z_arrived(part, net.z, False)

        @pl.when(net.z < 3)
        def _():
            self.z_arrived(part, net.z, True)

        return self.g[net.z, net.chip, net.core, :, self.lanes(part)].astype(F32)

    def drain(self):
        net = self.net
        for part in range(2):

            def body(m, c, part=part):
                for copy in self.across_copies(part, m) + self.side_copies(part, m):
                    copy.wait_send()
                self.each_z(part, m, lambda copy: copy.wait_send())
                return c

            lax.fori_loop(0, 4, body, 0)


def greet(net):
    barrier = pltpu.get_barrier_semaphore()
    for other in range(1, 8):
        pl.semaphore_signal(barrier, inc=1, device_id=(lax.rem(net.dp + other, 8), net.z), device_id_type=MESH)
    for k in range(1, 4):
        pl.semaphore_signal(barrier, inc=1, device_id=net.up(k), device_id_type=MESH)
    return barrier


def share_gains(net, parts, send, recv):
    copies = []
    for k in range(1, 8):
        copies.append(pltpu.make_async_remote_copy(
            src_ref=parts.at[net.dp], dst_ref=parts.at[net.dp], send_sem=send.at[k - 1], recv_sem=recv.at[net.dp],
            device_id=(lax.rem(net.dp + k, 8), net.z), device_id_type=MESH))
        copies[-1].start()
    return copies


def join_gains(net, parts, send, recv, gain):
    for k in range(1, 8):
        other = lax.rem(net.dp + k, 8)
        pltpu.make_async_remote_copy(
            src_ref=parts.at[other], dst_ref=parts.at[other], send_sem=send.at[k - 1], recv_sem=recv.at[other],
            device_id=net.sibling, device_id_type=MESH).wait_recv()
    total = jnp.zeros(gain.shape, F32)
    for d in range(8):
        piece = jnp.concatenate([parts[d], jnp.zeros((8, gain.shape[1] - 128), F32)], axis=1)
        total = total + pltpu.roll(piece, 96 * d, 1)
    gain[...] = total


def build_package(w, net, q_ref, k_ref, v_ref, o_ref, g_ref, u_ref, d_ref):
    lanes = low_lanes()
    ot = o_ref[...].T
    pad = jnp.zeros((96, 64), F32)
    at = (net.z, net.chip, net.core)

    def put(tile, value):
        w[at[0], at[1], at[2], :, 128 * tile : 128 * (tile + 1)] = value.astype(BF16)

    for j, ref in enumerate((q_ref, k_ref, v_ref)):
        put(2 * j, ref[:, 0:128])
        last = jnp.concatenate([ref[:, 128:192], pad], axis=1)
        extra = jnp.concatenate([ot[:, 64 * j : 64 * (j + 1)], pad], axis=1)
        put(2 * j + 1, jnp.where(lanes, last, pltpu.roll(extra, 64, 1)))
    w[at[0], at[1], at[2], :, 768:1280] = g_ref[...].astype(BF16)
    w[at[0], at[1], at[2], :, 1280:1792] = u_ref[...].astype(BF16)
    w[at[0], at[1], at[2], :, 1792:2304] = d_ref[...].astype(BF16)


def rows768(ref, m, lo, hi):
    return ref[m, :, :, :, lo:hi].reshape(768, hi - lo)


def put768(ref, m, lo, hi, value):
    ref[m, :, :, :, lo:hi] = value.reshape(4, 2, 96, hi - lo)


class RowGather:
    def __init__(self, net, pool, send, recv, ok):
        self.net, self.pool, self.send, self.recv, self.ok = net, pool, send, recv, ok

    def copy(self, m, way):
        net = self.net
        return pltpu.make_async_remote_copy(
            src_ref=self.pool.at[m], dst_ref=self.pool.at[m], send_sem=self.send.at[way, m], recv_sem=self.recv.at[m],
            device_id=net.along(1 - 2 * way), device_id_type=MESH)

    def each(self, m, act):
        net = self.net

        @pl.when(jnp.logical_and(m <= net.z, net.z < 3))
        def _():
            act(self.copy(m, 0))

        @pl.when(jnp.logical_and(m >= net.z, net.z > 0))
        def _():
            act(self.copy(m, 1))

    def start(self):
        net = self.net
        if self.ok is not None:
            for test, way in ((net.z < 3, 0), (net.z > 0, 1)):

                @pl.when(test)
                def _(way=way):
                    pl.semaphore_signal(self.ok.at[1 - way], inc=1, device_id=net.along(1 - 2 * way), device_id_type=MESH)

        for test, way in ((net.z < 3, 0), (net.z > 0, 1)):

            @pl.when(test)
            def _(way=way):
                if self.ok is not None:
                    pl.semaphore_wait(self.ok.at[way], 1)
                self.copy(net.z, way).start()

    def relay(self, i):
        z = self.net.z
        m = self.net.group(i)

        @pl.when(jnp.logical_and(z > 0, z < 3))
        def _():
            self.copy(m, 0).wait_recv()
            self.each(m, lambda copy: copy.start())

    def arrived(self, i):
        z = self.net.z
        m = self.net.group(i)

        @pl.when(jnp.logical_or(z == 0, z == 3))
        def _():
            self.copy(m, 0).wait_recv()

        return m

    def drain(self):
        def body(m, c):
            self.each(m, lambda copy: copy.wait_send())
            return c

        lax.fori_loop(0, 4, body, 0)


def mega_kernel(
    len_ref, x_ref, dy_ref, q_ref, k_ref, v_ref, o_ref, gate_ref, up_ref, down_ref, ga_ref, gf_ref,
    out_ref, gt_ref, gq_ref, gk_ref, gv_ref, go_ref, gate_grad_ref, up_grad_ref, down_grad_ref, gga_ref, ggf_ref,
    w, g, slots, pool, gain, gain_parts, gg_out, gg_in, gg_z, bias, n1t, n2t, dypt, n_b, qkv, hx, o_own, do, wo, lse, lse_t,
    h, acc, res, zbuf,
    ag_send, ag_recv, gn_send, gn_recv, in_sem, rs_sems, ok, gt_send, gt_recv, gt_ok, hx_send, hx_recv, out_sem, gs_send,
    gs_recv, gz_send, gz_recv,
):
    net = Net()
    bins = 4
    seq = 1536
    me = net.z
    xp, dyp, n1, n2 = (pool.at[j] for j in range(4))
    barrier = greet(net)
    halves = []
    for t, ref in enumerate((x_ref, dy_ref)):
        for j in range(2):
            halves.append(pltpu.make_async_copy(
                ref.at[j], g.at[t, :, :, :, 768 * j : 768 * (j + 1)], in_sem.at[2 * t + j]))
    for copy in halves:
        copy.start()
    ag = Gather(net, w, ag_send, ag_recv)
    rs = Reduce(net, g, slots, zbuf, rs_sems, ok)
    rows = RowGather(net, pool, gt_send, gt_recv, gt_ok)
    mids = RowGather(net, hx, hx_send, hx_recv, None)
    build_package(w, net, q_ref, k_ref, v_ref, o_ref, gate_ref, up_ref, down_ref)
    pad = jnp.zeros((1, 32), F32)
    mine = jnp.concatenate([
        jnp.concatenate([ga_ref[...], pad], axis=1), jnp.concatenate([gf_ref[...], pad], axis=1),
        jnp.zeros((6, 128), F32)], axis=0)
    gain_parts[net.dp] = mine.astype(BF16).astype(F32)
    pl.semaphore_wait(barrier, 10)
    gain_copies = share_gains(net, gain_parts, gn_send, gn_recv)
    ag.spread(0, 0)

    place = placement(len_ref, bins)
    lse[...] = jnp.zeros_like(lse)

    def set_bias(b):
        _, segment = packed_source(place, b * CAP, (CAP, 1), 0)
        _, segment_row = packed_source(place, b * CAP, (1, CAP), 1)
        bias[...] = jnp.where(segment == segment_row, 0.0, NEG)

    def pack(b, t, store):
        def body(j, c):
            source, _ = packed_source(place, b * CAP + j * 128, (128, 1), 0)
            pick = (source == lax.broadcasted_iota(jnp.int32, (128, seq), 1)).astype(BF16)
            value = nn(pick[:, 0:768], rows768(g, t, 0, 768)) + nn(pick[:, 768:1536], rows768(g, t, 768, 1536))
            store(pl.ds(pl.multiple_of(j * 128, 128), 128), value)
            return c

        lax.fori_loop(0, CAP // 128, body, 0)

    def drops(b, first, rows, count=1):
        source, _ = packed_source(place, b * CAP, (1, count * CAP), 1)
        return (lax.broadcasted_iota(jnp.int32, (rows, count * CAP), 0) + first == source).astype(BF16)

    def norm(src, dst, gain_row):
        def body(j, c):
            at = pl.ds(pl.multiple_of(j * 128, 128), 128)
            values = src[at, :]
            dst[at, :] = (values * rms_rows(values) * gain_row).astype(BF16)
            return c

        lax.fori_loop(0, CAP // 128, body, 0)

    for copy in halves:
        copy.wait()
    def store_x(at, value):
        xp[at, :] = value.astype(BF16)
        h[at, :] = value

    def store_dy(at, value):
        dyp[at, :] = value.astype(BF16)

    pack(me, 0, store_x)
    ag.spread(0, 1)
    ag.relay(0, 0)
    pack(me, 1, store_dy)
    join_gains(net, gain_parts, gn_send, gn_recv, gain)
    g1 = gain[0:1, :]
    g2 = gain[1:2, :]
    ag.spread(0, 2)
    ag.relay(0, 1)
    ag.across(0, 0)
    norm(h, n1, g1)
    n1t[...] = n1[...].T
    dypt[...] = dyp[...].T

    set_bias(me)
    ag.spread(0, 3)
    ag.relay(0, 2)
    ag.across(0, 1)
    ag.relay(0, 3)
    ag.across(0, 2)
    ag.spread(1, 0)
    ag.across(0, 3)

    def own_forward(i, c):
        m = net.group(i)
        ag.complete(0, i)
        first, second = out_weight_tiles_at(w, m)
        wo[m, :, 0:128] = first
        wo[m, :, 128:256] = second
        qkv[m] = nn(n1[...], rows768(w, m, 0, 768)).astype(BF16)
        attend_group(qkv, m, bias, o_own, m, lse)
        h[...] += nt(o_own[m], wo[m])

        @pl.when(i == 1)
        def _():
            ag.spread(1, 1)
            ag.relay(1, 0)

        return c

    lax.fori_loop(0, 4, own_forward, 0)
    hx[me] = h[...].astype(BF16)
    mids.start()
    norm(h, n2, g2)
    n2t[...] = n2[...].T
    lse_t[...] = lse[...].T
    acc[...] = jnp.zeros_like(acc)
    res[...] = h[...]

    def ffn_back(i, c):
        @pl.when(i == 0)
        def _():
            ag.spread(1, 2)
            ag.relay(1, 1)
            ag.across(1, 0)

        @pl.when(i == 1)
        def _():
            ag.spread(1, 3)
            ag.relay(1, 2)
            ag.across(1, 1)

        @pl.when(i == 2)
        def _():
            ag.relay(1, 3)
            ag.across(1, 2)

            mids.relay(1)

        @pl.when(i == 3)
        def _():
            ag.across(1, 3)
            mids.relay(2)

        m = net.group(i)
        ag.complete(1, i)
        for lo in (0, 256):
            w_gate = rows768(w, m, 768 + lo, 1024 + lo)
            w_up = rows768(w, m, 1280 + lo, 1536 + lo)
            w_down = rows768(w, m, 1792 + lo, 2048 + lo)
            a = nn(n2[...], w_gate)
            up = nn(n2[...], w_up)
            t = gelu_parts(a)
            gel = 0.5 * a * (1.0 + t)
            u = (gel * up).astype(BF16)
            res[...] += nt(u, w_down)
            put768(g, m, 1792 + lo, 2048 + lo, nn(dypt[...], u).astype(BF16))
            du = nn(dyp[...], w_down)
            slope = 0.5 * (1.0 + t) + 0.5 * a * (1.0 - t * t) * (GELU_COEF * (1.0 + 3.0 * GELU_CUBE * a * a))
            da = (du * up * slope).astype(BF16)
            db = (du * gel).astype(BF16)
            put768(g, m, 768 + lo, 1024 + lo, nn(n2t[...], da).astype(BF16))
            put768(g, m, 1280 + lo, 1536 + lo, nn(n2t[...], db).astype(BF16))
            acc[...] += nt(da, w_gate) + nt(db, w_up)

        @pl.when(i < 2)
        def _():
            rs.to_core(1, i, False)

        @pl.when(i >= 2)
        def _():
            rs.to_core(1, i, True)

        @pl.when(jnp.logical_and(i >= 1, i < 3))
        def _():
            rs.from_core(1, i - 1, (1, i + 1))

        @pl.when(i == 3)
        def _():
            rs.from_core(1, 2, (0, 0))

        return c

    lax.fori_loop(0, 4, ffn_back, 0)
    rs.start_across(1, 0)
    rs.start_across(1, 1)
    rs.start_across(1, 2)

    def hidden_back(j, total):
        at = pl.ds(pl.multiple_of(j * 128, 128), 128)
        ho = h[at, :]
        r2 = rms_rows(ho)
        dn2 = acc[at, :]
        wg = dn2 * g2
        dh = dyp[at, :].astype(F32) + r2 * wg - ho * (r2 * r2 * r2) * jnp.mean(wg * ho, axis=1, keepdims=True)
        h[at, :] = dh
        n2[at, :] = dh.astype(BF16)
        acc[at, :] = jnp.zeros_like(dh)
        return total + jnp.sum(dn2 * ho * r2, axis=0, keepdims=True)

    gg_ffn = lax.fori_loop(0, CAP // 128, hidden_back, jnp.zeros((1, 768), F32))
    n2t[...] = n2[...].T
    rs.from_core(1, 3, (0, 1))
    rs.start_across(1, 3)
    mids.relay(3)

    def attn_back(i, c):
        m = net.group(i)
        do[0] = nn(n2[...], wo[m]).astype(BF16)
        attend_group_back(qkv, m, bias, lse_t, do, 0, qkv)
        acc[...] += nt(qkv[m], rows768(w, m, 0, 768))
        rs.start_sides(1, i)
        return c

    lax.fori_loop(0, 4, attn_back, 0)

    def input_back(j, total):
        at = pl.ds(pl.multiple_of(j * 128, 128), 128)
        xb = xp[at, :].astype(F32)
        r1 = rms_rows(xb)
        dn1 = acc[at, :]
        wa = dn1 * g1
        gt = h[at, :] + r1 * wa - xb * (r1 * r1 * r1) * jnp.mean(wa * xb, axis=1, keepdims=True)
        n_b[at, :] = gt.astype(BF16)
        return total + jnp.sum(dn1 * xb * r1, axis=0, keepdims=True)

    gg_attn = lax.fori_loop(0, CAP // 128, input_back, jnp.zeros((1, 768), F32))
    pool[me] = n_b[...]
    rows.start()
    gg = jnp.concatenate([gg_attn, gg_ffn, jnp.zeros((6, 768), F32)], axis=0)
    for d in range(8):
        gg_out[d] = pltpu.roll(gg, (768 - 96 * d) % 768, 1)[:, 0:128] if d else gg[:, 0:128]

    def gg_copy(k):
        to = lax.rem(net.dp + k, 8)
        return pltpu.make_async_remote_copy(
            src_ref=gg_out.at[to], dst_ref=gg_in.at[net.dp], send_sem=gs_send.at[k - 1], recv_sem=gs_recv.at[net.dp],
            device_id=(to, net.z), device_id_type=MESH)

    for k in range(1, 8):
        gg_copy(k).start()

    def attn_grads(i, c):
        m = net.group(i)
        go = nn(n2t[...], o_own[m])
        lanes = low_lanes()
        for j in range(3):
            grad = nn(n1t[...], qkv[m, :, 256 * j : 256 * (j + 1)])
            put768(g, m, 256 * j, 256 * j + 128, grad[:, 0:128].astype(BF16))
            if j == 1:
                extra = go[:, 0:128]
            else:
                extra = pltpu.roll(go[:, 64 * j : 64 * j + 128], 64, 1)
            put768(g, m, 256 * j + 128, 256 * (j + 1), jnp.where(lanes, grad[:, 128:256], extra).astype(BF16))

        rs.to_core(0, i, True)

        @pl.when(jnp.logical_and(i >= 1, i < 3))
        def _():
            rs.from_core(0, i - 1, (0, i + 1))

        @pl.when(i == 3)
        def _():
            rs.from_core(0, 2, None)

        return c

    lax.fori_loop(0, 4, attn_grads, 0)
    rs.from_core(0, 3, None)
    for i in range(4):
        rs.start_across(0, i)

    part = gg_out[net.dp]
    for k in range(1, 8):
        other = lax.rem(net.dp + k, 8)
        pltpu.make_async_remote_copy(
            src_ref=gg_out.at[other], dst_ref=gg_in.at[other], send_sem=gs_send.at[k - 1], recv_sem=gs_recv.at[other],
            device_id=net.sibling, device_id_type=MESH).wait_recv()
        part = part + gg_in[other]
    gg_z[me] = part
    gz_copies = [pltpu.make_async_remote_copy(
        src_ref=gg_z.at[me], dst_ref=gg_z.at[me], send_sem=gz_send.at[k - 1], recv_sem=gz_recv.at[me],
        device_id=net.up(k), device_id_type=MESH) for k in range(1, 4)]
    for copy in gz_copies:
        copy.start()

    rs.gather_sides(1, 0)
    rs.gather_sides(1, 1)
    mids.drain()
    hx[me] = res[...].astype(BF16)

    def ffn_out(j, c):
        b = mids.arrived(j)
        acc[...] = hx[b].astype(F32)
        norm(acc, n_b, g2)

        def ffn(m, c):
            a = nn(n_b[...], rows768(w, m, 768, 1280))
            up = nn(n_b[...], rows768(w, m, 1280, 1792))
            u = (0.5 * a * (1.0 + gelu_parts(a)) * up).astype(BF16)
            acc[...] += nt(u, rows768(w, m, 1792, 2304))
            return c

        lax.fori_loop(0, 4, ffn, 0)
        hx[b] = acc[...].astype(BF16)

        @pl.when(j == 1)
        def _():
            rows.relay(1)
            rows.relay(2)
            rs.start_sides(0, 0)
            rs.start_sides(0, 1)
            rs.gather_sides(1, 2)
            rs.gather_sides(1, 3)
            rs.start_z(1, 0)
            rs.start_z(1, 1)

        @pl.when(j == 2)
        def _():
            rs.start_sides(0, 2)
            rs.start_sides(0, 3)
            rs.start_z(1, 2)
            rs.start_z(1, 3)
            rows.relay(3)

        return c

    lax.fori_loop(1, 4, ffn_out, 0)

    def place_out(j, c):
        at = pl.ds(pl.multiple_of(j * 256, 256), 256)
        pick = drops(0, j * 256, 256, 4)
        value = nn(pick[:, 0:CAP], hx[0])
        for b in range(1, 4):
            value = value + nn(pick[:, b * CAP : (b + 1) * CAP], hx[b])
        out_ref[at, :] = value.astype(BF16)
        return c

    lax.fori_loop(0, seq // 256, place_out, 0)
    for i in range(4):
        rs.gather_sides(0, i)
    for m in range(4):
        rs.start_z(0, m)

    def place_rows(bs, first):
        def body(j, c):
            value = nn(drops(bs[0], CAP * j, CAP), pool[bs[0]])
            for b in bs[1:]:
                value = value + nn(drops(b, CAP * j, CAP), pool[b])
            if not first:
                value = value + qkv[j].astype(F32)
            qkv[j] = value.astype(BF16)
            return c

        lax.fori_loop(0, 3, body, 0)

    place_rows([me, rows.arrived(1), rows.arrived(2)], True)
    place_rows([rows.arrived(3)], False)
    out = pltpu.make_async_copy(qkv.at[0:3], gt_ref, out_sem)
    out.start()

    for k in range(1, 4):
        other = lax.rem(me + k, 4)
        pltpu.make_async_remote_copy(
            src_ref=gg_z.at[other], dst_ref=gg_z.at[other], send_sem=gz_send.at[k - 1], recv_sem=gz_recv.at[other],
            device_id=net.up(k), device_id_type=MESH).wait_recv()
        part = part + gg_z[other]
    gga_ref[...] = part[0:1, 0:96]
    ggf_ref[...] = part[1:2, 0:96]
    ffn_sum = rs.total(1)
    gate_grad_ref[...] = ffn_sum[:, 0:512]
    up_grad_ref[...] = ffn_sum[:, 512:1024]
    down_grad_ref[...] = ffn_sum[:, 1024:1536]
    attn_sum = rs.total(0)
    gq_ref[...] = attn_sum[:, 0:192]
    gk_ref[...] = attn_sum[:, 256:448]
    gv_ref[...] = attn_sum[:, 512:704]
    go_ref[...] = jnp.concatenate([attn_sum[:, 192:256], attn_sum[:, 448:512], attn_sum[:, 704:768]], axis=1).T
    out.wait()
    for copy in gain_copies + gz_copies:
        copy.wait_send()
    for k in range(1, 8):
        gg_copy(k).wait_send()
    rows.drain()
    rs.drain()
    ag.drain()


def finish_kernel(*refs):
    count = len(refs) // 2
    refs[count][...] = refs[0][...].astype(F32)
    refs[count + 1][...] = refs[1][...]

    @pl.when(pl.program_id(0) == 0)
    def _():
        for j in range(2, count):
            refs[count + j][...] = refs[j][...]


def out_weight_tiles_at(w, m):
    lanes = low_lanes()
    t1 = rows768(w, m, 128, 256).astype(F32)
    t3 = rows768(w, m, 384, 512).astype(F32)
    t5 = rows768(w, m, 640, 768).astype(F32)
    first = jnp.where(lanes, pltpu.roll(t1, 64, 1), t3)
    second = jnp.where(lanes, pltpu.roll(t5, 64, 1), 0.0)
    return first.astype(BF16), second.astype(BF16)


def on_this_slice(
    tokens, lengths, query_weight, key_weight, value_weight, out_weight, attn_gain, gate_weight, up_weight, down_weight,
    ffn_gain, cotangent,
):
    rows, seq, width = tokens.shape
    vmem = pl.BlockSpec(memory_space=pltpu.VMEM)
    smem = pl.BlockSpec(memory_space=pltpu.SMEM)
    dma = pltpu.SemaphoreType.DMA
    act = pltpu.VMEM((CAP, width), BF16)
    act_t = pltpu.VMEM((width, CAP), BF16)
    wide = pltpu.VMEM((CAP, width), F32)
    hbm = pl.BlockSpec(memory_space=pl.ANY)

    def f32(*shape):
        return jax.ShapeDtypeStruct(shape, F32)

    out, gt, gq, gk, gv, go, gate, up, down, gain_a, gain_f = pl.pallas_call(
        mega_kernel,
        out_shape=(
            jax.ShapeDtypeStruct((seq, width), BF16), jax.ShapeDtypeStruct((3, CAP, width), BF16),
            f32(96, 192), f32(96, 192), f32(96, 192), f32(192, 96), f32(96, 512), f32(96, 512), f32(96, 512), f32(1, 96), f32(1, 96),
        ),
        in_specs=[smem, hbm, hbm] + [vmem] * 9,
        out_specs=[vmem, hbm] + [vmem] * 9,
        scratch_shapes=[
            pltpu.VMEM((4, 4, 2, 96, 2304), BF16),
            pltpu.VMEM((4, 4, 2, 96, 2304), BF16),
            pltpu.VMEM((2, 4, 96, 1536), BF16),
            pltpu.VMEM((4, CAP, width), BF16),
            pltpu.VMEM((8, width), F32),
            pltpu.VMEM((8, 8, 128), F32), pltpu.VMEM((8, 8, 128), F32), pltpu.VMEM((8, 8, 128), F32),
            pltpu.VMEM((4, 8, 128), F32),
            pltpu.VMEM((CAP, CAP), F32),
            act_t, act_t, act_t, act,
            pltpu.VMEM((4, CAP, width), BF16),
            pltpu.VMEM((4, CAP, width), BF16),
            pltpu.VMEM((4, CAP, 256), BF16),
            pltpu.VMEM((1, CAP, 256), BF16),
            pltpu.VMEM((4, width, 256), BF16),
            pltpu.VMEM((CAP, 128), F32),
            pltpu.VMEM((128, CAP), F32),
            wide, wide, wide,
            pltpu.VMEM((96, 2304), BF16),
            dma((2, 4, 4, 5)), dma((2, 4, 4, 2, 3)), dma((7,)), dma((8,)), dma((4,)),
            dma((2, 7, 2, 4)), pltpu.SemaphoreType.REGULAR((4, 2, 4)),
            dma((2, 4)), dma((4,)), pltpu.SemaphoreType.REGULAR((2,)), dma((2, 4)), dma((4,)), dma, dma((7,)), dma((8,)), dma((3,)), dma((4,)),
        ],
        compiler_params=pltpu.CompilerParams(
            vmem_limit_bytes=60 * 2**20, collective_id=0, has_side_effects=True),
        name="layer",
    )(lengths, tokens.reshape(2, 4, 2, 96, width), cotangent.reshape(2, 4, 2, 96, width), query_weight, key_weight,
      value_weight, out_weight, gate_weight, up_weight, down_weight.T, attn_gain.reshape(1, 96), ffn_gain.reshape(1, 96))
    rest = (out, gq, gk, gv, go, gate, up, down, gain_a, gain_f)
    block = pl.BlockSpec((256, width), lambda i: (i, 0))
    whole = [pl.BlockSpec(a.shape, lambda i: (0, 0)) for a in rest[1:]]
    gt, out, gq, gk, gv, go, gate, up, down, gain_a, gain_f = pl.pallas_call(
        finish_kernel,
        grid=(seq // 256,),
        out_shape=(f32(seq, width),) + tuple(jax.ShapeDtypeStruct(a.shape, a.dtype) for a in rest),
        in_specs=[block, block] + whole,
        out_specs=(block, block) + tuple(whole),
        name="finish",
    )(gt.reshape(seq, width), *rest)
    return (
        out.reshape(rows, seq, width), gt.reshape(rows, seq, width), gq, gk, gv, go, gain_a.reshape(96), gate, up, down.T,
        gain_f.reshape(96),
    )
def solution(mesh):
    body = on_this_slice if dict(mesh.shape) == {"dp": 8, "mp": 4} else per_device
    return jax.shard_map(
        body,
        mesh=mesh,
        in_specs=(
            P("dp", None, None), P("dp", None), P("dp", "mp"), P("dp", "mp"), P("dp", "mp"), P("mp", "dp"), P("dp"),
            P("dp", "mp"), P("dp", "mp"), P("mp", "dp"), P("dp"), P("dp", None, None),
        ),
        out_specs=(
            P("dp", None, None), P("dp", None, None), P("dp", "mp"), P("dp", "mp"), P("dp", "mp"), P("mp", "dp"),
            P("dp"), P("dp", "mp"), P("dp", "mp"), P("mp", "dp"), P("dp"),
        ),
        check_vma=False,
    )
```

```python
import functools
import jax
import jax.numpy as jnp
from jax import lax
from jax.experimental import pallas as pl
from jax.experimental.pallas import tpu as pltpu
from jax.sharding import PartitionSpec as P

EPSILON = 1e-06
GELU_COEF = 0.7978845608028654
GELU_CUBE = 0.044715
CAP = 512
NEG = -1e30
F32 = jnp.float32
BF16 = jnp.bfloat16


def nn(a, b):
    return lax.dot_general(a, b, (((1,), (0,)), ((), ())), preferred_element_type=F32)


def nt(a, b):
    return lax.dot_general(a, b, (((1,), (1,)), ((), ())), preferred_element_type=F32)


def tn(a, b):
    return lax.dot_general(a, b, (((0,), (0,)), ((), ())), preferred_element_type=F32)


def placement(len_ref, bins):
    count = len_ref.shape[1]
    sizes = [len_ref[0, i] for i in range(count)]
    starts = [jnp.int32(0)]
    for i in range(count - 1):
        starts.append(starts[-1] + sizes[i])
    ranks = []
    for i in range(count):
        rank = jnp.int32(0)
        for j in range(count):
            if j < i:
                rank = rank + jnp.where(sizes[j] >= sizes[i], 1, 0)
            elif j > i:
                rank = rank + jnp.where(sizes[j] > sizes[i], 1, 0)
        ranks.append(rank)
    fills = [jnp.int32(0)] * (bins - 1)
    spots = [jnp.int32(0)] * count
    for k in range(count):
        size = jnp.int32(0)
        for i in range(count):
            size = size + jnp.where(ranks[i] == k, sizes[i], 0)
        if k == 0:
            spot = jnp.int32((bins - 1) * CAP)
        else:
            free = jnp.int32(1)
            spot = jnp.int32(0)
            for b in range(bins - 1):
                fits = jnp.where(fills[b] + size <= CAP, free, 0) if b < bins - 2 else free
                spot = spot + fits * (b * CAP + fills[b])
                fills[b] = fills[b] + fits * size
                free = free - fits
        for i in range(count):
            spots[i] = spots[i] + jnp.where(ranks[i] == k, spot, 0)
    return starts, sizes, spots


def packed_source(place, first, shape, axis):
    spot = lax.broadcasted_iota(jnp.int32, shape, axis) + first
    source = jnp.full(shape, -1, jnp.int32)
    segment = jnp.full(shape, -1, jnp.int32)
    for i, (start, size, at) in enumerate(zip(*place)):
        here = (spot >= at) & (spot < at + size)
        source = jnp.where(here, spot + (start - at), source)
        segment = jnp.where(here, i, segment)
    return source, segment


def low_lanes():
    return lax.broadcasted_iota(jnp.int32, (1, 128), 1) < 64


def half(tile, low):
    lanes = low_lanes()
    return jnp.where(lanes if low else jnp.logical_not(lanes), tile, jnp.zeros_like(tile))


HEADS = ((0, 2, 4, True), (0, 2, 4, False), (1, 3, 5, True))


def tile_of(ref, m, t, rows=slice(None)):
    return ref[m, rows, 128 * t : 128 * (t + 1)]


def attend_group(qkv, m, bias, o_ref, at, lse_ref=None, qb=256):
    for i in range(CAP // qb):
        rows = slice(i * qb, (i + 1) * qb)
        scores = []
        for tq, tk, tv, low in HEADS:
            q = half(tile_of(qkv, m, tq, rows), low) * jnp.asarray(0.125, BF16)
            scores.append(nt(q, tile_of(qkv, m, tk)))
        shares, totals = [], []
        for head, s in enumerate(scores):
            s = s + bias[rows, :]
            top = jnp.max(s, axis=1, keepdims=True)
            e = jnp.exp(s - top)
            total = jnp.sum(e, axis=1, keepdims=True)
            shares.append(e.astype(BF16))
            totals.append(total)
            if lse_ref is not None:
                lane = lax.broadcasted_iota(jnp.int32, (1, 128), 1)
                lse_ref[rows, :] = jnp.where(lane == 3 * m + head, top + jnp.log(total), lse_ref[rows, :])
        parts = []
        for (tq, tk, tv, low), e, total in zip(HEADS, shares, totals):
            parts.append(nn(e, half(tile_of(qkv, m, tv), low)) * (1.0 / total))
        o_ref[at, rows, 0:128] = (parts[0] + parts[1]).astype(BF16)
        o_ref[at, rows, 128:256] = parts[2].astype(BF16)


def attend_group_back(qkv, m, bias, lse_t, do_ref, at, dqkv):
    dk = [None, None]
    dv = [None, None]
    dq = [None, None]
    scale = jnp.asarray(0.125, BF16)
    for head, (tq, tk, tv, low) in enumerate(HEADS):
        j = 0 if head < 2 else 1
        k = half(tile_of(qkv, m, tk), low) * scale
        s = nt(k, tile_of(qkv, m, tq))
        do = do_ref[at, :, 128 * j : 128 * (j + 1)]
        dp = nt(half(tile_of(qkv, m, tv), low), do)
        p = jnp.exp(s + bias[...] - lse_t[pl.ds(3 * m + head, 1), :])
        delta = jnp.sum(p * dp, axis=0, keepdims=True)
        ds = (p * (dp - delta)).astype(BF16)
        parts = (
            nn(p.astype(BF16), half(do, low)), nn(ds, half(tile_of(qkv, m, tq), low) * scale), tn(ds, k))
        for total, part in zip((dv, dk, dq), parts):
            total[j] = part if total[j] is None else total[j] + part
    for j in range(2):
        for t, total in ((0, dq), (2, dk), (4, dv)):
            dqkv[m, :, 128 * (t + j) : 128 * (t + j + 1)] = total[j].astype(BF16)


def out_weight_tiles(w, m):
    lanes = low_lanes()
    t1 = tile_of(w, m, 1).astype(F32)
    t3 = tile_of(w, m, 3).astype(F32)
    t5 = tile_of(w, m, 5).astype(F32)
    first = jnp.where(lanes, pltpu.roll(t1, 64, 1), t3)
    second = jnp.where(lanes, pltpu.roll(t5, 64, 1), 0.0)
    return first.astype(BF16), second.astype(BF16)


def gelu_parts(a):
    inner = GELU_COEF * (a + GELU_CUBE * a * a * a)
    t = jnp.tanh(inner)
    return t


def rms_rows(values):
    return lax.rsqrt(jnp.mean(values * values, axis=1, keepdims=True) + EPSILON)


def layer_kernel(
    len_ref, x_ref, dy_ref, w_ref, gain_ref, which_ref,
    out_ref, gt_ref, g_ref, gg_ref,
    bias, xp, dyp, n1, n1t, n2, n2t, dypt, dhbt, qkv, o_all, wo, lse, lse_t, do, dqkv, h, acc,
):
    bins = w_ref.shape[0]
    seq = x_ref.shape[0]
    place = placement(len_ref, bins)
    me = which_ref[0]
    g1 = gain_ref[0:1, :]
    g2 = gain_ref[1:2, :]

    def wo_body(m, c):
        first, second = out_weight_tiles(w_ref, m)
        wo[m, :, 0:128] = first
        wo[m, :, 128:256] = second
        return c

    lax.fori_loop(0, bins, wo_body, 0)
    lse[...] = jnp.zeros_like(lse)

    def forward(b):
        source, segment = packed_source(place, b * CAP, (CAP, 1), 0)
        _, segment_row = packed_source(place, b * CAP, (1, CAP), 1)
        bias[...] = jnp.where(segment == segment_row, 0.0, NEG)
        pick = (source == lax.broadcasted_iota(jnp.int32, (CAP, seq), 1)).astype(BF16)
        xb = nn(pick, x_ref[...])
        xp[...] = xb.astype(BF16)
        dyp[...] = nn(pick, dy_ref[...]).astype(BF16)
        n1[...] = (xb * rms_rows(xb) * g1).astype(BF16)
        h[...] = xb

        def m_body(m, c):
            qkv[m] = nn(n1[...], w_ref[m, :, 0:768]).astype(BF16)
            attend_group(qkv, m, bias, o_all, m, lse)
            h[...] += nt(o_all[m], wo[m])
            return c

        lax.fori_loop(0, bins, m_body, 0)
        hb = h[...]
        n2[...] = (hb * rms_rows(hb) * g2).astype(BF16)

    def ffn_out(b):
        acc[...] = h[...]

        def m_body(m, c):
            a = nn(n2[...], w_ref[m, :, 768:1280])
            up = nn(n2[...], w_ref[m, :, 1280:1792])
            u = (0.5 * a * (1.0 + gelu_parts(a)) * up).astype(BF16)
            acc[...] += nt(u, w_ref[m, :, 1792:2304])
            return c

        lax.fori_loop(0, bins, m_body, 0)
        source, _ = packed_source(place, b * CAP, (1, CAP), 1)
        drop = (lax.broadcasted_iota(jnp.int32, (seq, CAP), 0) == source).astype(BF16)
        out_ref[...] = (out_ref[...].astype(F32) + nn(drop, acc[...].astype(BF16))).astype(BF16)

    out_ref[...] = jnp.zeros_like(out_ref)

    def others(i, c):
        b = lax.rem(me + 1 + i, bins)
        forward(b)
        ffn_out(b)
        return c

    lax.fori_loop(0, bins, others, 0)

    n1t[...] = n1[...].T
    n2t[...] = n2[...].T
    dypt[...] = dyp[...].T
    lse_t[...] = lse[...].T
    acc[...] = jnp.zeros_like(acc)

    def ffn_back(m, c):
        a = nn(n2[...], w_ref[m, :, 768:1280])
        up = nn(n2[...], w_ref[m, :, 1280:1792])
        t = gelu_parts(a)
        gel = 0.5 * a * (1.0 + t)
        u = (gel * up).astype(BF16)
        du = nn(dyp[...], w_ref[m, :, 1792:2304])
        slope = 0.5 * (1.0 + t) + 0.5 * a * (1.0 - t * t) * (GELU_COEF * (1.0 + 3.0 * GELU_CUBE * a * a))
        da = (du * up * slope).astype(BF16)
        db = (du * gel).astype(BF16)
        g_ref[m, :, 1792:2304] = nn(dypt[...], u).astype(BF16)
        g_ref[m, :, 768:1280] = nn(n2t[...], da).astype(BF16)
        g_ref[m, :, 1280:1792] = nn(n2t[...], db).astype(BF16)
        acc[...] += nt(da, w_ref[m, :, 768:1280]) + nt(db, w_ref[m, :, 1280:1792])
        return c

    lax.fori_loop(0, bins, ffn_back, 0)
    hb = h[...]
    r2 = rms_rows(hb)
    dn2 = acc[...]
    gg_ffn = jnp.sum(dn2 * hb * r2, axis=0, keepdims=True)
    wg = dn2 * g2
    dh = dyp[...].astype(F32) + r2 * wg - hb * (r2 * r2 * r2) * jnp.mean(wg * hb, axis=1, keepdims=True)
    h[...] = dh
    dhb = dh.astype(BF16)
    dhbt[...] = dhb.T
    n2[...] = dhb
    acc[...] = jnp.zeros_like(acc)

    def attn_back(m, c):
        do[m] = nn(n2[...], wo[m]).astype(BF16)
        attend_group_back(qkv, m, bias, lse_t, do, m, dqkv)
        acc[...] += nt(dqkv[m], w_ref[m, :, 0:768])
        grad = nn(n1t[...], dqkv[m])
        go = nn(dhbt[...], o_all[m])
        lanes = low_lanes()
        for t in range(6):
            g = grad[:, 128 * t : 128 * (t + 1)]
            if t == 1:
                g = jnp.where(lanes, g, pltpu.roll(go[:, 0:128], 64, 1))
            elif t == 3:
                g = jnp.where(lanes, g, go[:, 0:128])
            elif t == 5:
                g = jnp.where(lanes, g, pltpu.roll(go[:, 128:256], 64, 1))
            g_ref[m, :, 128 * t : 128 * (t + 1)] = g.astype(BF16)
        return c

    lax.fori_loop(0, bins, attn_back, 0)
    xb = xp[...].astype(F32)
    r1 = rms_rows(xb)
    dn1 = acc[...]
    gg_attn = jnp.sum(dn1 * xb * r1, axis=0, keepdims=True)
    wa = dn1 * g1
    gt = h[...] + r1 * wa - xb * (r1 * r1 * r1) * jnp.mean(wa * xb, axis=1, keepdims=True)
    gt_ref[...] = gt.astype(BF16)
    gg_ref[0:1, :] = gg_attn
    gg_ref[1:2, :] = gg_ffn


def unpack_kernel(len_ref, gt_ref, out_ref):
    bins = gt_ref.shape[0]
    seq = out_ref.shape[0]
    place = placement(len_ref, bins)
    total = jnp.zeros(out_ref.shape, F32)
    for b in range(bins):
        source, _ = packed_source(place, b * CAP, (1, CAP), 1)
        drop = (lax.broadcasted_iota(jnp.int32, (seq, CAP), 0) == source).astype(BF16)
        total = total + nn(drop, gt_ref[b])
    out_ref[...] = total


def per_device(
    tokens, lengths, query_weight, key_weight, value_weight, out_weight, attn_gain, gate_weight, up_weight, down_weight,
    ffn_gain, cotangent,
):
    rows, seq, width = tokens.shape
    bins = lax.axis_size("mp")
    q, k, v, o = (w.astype(BF16) for w in (query_weight, key_weight, value_weight, out_weight.T))
    package = jnp.concatenate(
        [q, o[:, 0:64], k, o[:, 64:128], v, o[:, 128:192], gate_weight.astype(BF16), up_weight.astype(BF16),
         down_weight.T.astype(BF16)], axis=1)
    w = lax.all_gather(lax.all_gather(package, "dp", axis=0, tiled=True), "mp", axis=0)
    gains = jnp.stack([attn_gain, ffn_gain]).astype(BF16)
    gains = lax.all_gather(gains, "dp", axis=1, tiled=True).astype(F32)
    gains = jnp.concatenate([gains, jnp.zeros((6, width), F32)], axis=0)
    which = lax.axis_index("mp").astype(jnp.int32).reshape(1)
    vmem = pl.BlockSpec(memory_space=pltpu.VMEM)
    smem = pl.BlockSpec(memory_space=pltpu.SMEM)
    group = w.shape[2]
    x = tokens.reshape(seq, width)
    dy = cotangent.reshape(seq, width)
    out, gt, g, gg = pl.pallas_call(
        layer_kernel,
        out_shape=(
            jax.ShapeDtypeStruct((seq, width), BF16),
            jax.ShapeDtypeStruct((CAP, width), BF16),
            jax.ShapeDtypeStruct((bins, width, group), BF16),
            jax.ShapeDtypeStruct((8, width), F32),
        ),
        in_specs=[smem, vmem, vmem, vmem, vmem, smem],
        out_specs=[vmem] * 4,
        scratch_shapes=[
            pltpu.VMEM((CAP, CAP), F32),
            pltpu.VMEM((CAP, width), BF16),
            pltpu.VMEM((CAP, width), BF16),
            pltpu.VMEM((CAP, width), BF16),
            pltpu.VMEM((width, CAP), BF16),
            pltpu.VMEM((CAP, width), BF16),
            pltpu.VMEM((width, CAP), BF16),
            pltpu.VMEM((width, CAP), BF16),
            pltpu.VMEM((width, CAP), BF16),
            pltpu.VMEM((bins, CAP, width), BF16),
            pltpu.VMEM((bins, CAP, 256), BF16),
            pltpu.VMEM((bins, width, 256), BF16),
            pltpu.VMEM((CAP, 128), F32),
            pltpu.VMEM((128, CAP), F32),
            pltpu.VMEM((bins, CAP, 256), BF16),
            pltpu.VMEM((bins, CAP, width), BF16),
            pltpu.VMEM((CAP, width), F32),
            pltpu.VMEM((CAP, width), F32),
        ],
        compiler_params=pltpu.CompilerParams(vmem_limit_bytes=63 * 2**20+900000),
        name="layer",
    )(lengths, x, dy, w, gains, which)
    gt_all = lax.all_gather(gt, "mp", axis=0)
    grad_tokens = pl.pallas_call(
        unpack_kernel,
        out_shape=jax.ShapeDtypeStruct((seq, width), F32),
        in_specs=[smem, vmem],
        out_specs=vmem,
        compiler_params=pltpu.CompilerParams(vmem_limit_bytes=60 * 2**20),
        name="unpack",
    )(lengths, gt_all)
    g = lax.psum_scatter(g, "mp", scatter_dimension=0, tiled=False)
    g = lax.psum_scatter(g, "dp", scatter_dimension=0, tiled=True).astype(F32)
    gg = lax.psum_scatter(lax.psum(gg[0:2], "mp"), "dp", scatter_dimension=1, tiled=True)
    go = jnp.concatenate([g[:, 192:256], g[:, 448:512], g[:, 704:768]], axis=1).T
    return (
        out.reshape(rows, seq, width),
        grad_tokens.reshape(rows, seq, width),
        g[:, 0:192],
        g[:, 256:448],
        g[:, 512:704],
        go,
        gg[0],
        g[:, 768:1280],
        g[:, 1280:1792],
        g[:, 1792:2304].T,
        gg[1],
    )


MESH = pl.DeviceIdType.MESH
PARTS = ((0, 768), (768, 2304))


class Net:
    def __init__(self):
        self.dp = lax.axis_index("dp")
        self.z = lax.axis_index("mp")
        self.core = lax.rem(self.dp, 2)
        self.chip = lax.div(self.dp, 2)
        self.chip_x = self.chip + 1 - 2 * lax.rem(self.chip, 2)
        self.chip_y = lax.rem(self.chip + 2, 4)
        self.chip_d = 3 - self.chip
        self.sibling = (2 * self.chip + 1 - self.core, self.z)
        self.x = (2 * self.chip_x + self.core, self.z)
        self.y = (2 * self.chip_y + self.core, self.z)

    def up(self, k):
        return (self.dp, lax.rem(self.z + k, 4))

    def along(self, step):
        return (self.dp, lax.rem(self.z + 4 + step, 4))

    def group(self, i):
        z = self.z
        one = jnp.where(z == 0, 1, jnp.where(z == 1, 0, jnp.where(z == 2, 3, 2)))
        two = jnp.where(z < 2, 2, 1)
        return jnp.where(i == 0, z, jnp.where(i == 1, one, jnp.where(i == 2, two, 6 - z - one - two)))


class Gather:
    def __init__(self, net, w, send, recv):
        self.net, self.w, self.send, self.recv = net, w, send, recv

    def copy(self, part, m, chip, core, kind, to, rows=None):
        lo, hi = PARTS[part]
        first, last, mark = (0, 96, 0) if rows is None else (48 * rows, 48 * (rows + 1), 1 + rows)
        ref = self.w.at[m, chip, core, first:last, lo:hi]
        return pltpu.make_async_remote_copy(
            src_ref=ref, dst_ref=ref, send_sem=self.send.at[part, m, chip, kind],
            recv_sem=self.recv.at[part, m, chip, core, mark], device_id=to, device_id_type=MESH)

    def wait(self, part, m, chip, core, rows=None):
        self.copy(part, m, chip, core, 0, self.net.sibling, rows).wait_recv()

    def each_along_z(self, part, m, act):
        net = self.net

        @pl.when(jnp.logical_and(m <= net.z, net.z < 3))
        def _():
            act(self.copy(part, m, net.chip, net.core, 3, net.along(1)))

        @pl.when(jnp.logical_and(m >= net.z, net.z > 0))
        def _():
            act(self.copy(part, m, net.chip, net.core, 4, net.along(-1)))

    def own_copies(self, part, m):
        net = self.net
        return [self.copy(part, m, net.chip, net.core, k, to) for k, to in enumerate((net.x, net.y, net.sibling))]

    def relay_copies(self, part, m):
        net = self.net
        return [
            self.copy(part, m, net.chip_x, net.core, 0, net.y, 0), self.copy(part, m, net.chip_x, net.core, 2, net.sibling),
            self.copy(part, m, net.chip_y, net.core, 1, net.x, 1), self.copy(part, m, net.chip_y, net.core, 2, net.sibling)]

    def along_z(self, part, i):
        net = self.net
        m = net.group(i)
        if not isinstance(i, int) or i > 0:
            self.wait(part, m, net.chip, net.core)
        self.each_along_z(part, m, lambda copy: copy.start())

    def sideways(self, part, i):
        for copy in self.own_copies(part, self.net.group(i)):
            copy.start()

    def spread(self, part, i):
        self.along_z(part, i)
        self.sideways(part, i)

    def relay(self, part, i):
        net = self.net
        m = net.group(i)
        copies = self.relay_copies(part, m)
        for j, chip in enumerate((net.chip_x, net.chip_y)):
            self.wait(part, m, chip, net.core)
            copies[2 * j].start()
            copies[2 * j + 1].start()

    def across(self, part, i):
        net = self.net
        m = net.group(i)
        self.wait(part, m, net.chip_d, net.core, 0)
        self.wait(part, m, net.chip_d, net.core, 1)
        self.copy(part, m, net.chip_d, net.core, 2, net.sibling).start()

    def complete(self, part, i):
        net = self.net
        m = net.group(i)
        for chip in range(4):
            self.wait(part, m, chip, 1 - net.core)

    def drain(self):
        net = self.net
        for part in range(2):

            def body(m, c, part=part):
                self.each_along_z(part, m, lambda copy: copy.wait_send())
                for copy in self.own_copies(part, m) + self.relay_copies(part, m):
                    copy.wait_send()
                self.copy(part, m, net.chip_d, net.core, 2, net.sibling).wait_send()
                return c

            lax.fori_loop(0, 4, body, 0)


class Reduce:
    def __init__(self, net, g, slots, zbuf, sems, ok):
        self.net, self.g, self.slots, self.zbuf, self.sems, self.ok = net, g, slots, zbuf, sems, ok

    def lanes(self, part):
        return slice(*PARTS[part])

    def unit(self, part, m, chip, core, rows=slice(0, 96)):
        return self.g.at[m, chip, core, rows, self.lanes(part)]

    def copy(self, kind, part, key, src, dst, to):
        return pltpu.make_async_remote_copy(
            src_ref=src, dst_ref=dst, send_sem=self.sems.at[0, kind, part, key], recv_sem=self.sems.at[1, kind, part, key],
            device_id=to, device_id_type=MESH)

    def core_copy(self, part, i):
        m = self.net.group(i)
        lo, hi = PARTS[part]
        return self.copy(
            0, part, m, self.g.at[m, :, 1 - self.net.core, :, lo:hi],
            self.slots.at[lax.rem(i, 2), :, :, 0 : hi - lo], self.net.sibling)

    def to_core(self, part, i, credit):
        if credit:
            pl.semaphore_wait(self.ok.at[3, part, self.net.group(i)], 1)
        self.core_copy(part, i).start()

    def from_core(self, part, i, credit):
        net = self.net
        m = net.group(i)
        lo, hi = PARTS[part]
        copy = self.core_copy(part, i)
        copy.wait_recv()
        slot = lax.rem(i, 2)
        for chip in range(4):
            self.g[m, chip, net.core, :, lo:hi] = self.g[m, chip, net.core, :, lo:hi] + self.slots[slot, chip, :, 0 : hi - lo]
        if credit is not None:
            p, j = credit
            pl.semaphore_signal(self.ok.at[3, p, net.group(j)], inc=1, device_id=net.sibling, device_id_type=MESH)
        copy.wait_send()
        pl.semaphore_signal(self.ok.at[0, part, m], inc=1, device_id=net.x, device_id_type=MESH)
        pl.semaphore_signal(self.ok.at[1, part, m], inc=1, device_id=net.y, device_id_type=MESH)

        @pl.when(jnp.logical_and(m >= net.z, net.z > 0))
        def _():
            pl.semaphore_signal(self.ok.at[2, part, m], inc=1, device_id=net.along(-1), device_id_type=MESH)

        @pl.when(jnp.logical_and(m <= net.z, net.z < 3))
        def _():
            pl.semaphore_signal(self.ok.at[2, part, m], inc=1, device_id=net.along(1), device_id_type=MESH)

    def across_copies(self, part, m):
        net = self.net
        out = []
        for kind, rows, to in ((1, slice(0, 48), net.y), (2, slice(48, 96), net.x)):
            out.append(self.copy(
                kind, part, m, self.unit(part, m, net.chip_d, net.core, rows),
                self.unit(part, m, 0, 1 - net.core, rows), to))
        return out

    def side_copies(self, part, m):
        net = self.net
        return [
            self.copy(kind, part, m, self.unit(part, m, chip, net.core), self.unit(part, m, slot, 1 - net.core), to)
            for kind, chip, slot, to in ((3, net.chip_x, 1, net.x), (4, net.chip_y, 2, net.y))]

    def each_z(self, part, m, act):
        net = self.net
        z = net.z
        src = self.unit(part, m, net.chip, net.core)
        far = self.unit(part, m, 3, 1 - net.core)
        lo, hi = PARTS[part]
        near = self.zbuf.at[:, lo:hi]

        def copy(dst, kind, step):
            return pltpu.make_async_remote_copy(
                src_ref=src, dst_ref=dst, send_sem=self.sems.at[0, 5, part, m], recv_sem=self.sems.at[1, kind, part, m],
                device_id=net.along(step), device_id_type=MESH)

        for test, dst, kind, step in ((m > z, far, 5, 1), (m < z - 1, far, 5, -1), (m == z - 1, near, 6, -1)):

            @pl.when(test)
            def _(dst=dst, kind=kind, step=step):
                act(copy(dst, kind, step))

    def z_arrived(self, part, m, near):
        net = self.net
        lo, hi = PARTS[part]
        ref = self.zbuf.at[:, lo:hi] if near else self.unit(part, m, 3, 1 - net.core)
        pltpu.make_async_remote_copy(
            src_ref=ref, dst_ref=ref, send_sem=self.sems.at[0, 5, part, m],
            recv_sem=self.sems.at[1, 6 if near else 5, part, m], device_id=net.sibling, device_id_type=MESH).wait_recv()
        if near:
            mine = self.g[m, net.chip, net.core, :, lo:hi]
            self.g[m, net.chip, net.core, :, lo:hi] = mine + self.zbuf[:, lo:hi]
        else:
            self.add(part, m, net.chip, 3)

    def add(self, part, m, chip, slot, rows=slice(0, 96)):
        net = self.net
        lanes = self.lanes(part)
        self.g[m, chip, net.core, rows, lanes] = self.g[m, chip, net.core, rows, lanes] + self.g[m, slot, 1 - net.core, rows, lanes]

    def start_across(self, part, i):
        m = self.net.group(i)
        pl.semaphore_wait(self.ok.at[0, part, m], 1)
        pl.semaphore_wait(self.ok.at[1, part, m], 1)
        for copy in self.across_copies(part, m):
            copy.start()

    def start_sides(self, part, i):
        net = self.net
        m = net.group(i)
        by_y, by_x = self.across_copies(part, m)
        by_y.wait_recv()
        self.add(part, m, net.chip_x, 0, slice(0, 48))
        by_x.wait_recv()
        self.add(part, m, net.chip_y, 0, slice(48, 96))
        for copy in self.side_copies(part, m):
            copy.start()

    def gather_sides(self, part, i):
        net = self.net
        m = net.group(i)
        for slot, copy in zip((1, 2), self.side_copies(part, m)):
            copy.wait_recv()
            self.add(part, m, net.chip, slot)

    def send_z(self, part, m):
        pl.semaphore_wait(self.ok.at[2, part, m], 1)
        self.each_z(part, m, lambda copy: copy.start())

    def pass_z(self, part, m):
        self.z_arrived(part, m, False)
        self.send_z(part, m)

    def wave(self, part, n):
        z = self.net.z
        for at, groups, act in (
            ((0, (3, 2, 1), self.send_z), (3, (0, 1, 2), self.send_z)),
            ((1, (3, 2), self.pass_z), (2, (0, 1), self.pass_z)),
            ((1, (0,), self.pass_z), (2, (3,), self.pass_z)),
        )[n]:

            @pl.when(z == at)
            def _(groups=groups, act=act):
                for m in groups:
                    act(part, m)

    def step(self, n):
        if n > 0:
            self.start_sides(1 if n < 5 else 0, (n - 1) % 4)
        if n < 8:
            self.start_across(1 if n < 4 else 0, n % 4)

    def total(self, part):
        net = self.net

        @pl.when(net.z > 0)
        def _():
            self.z_arrived(part, net.z, False)

        @pl.when(net.z < 3)
        def _():
            self.z_arrived(part, net.z, True)

        return self.g[net.z, net.chip, net.core, :, self.lanes(part)].astype(F32)

    def drain(self):
        net = self.net
        for part in range(2):

            def body(m, c, part=part):
                for copy in self.across_copies(part, m) + self.side_copies(part, m):
                    copy.wait_send()
                self.each_z(part, m, lambda copy: copy.wait_send())
                return c

            lax.fori_loop(0, 4, body, 0)


def greet(net):
    barrier = pltpu.get_barrier_semaphore()
    for other in range(1, 8):
        pl.semaphore_signal(barrier, inc=1, device_id=(lax.rem(net.dp + other, 8), net.z), device_id_type=MESH)
    for k in range(1, 4):
        pl.semaphore_signal(barrier, inc=1, device_id=net.up(k), device_id_type=MESH)
    return barrier


def share_gains(net, parts, send, recv):
    copies = []
    for k in range(1, 8):
        copies.append(pltpu.make_async_remote_copy(
            src_ref=parts.at[net.dp], dst_ref=parts.at[net.dp], send_sem=send.at[k - 1], recv_sem=recv.at[net.dp],
            device_id=(lax.rem(net.dp + k, 8), net.z), device_id_type=MESH))
        copies[-1].start()
    return copies


def join_gains(net, parts, send, recv, gain):
    for k in range(1, 8):
        other = lax.rem(net.dp + k, 8)
        pltpu.make_async_remote_copy(
            src_ref=parts.at[other], dst_ref=parts.at[other], send_sem=send.at[k - 1], recv_sem=recv.at[other],
            device_id=net.sibling, device_id_type=MESH).wait_recv()
    total = jnp.zeros(gain.shape, F32)
    for d in range(8):
        piece = jnp.concatenate([parts[d], jnp.zeros((8, gain.shape[1] - 128), F32)], axis=1)
        total = total + pltpu.roll(piece, 96 * d, 1)
    gain[...] = total


def build_package(w, net, q_ref, k_ref, v_ref, o_ref, g_ref, u_ref, d_ref):
    lanes = low_lanes()
    ot = o_ref[...].T
    pad = jnp.zeros((96, 64), F32)
    at = (net.z, net.chip, net.core)

    def put(tile, value):
        w[at[0], at[1], at[2], :, 128 * tile : 128 * (tile + 1)] = value.astype(BF16)

    for j, ref in enumerate((q_ref, k_ref, v_ref)):
        put(2 * j, ref[:, 0:128])
        last = jnp.concatenate([ref[:, 128:192], pad], axis=1)
        extra = jnp.concatenate([ot[:, 64 * j : 64 * (j + 1)], pad], axis=1)
        put(2 * j + 1, jnp.where(lanes, last, pltpu.roll(extra, 64, 1)))
    w[at[0], at[1], at[2], :, 768:1280] = g_ref[...].astype(BF16)
    w[at[0], at[1], at[2], :, 1280:1792] = u_ref[...].astype(BF16)
    w[at[0], at[1], at[2], :, 1792:2304] = d_ref[...].astype(BF16)


def rows768(ref, m, lo, hi):
    return ref[m, :, :, :, lo:hi].reshape(768, hi - lo)


def put768(ref, m, lo, hi, value):
    ref[m, :, :, :, lo:hi] = value.reshape(4, 2, 96, hi - lo)


class RowGather:
    def __init__(self, net, pool, send, recv, ok):
        self.net, self.pool, self.send, self.recv, self.ok = net, pool, send, recv, ok

    def copy(self, m, way):
        net = self.net
        return pltpu.make_async_remote_copy(
            src_ref=self.pool.at[m], dst_ref=self.pool.at[m], send_sem=self.send.at[way, m], recv_sem=self.recv.at[m],
            device_id=net.along(1 - 2 * way), device_id_type=MESH)

    def each(self, m, act):
        net = self.net

        @pl.when(jnp.logical_and(m <= net.z, net.z < 3))
        def _():
            act(self.copy(m, 0))

        @pl.when(jnp.logical_and(m >= net.z, net.z > 0))
        def _():
            act(self.copy(m, 1))

    def start(self):
        net = self.net
        if self.ok is not None:
            for test, way in ((net.z < 3, 0), (net.z > 0, 1)):

                @pl.when(test)
                def _(way=way):
                    pl.semaphore_signal(self.ok.at[1 - way], inc=1, device_id=net.along(1 - 2 * way), device_id_type=MESH)

        for test, way in ((net.z < 3, 0), (net.z > 0, 1)):

            @pl.when(test)
            def _(way=way):
                if self.ok is not None:
                    pl.semaphore_wait(self.ok.at[way], 1)
                self.copy(net.z, way).start()

    def relay(self, i):
        z = self.net.z
        m = self.net.group(i)

        @pl.when(jnp.logical_and(z > 0, z < 3))
        def _():
            self.copy(m, 0).wait_recv()
            self.each(m, lambda copy: copy.start())

    def arrived(self, i):
        z = self.net.z
        m = self.net.group(i)

        @pl.when(jnp.logical_or(z == 0, z == 3))
        def _():
            self.copy(m, 0).wait_recv()

        return m

    def drain(self):
        def body(m, c):
            self.each(m, lambda copy: copy.wait_send())
            return c

        lax.fori_loop(0, 4, body, 0)


def mega_kernel(
    len_ref, x_ref, dy_ref, q_ref, k_ref, v_ref, o_ref, gate_ref, up_ref, down_ref, ga_ref, gf_ref,
    out_ref, gt_ref, gq_ref, gk_ref, gv_ref, go_ref, gate_grad_ref, up_grad_ref, down_grad_ref, gga_ref, ggf_ref,
    w, g, slots, pool, gain, gain_parts, gg_out, gg_in, gg_z, bias, n1t, n2t, dypt, spare, qkv, hx, o_own, wo, lse, lse_t,
    h, acc, res, zbuf,
    ag_send, ag_recv, gn_send, gn_recv, in_sem, rs_sems, ok, gt_send, gt_recv, gt_ok, hx_send, hx_recv, out_sem, gs_send,
    gs_recv, gz_send, gz_recv,
):
    net = Net()
    bins = 4
    seq = 1536
    me = net.z
    xp, dyp, n1, n2 = (pool.at[j] for j in range(4))
    n_b = spare.at[0]
    barrier = greet(net)
    halves = []
    for t, ref in enumerate((x_ref, dy_ref)):
        for j in range(2):
            halves.append(pltpu.make_async_copy(
                ref.at[j], g.at[t, :, :, :, 768 * j : 768 * (j + 1)], in_sem.at[2 * t + j]))
    for copy in halves:
        copy.start()
    ag = Gather(net, w, ag_send, ag_recv)
    rs = Reduce(net, g, slots, zbuf, rs_sems, ok)
    rows = RowGather(net, pool, gt_send, gt_recv, gt_ok)
    mids = RowGather(net, hx, hx_send, hx_recv, None)
    build_package(w, net, q_ref, k_ref, v_ref, o_ref, gate_ref, up_ref, down_ref)
    pad = jnp.zeros((1, 32), F32)
    mine = jnp.concatenate([
        jnp.concatenate([ga_ref[...], pad], axis=1), jnp.concatenate([gf_ref[...], pad], axis=1),
        jnp.zeros((6, 128), F32)], axis=0)
    gain_parts[net.dp] = mine.astype(BF16).astype(F32)
    pl.semaphore_wait(barrier, 10)
    gain_copies = share_gains(net, gain_parts, gn_send, gn_recv)
    ag.spread(0, 0)

    place = placement(len_ref, bins)
    lse[...] = jnp.zeros_like(lse)

    def set_bias(b):
        _, segment = packed_source(place, b * CAP, (CAP, 1), 0)
        _, segment_row = packed_source(place, b * CAP, (1, CAP), 1)
        bias[...] = jnp.where(segment == segment_row, 0.0, NEG)

    def pack(b, t, store):
        def body(j, c):
            source, _ = packed_source(place, b * CAP + j * 128, (128, 1), 0)
            pick = (source == lax.broadcasted_iota(jnp.int32, (128, seq), 1)).astype(BF16)
            value = nn(pick[:, 0:768], rows768(g, t, 0, 768)) + nn(pick[:, 768:1536], rows768(g, t, 768, 1536))
            store(pl.ds(pl.multiple_of(j * 128, 128), 128), value)
            return c

        lax.fori_loop(0, CAP // 128, body, 0)

    def drops(b, first, rows, count=1):
        source, _ = packed_source(place, b * CAP, (1, count * CAP), 1)
        return (lax.broadcasted_iota(jnp.int32, (rows, count * CAP), 0) + first == source).astype(BF16)

    def norm(src, dst, gain_row):
        def body(j, c):
            at = pl.ds(pl.multiple_of(j * 128, 128), 128)
            values = src[at, :]
            dst[at, :] = (values * rms_rows(values) * gain_row).astype(BF16)
            return c

        lax.fori_loop(0, CAP // 128, body, 0)

    for copy in halves:
        copy.wait()
    def store_x(at, value):
        xp[at, :] = value.astype(BF16)
        h[at, :] = value

    def store_dy(at, value):
        dyp[at, :] = value.astype(BF16)

    pack(me, 0, store_x)
    ag.spread(0, 1)
    ag.relay(0, 0)
    pack(me, 1, store_dy)
    join_gains(net, gain_parts, gn_send, gn_recv, gain)
    g1 = gain[0:1, :]
    g2 = gain[1:2, :]
    ag.spread(0, 2)
    ag.relay(0, 1)
    ag.across(0, 0)
    norm(h, n1, g1)
    n1t[...] = n1[...].T
    dypt[...] = dyp[...].T

    set_bias(me)
    ag.spread(0, 3)
    ag.relay(0, 2)
    ag.across(0, 1)
    ag.along_z(1, 0)
    ag.relay(0, 3)
    ag.across(0, 2)
    ag.sideways(1, 0)
    ag.across(0, 3)
    ag.along_z(1, 1)
    ag.sideways(1, 1)

    def own_forward(i, c):
        m = net.group(i)
        ag.complete(0, i)
        first, second = out_weight_tiles_at(w, m)
        wo[m, :, 0:128] = first
        wo[m, :, 128:256] = second
        qkv[m] = nn(n1[...], rows768(w, m, 0, 768)).astype(BF16)
        attend_group(qkv, m, bias, o_own, m, lse)
        h[...] += nt(o_own[m], wo[m])

        @pl.when(i == 0)
        def _():
            ag.along_z(1, 2)

        @pl.when(i == 1)
        def _():
            ag.relay(1, 0)
            ag.sideways(1, 2)

        @pl.when(i == 3)
        def _():
            ag.along_z(1, 3)
            ag.relay(1, 1)
            ag.across(1, 0)
            ag.sideways(1, 3)

        return c

    lax.fori_loop(0, 4, own_forward, 0)
    hx[me] = h[...].astype(BF16)
    mids.start()
    norm(h, n2, g2)
    n2t[...] = n2[...].T
    lse_t[...] = lse[...].T[0:16, :]
    acc[...] = jnp.zeros_like(acc)
    res[...] = h[...]

    def ffn_back(i, c):
        @pl.when(i == 1)
        def _():
            ag.relay(1, 2)
            ag.across(1, 1)

        @pl.when(i == 2)
        def _():
            ag.relay(1, 3)
            ag.across(1, 2)
            mids.relay(1)
            mids.relay(2)

        @pl.when(i == 3)
        def _():
            ag.across(1, 3)

        m = net.group(i)
        ag.complete(1, i)

        @pl.when(i == 3)
        def _():
            rs.step(0)

        for lo in (0, 256):
            w_gate = rows768(w, m, 768 + lo, 1024 + lo)
            w_up = rows768(w, m, 1280 + lo, 1536 + lo)
            w_down = rows768(w, m, 1792 + lo, 2048 + lo)
            a = nn(n2[...], w_gate)
            up = nn(n2[...], w_up)
            t = gelu_parts(a)
            gel = 0.5 * a * (1.0 + t)
            u = (gel * up).astype(BF16)
            res[...] += nt(u, w_down)
            put768(g, m, 1792 + lo, 2048 + lo, nn(dypt[...], u).astype(BF16))
            du = nn(dyp[...], w_down)
            slope = 0.5 * (1.0 + t) + 0.5 * a * (1.0 - t * t) * (GELU_COEF * (1.0 + 3.0 * GELU_CUBE * a * a))
            da = (du * up * slope).astype(BF16)
            db = (du * gel).astype(BF16)
            put768(g, m, 768 + lo, 1024 + lo, nn(n2t[...], da).astype(BF16))
            put768(g, m, 1280 + lo, 1536 + lo, nn(n2t[...], db).astype(BF16))
            acc[...] += nt(da, w_gate) + nt(db, w_up)

        @pl.when(i < 2)
        def _():
            rs.to_core(1, i, False)

        @pl.when(i >= 2)
        def _():
            rs.to_core(1, i, True)

        @pl.when(jnp.logical_and(i >= 1, i < 3))
        def _():
            rs.from_core(1, i - 1, (1, i + 1))

        @pl.when(i == 3)
        def _():
            rs.from_core(1, 2, (0, 0))

        return c

    lax.fori_loop(0, 4, ffn_back, 0)
    rs.step(1)

    def hidden_back(j, total):
        at = pl.ds(pl.multiple_of(j * 128, 128), 128)
        ho = h[at, :]
        r2 = rms_rows(ho)
        dn2 = acc[at, :]
        wg = dn2 * g2
        dh = dyp[at, :].astype(F32) + r2 * wg - ho * (r2 * r2 * r2) * jnp.mean(wg * ho, axis=1, keepdims=True)
        h[at, :] = dh
        n2[at, :] = dh.astype(BF16)
        acc[at, :] = jnp.zeros_like(dh)
        return total + jnp.sum(dn2 * ho * r2, axis=0, keepdims=True)

    gg_ffn = lax.fori_loop(0, CAP // 128, hidden_back, jnp.zeros((1, 768), F32))
    n2t[...] = n2[...].T
    rs.from_core(1, 3, (0, 1))

    def attn_back(i, c):
        m = net.group(i)
        spare[0, :, 0:256] = nn(n2[...], wo[m]).astype(BF16)
        attend_group_back(qkv, m, bias, lse_t, spare, 0, qkv)
        acc[...] += nt(qkv[m], rows768(w, m, 0, 768))

        @pl.when(i == 0)
        def _():
            mids.relay(3)

        @pl.when(i == 1)
        def _():
            rs.step(2)

        @pl.when(i == 2)
        def _():
            rs.gather_sides(1, 0)

        return c

    lax.fori_loop(0, 4, attn_back, 0)

    def input_back(j, total):
        at = pl.ds(pl.multiple_of(j * 128, 128), 128)
        xb = xp[at, :].astype(F32)
        r1 = rms_rows(xb)
        dn1 = acc[at, :]
        wa = dn1 * g1
        gt = h[at, :] + r1 * wa - xb * (r1 * r1 * r1) * jnp.mean(wa * xb, axis=1, keepdims=True)
        n_b[at, :] = gt.astype(BF16)
        return total + jnp.sum(dn1 * xb * r1, axis=0, keepdims=True)

    gg_attn = lax.fori_loop(0, CAP // 128, input_back, jnp.zeros((1, 768), F32))
    pool[me] = n_b[...]
    rows.start()
    rs.step(3)
    gg = jnp.concatenate([gg_attn, gg_ffn, jnp.zeros((6, 768), F32)], axis=0)
    for d in range(8):
        gg_out[d] = pltpu.roll(gg, (768 - 96 * d) % 768, 1)[:, 0:128] if d else gg[:, 0:128]

    def gg_copy(k):
        to = lax.rem(net.dp + k, 8)
        return pltpu.make_async_remote_copy(
            src_ref=gg_out.at[to], dst_ref=gg_in.at[net.dp], send_sem=gs_send.at[k - 1], recv_sem=gs_recv.at[net.dp],
            device_id=(to, net.z), device_id_type=MESH)

    for k in range(1, 8):
        gg_copy(k).start()

    def attn_grads(i, c):
        m = net.group(i)
        go = nn(n2t[...], o_own[m])
        lanes = low_lanes()
        for j in range(3):
            grad = nn(n1t[...], qkv[m, :, 256 * j : 256 * (j + 1)])
            put768(g, m, 256 * j, 256 * j + 128, grad[:, 0:128].astype(BF16))
            if j == 1:
                extra = go[:, 0:128]
            else:
                extra = pltpu.roll(go[:, 64 * j : 64 * j + 128], 64, 1)
            put768(g, m, 256 * j + 128, 256 * (j + 1), jnp.where(lanes, grad[:, 128:256], extra).astype(BF16))

        rs.to_core(0, i, True)

        @pl.when(jnp.logical_and(i >= 1, i < 3))
        def _():
            rs.from_core(0, i - 1, (0, i + 1))

        @pl.when(i == 3)
        def _():
            rs.from_core(0, 2, None)
            rs.gather_sides(1, 1)

        return c

    lax.fori_loop(0, 4, attn_grads, 0)
    rs.from_core(0, 3, None)
    rs.step(4)

    part = gg_out[net.dp]
    for k in range(1, 8):
        other = lax.rem(net.dp + k, 8)
        pltpu.make_async_remote_copy(
            src_ref=gg_out.at[other], dst_ref=gg_in.at[other], send_sem=gs_send.at[k - 1], recv_sem=gs_recv.at[other],
            device_id=net.sibling, device_id_type=MESH).wait_recv()
        part = part + gg_in[other]
    gg_z[me] = part
    gz_copies = [pltpu.make_async_remote_copy(
        src_ref=gg_z.at[me], dst_ref=gg_z.at[me], send_sem=gz_send.at[k - 1], recv_sem=gz_recv.at[me],
        device_id=net.up(k), device_id_type=MESH) for k in range(1, 4)]
    for copy in gz_copies:
        copy.start()

    mids.drain()
    hx[me] = res[...].astype(BF16)

    def ffn_out(j, c):
        b = mids.arrived(j)
        acc[...] = hx[b].astype(F32)
        norm(acc, n_b, g2)

        def ffn(m, c):
            a = nn(n_b[...], rows768(w, m, 768, 1280))
            up = nn(n_b[...], rows768(w, m, 1280, 1792))
            u = (0.5 * a * (1.0 + gelu_parts(a)) * up).astype(BF16)
            acc[...] += nt(u, rows768(w, m, 1792, 2304))

            @pl.when(jnp.logical_and(j == 2, m == 1))
            def _():
                rs.step(5)
                rs.gather_sides(1, 2)
                rs.gather_sides(1, 3)

            @pl.when(jnp.logical_and(j == 3, m == 1))
            def _():
                rs.step(6)

            return c

        lax.fori_loop(0, 4, ffn, 0)
        hx[b] = acc[...].astype(BF16)

        @pl.when(j == 2)
        def _():
            rows.relay(1)
            rows.relay(2)
            rs.wave(1, 0)

        @pl.when(j == 3)
        def _():
            rs.step(7)

        return c

    lax.fori_loop(1, 4, ffn_out, 0)

    def place_out(j, c):
        at = pl.ds(pl.multiple_of(j * 256, 256), 256)
        pick = drops(0, j * 256, 256, 4)
        value = nn(pick[:, 0:CAP], hx[0])
        for b in range(1, 4):
            value = value + nn(pick[:, b * CAP : (b + 1) * CAP], hx[b])
        out_ref[at, :] = value.astype(BF16)
        return c

    lax.fori_loop(0, seq // 256, place_out, 0)
    rs.step(8)
    rows.relay(3)
    rs.wave(1, 1)
    for i in range(3):
        rs.gather_sides(0, i)

    def place_rows(bs, first):
        def body(j, c):
            value = nn(drops(bs[0], CAP * j, CAP), pool[bs[0]])
            for b in bs[1:]:
                value = value + nn(drops(b, CAP * j, CAP), pool[b])
            if not first:
                value = value + qkv[j].astype(F32)
            qkv[j] = value.astype(BF16)
            return c

        lax.fori_loop(0, 3, body, 0)

    place_rows([me, rows.arrived(1), rows.arrived(2)], True)
    rs.gather_sides(0, 3)
    rs.wave(0, 0)
    rs.wave(1, 2)
    rs.wave(0, 1)
    ffn_sum = rs.total(1)
    gate_grad_ref[...] = ffn_sum[:, 0:512]
    up_grad_ref[...] = ffn_sum[:, 512:1024]
    down_grad_ref[...] = ffn_sum[:, 1024:1536]
    rs.wave(0, 2)
    place_rows([rows.arrived(3)], False)
    out = pltpu.make_async_copy(qkv.at[0:3], gt_ref, out_sem)
    out.start()

    for k in range(1, 4):
        other = lax.rem(me + k, 4)
        pltpu.make_async_remote_copy(
            src_ref=gg_z.at[other], dst_ref=gg_z.at[other], send_sem=gz_send.at[k - 1], recv_sem=gz_recv.at[other],
            device_id=net.up(k), device_id_type=MESH).wait_recv()
        part = part + gg_z[other]
    gga_ref[...] = part[0:1, 0:96]
    ggf_ref[...] = part[1:2, 0:96]
    attn_sum = rs.total(0)
    gq_ref[...] = attn_sum[:, 0:192]
    gk_ref[...] = attn_sum[:, 256:448]
    gv_ref[...] = attn_sum[:, 512:704]
    go_ref[...] = jnp.concatenate([attn_sum[:, 192:256], attn_sum[:, 448:512], attn_sum[:, 704:768]], axis=1).T
    out.wait()
    for copy in gain_copies + gz_copies:
        copy.wait_send()
    for k in range(1, 8):
        gg_copy(k).wait_send()
    rows.drain()
    rs.drain()
    ag.drain()


def finish_kernel(*refs):
    count = len(refs) // 2
    refs[count][...] = refs[0][...].astype(F32)
    refs[count + 1][...] = refs[1][...]

    @pl.when(pl.program_id(0) == 0)
    def _():
        for j in range(2, count):
            refs[count + j][...] = refs[j][...]


def out_weight_tiles_at(w, m):
    lanes = low_lanes()
    t1 = rows768(w, m, 128, 256).astype(F32)
    t3 = rows768(w, m, 384, 512).astype(F32)
    t5 = rows768(w, m, 640, 768).astype(F32)
    first = jnp.where(lanes, pltpu.roll(t1, 64, 1), t3)
    second = jnp.where(lanes, pltpu.roll(t5, 64, 1), 0.0)
    return first.astype(BF16), second.astype(BF16)


def on_this_slice(
    tokens, lengths, query_weight, key_weight, value_weight, out_weight, attn_gain, gate_weight, up_weight, down_weight,
    ffn_gain, cotangent,
):
    rows, seq, width = tokens.shape
    vmem = pl.BlockSpec(memory_space=pltpu.VMEM)
    smem = pl.BlockSpec(memory_space=pltpu.SMEM)
    dma = pltpu.SemaphoreType.DMA
    act = pltpu.VMEM((CAP, width), BF16)
    act_t = pltpu.VMEM((width, CAP), BF16)
    wide = pltpu.VMEM((CAP, width), F32)
    hbm = pl.BlockSpec(memory_space=pl.ANY)

    def f32(*shape):
        return jax.ShapeDtypeStruct(shape, F32)

    out, gt, gq, gk, gv, go, gate, up, down, gain_a, gain_f = pl.pallas_call(
        mega_kernel,
        out_shape=(
            jax.ShapeDtypeStruct((seq, width), BF16), jax.ShapeDtypeStruct((3, CAP, width), BF16),
            f32(96, 192), f32(96, 192), f32(96, 192), f32(192, 96), f32(96, 512), f32(96, 512), f32(96, 512), f32(1, 96), f32(1, 96),
        ),
        in_specs=[smem, hbm, hbm] + [vmem] * 9,
        out_specs=[vmem, hbm] + [vmem] * 9,
        scratch_shapes=[
            pltpu.VMEM((4, 4, 2, 96, 2304), BF16),
            pltpu.VMEM((4, 4, 2, 96, 2304), BF16),
            pltpu.VMEM((2, 4, 96, 1536), BF16),
            pltpu.VMEM((4, CAP, width), BF16),
            pltpu.VMEM((8, width), F32),
            pltpu.VMEM((8, 8, 128), F32), pltpu.VMEM((8, 8, 128), F32), pltpu.VMEM((8, 8, 128), F32),
            pltpu.VMEM((4, 8, 128), F32),
            pltpu.VMEM((CAP, CAP), F32),
            act_t, act_t, act_t, pltpu.VMEM((1, CAP, width), BF16),
            pltpu.VMEM((4, CAP, width), BF16),
            pltpu.VMEM((4, CAP, width), BF16),
            pltpu.VMEM((4, CAP, 256), BF16),
            pltpu.VMEM((4, width, 256), BF16),
            pltpu.VMEM((CAP, 128), F32),
            pltpu.VMEM((16, CAP), F32),
            wide, wide, wide,
            pltpu.VMEM((96, 2304), BF16),
            dma((2, 4, 4, 5)), dma((2, 4, 4, 2, 3)), dma((7,)), dma((8,)), dma((4,)),
            dma((2, 7, 2, 4)), pltpu.SemaphoreType.REGULAR((4, 2, 4)),
            dma((2, 4)), dma((4,)), pltpu.SemaphoreType.REGULAR((2,)), dma((2, 4)), dma((4,)), dma, dma((7,)), dma((8,)), dma((3,)), dma((4,)),
        ],
        compiler_params=pltpu.CompilerParams(
            vmem_limit_bytes=60 * 2**20, collective_id=0, has_side_effects=True),
        name="layer",
    )(lengths, tokens.reshape(2, 4, 2, 96, width), cotangent.reshape(2, 4, 2, 96, width), query_weight, key_weight,
      value_weight, out_weight, gate_weight, up_weight, down_weight.T, attn_gain.reshape(1, 96), ffn_gain.reshape(1, 96))
    rest = (out, gq, gk, gv, go, gate, up, down, gain_a, gain_f)
    block = pl.BlockSpec((256, width), lambda i: (i, 0))
    whole = [pl.BlockSpec(a.shape, lambda i: (0, 0)) for a in rest[1:]]
    gt, out, gq, gk, gv, go, gate, up, down, gain_a, gain_f = pl.pallas_call(
        finish_kernel,
        grid=(seq // 256,),
        out_shape=(f32(seq, width),) + tuple(jax.ShapeDtypeStruct(a.shape, a.dtype) for a in rest),
        in_specs=[block, block] + whole,
        out_specs=(block, block) + tuple(whole),
        name="finish",
    )(gt.reshape(seq, width), *rest)
    return (
        out.reshape(rows, seq, width), gt.reshape(rows, seq, width), gq, gk, gv, go, gain_a.reshape(96), gate, up, down.T,
        gain_f.reshape(96),
    )
def solution(mesh):
    body = on_this_slice if dict(mesh.shape) == {"dp": 8, "mp": 4} else per_device
    return jax.shard_map(
        body,
        mesh=mesh,
        in_specs=(
            P("dp", None, None), P("dp", None), P("dp", "mp"), P("dp", "mp"), P("dp", "mp"), P("mp", "dp"), P("dp"),
            P("dp", "mp"), P("dp", "mp"), P("mp", "dp"), P("dp"), P("dp", None, None),
        ),
        out_specs=(
            P("dp", None, None), P("dp", None, None), P("dp", "mp"), P("dp", "mp"), P("dp", "mp"), P("mp", "dp"),
            P("dp"), P("dp", "mp"), P("dp", "mp"), P("mp", "dp"), P("dp"),
        ),
        check_vma=False,
    )
```

```python
import functools
import jax
import jax.numpy as jnp
from jax import lax
from jax.experimental import pallas as pl
from jax.experimental.pallas import tpu as pltpu
from jax.sharding import PartitionSpec as P

EPSILON = 1e-06
GELU_COEF = 0.7978845608028654
GELU_CUBE = 0.044715
CAP = 512
NEG = -1e30
F32 = jnp.float32
BF16 = jnp.bfloat16


def nn(a, b):
    return lax.dot_general(a, b, (((1,), (0,)), ((), ())), preferred_element_type=F32)


def nt(a, b):
    return lax.dot_general(a, b, (((1,), (1,)), ((), ())), preferred_element_type=F32)


def tn(a, b):
    return lax.dot_general(a, b, (((0,), (0,)), ((), ())), preferred_element_type=F32)


def placement(len_ref, bins):
    count = len_ref.shape[1]
    sizes = [len_ref[0, i] for i in range(count)]
    starts = [jnp.int32(0)]
    for i in range(count - 1):
        starts.append(starts[-1] + sizes[i])
    ranks = []
    for i in range(count):
        rank = jnp.int32(0)
        for j in range(count):
            if j < i:
                rank = rank + jnp.where(sizes[j] >= sizes[i], 1, 0)
            elif j > i:
                rank = rank + jnp.where(sizes[j] > sizes[i], 1, 0)
        ranks.append(rank)
    fills = [jnp.int32(0)] * (bins - 1)
    spots = [jnp.int32(0)] * count
    for k in range(count):
        size = jnp.int32(0)
        for i in range(count):
            size = size + jnp.where(ranks[i] == k, sizes[i], 0)
        if k == 0:
            spot = jnp.int32((bins - 1) * CAP)
        else:
            free = jnp.int32(1)
            spot = jnp.int32(0)
            for b in range(bins - 1):
                fits = jnp.where(fills[b] + size <= CAP, free, 0) if b < bins - 2 else free
                spot = spot + fits * (b * CAP + fills[b])
                fills[b] = fills[b] + fits * size
                free = free - fits
        for i in range(count):
            spots[i] = spots[i] + jnp.where(ranks[i] == k, spot, 0)
    return starts, sizes, spots


def packed_source(place, first, shape, axis):
    spot = lax.broadcasted_iota(jnp.int32, shape, axis) + first
    source = jnp.full(shape, -1, jnp.int32)
    segment = jnp.full(shape, -1, jnp.int32)
    for i, (start, size, at) in enumerate(zip(*place)):
        here = (spot >= at) & (spot < at + size)
        source = jnp.where(here, spot + (start - at), source)
        segment = jnp.where(here, i, segment)
    return source, segment


def low_lanes():
    return lax.broadcasted_iota(jnp.int32, (1, 128), 1) < 64


def half(tile, low):
    lanes = low_lanes()
    return jnp.where(lanes if low else jnp.logical_not(lanes), tile, jnp.zeros_like(tile))


HEADS = ((0, 2, 4, True), (0, 2, 4, False), (1, 3, 5, True))


def tile_of(ref, m, t, rows=slice(None)):
    return ref[m, rows, 128 * t : 128 * (t + 1)]


def attend_group(qkv, m, bias, o_ref, at, lse_ref=None, qb=256):
    for i in range(CAP // qb):
        rows = slice(i * qb, (i + 1) * qb)
        scores = []
        for tq, tk, tv, low in HEADS:
            q = half(tile_of(qkv, m, tq, rows), low) * jnp.asarray(0.125, BF16)
            scores.append(nt(q, tile_of(qkv, m, tk)))
        shares, totals = [], []
        for head, s in enumerate(scores):
            s = s + bias[rows, :]
            top = jnp.max(s, axis=1, keepdims=True)
            e = jnp.exp(s - top)
            total = jnp.sum(e, axis=1, keepdims=True)
            shares.append(e.astype(BF16))
            totals.append(total)
            if lse_ref is not None:
                lane = lax.broadcasted_iota(jnp.int32, (1, 128), 1)
                lse_ref[rows, :] = jnp.where(lane == 3 * m + head, top + jnp.log(total), lse_ref[rows, :])
        parts = []
        for (tq, tk, tv, low), e, total in zip(HEADS, shares, totals):
            parts.append(nn(e, half(tile_of(qkv, m, tv), low)) * (1.0 / total))
        o_ref[at, rows, 0:128] = (parts[0] + parts[1]).astype(BF16)
        o_ref[at, rows, 128:256] = parts[2].astype(BF16)


def attend_group_back(qkv, m, bias, lse_t, do_ref, at, dqkv):
    dk = [None, None]
    dv = [None, None]
    dq = [None, None]
    scale = jnp.asarray(0.125, BF16)
    for head, (tq, tk, tv, low) in enumerate(HEADS):
        j = 0 if head < 2 else 1
        k = half(tile_of(qkv, m, tk), low) * scale
        s = nt(k, tile_of(qkv, m, tq))
        do = do_ref[at, :, 128 * j : 128 * (j + 1)]
        dp = nt(half(tile_of(qkv, m, tv), low), do)
        p = jnp.exp(s + bias[...] - lse_t[pl.ds(3 * m + head, 1), :])
        delta = jnp.sum(p * dp, axis=0, keepdims=True)
        ds = (p * (dp - delta)).astype(BF16)
        parts = (
            nn(p.astype(BF16), half(do, low)), nn(ds, half(tile_of(qkv, m, tq), low) * scale), tn(ds, k))
        for total, part in zip((dv, dk, dq), parts):
            total[j] = part if total[j] is None else total[j] + part
    for j in range(2):
        for t, total in ((0, dq), (2, dk), (4, dv)):
            dqkv[m, :, 128 * (t + j) : 128 * (t + j + 1)] = total[j].astype(BF16)


def out_weight_tiles(w, m):
    lanes = low_lanes()
    t1 = tile_of(w, m, 1).astype(F32)
    t3 = tile_of(w, m, 3).astype(F32)
    t5 = tile_of(w, m, 5).astype(F32)
    first = jnp.where(lanes, pltpu.roll(t1, 64, 1), t3)
    second = jnp.where(lanes, pltpu.roll(t5, 64, 1), 0.0)
    return first.astype(BF16), second.astype(BF16)


def gelu_parts(a):
    inner = GELU_COEF * (a + GELU_CUBE * a * a * a)
    t = jnp.tanh(inner)
    return t


def rms_rows(values):
    return lax.rsqrt(jnp.mean(values * values, axis=1, keepdims=True) + EPSILON)


def layer_kernel(
    len_ref, x_ref, dy_ref, w_ref, gain_ref, which_ref,
    out_ref, gt_ref, g_ref, gg_ref,
    bias, xp, dyp, n1, n1t, n2, n2t, dypt, dhbt, qkv, o_all, wo, lse, lse_t, do, dqkv, h, acc,
):
    bins = w_ref.shape[0]
    seq = x_ref.shape[0]
    place = placement(len_ref, bins)
    me = which_ref[0]
    g1 = gain_ref[0:1, :]
    g2 = gain_ref[1:2, :]

    def wo_body(m, c):
        first, second = out_weight_tiles(w_ref, m)
        wo[m, :, 0:128] = first
        wo[m, :, 128:256] = second
        return c

    lax.fori_loop(0, bins, wo_body, 0)
    lse[...] = jnp.zeros_like(lse)

    def forward(b):
        source, segment = packed_source(place, b * CAP, (CAP, 1), 0)
        _, segment_row = packed_source(place, b * CAP, (1, CAP), 1)
        bias[...] = jnp.where(segment == segment_row, 0.0, NEG)
        pick = (source == lax.broadcasted_iota(jnp.int32, (CAP, seq), 1)).astype(BF16)
        xb = nn(pick, x_ref[...])
        xp[...] = xb.astype(BF16)
        dyp[...] = nn(pick, dy_ref[...]).astype(BF16)
        n1[...] = (xb * rms_rows(xb) * g1).astype(BF16)
        h[...] = xb

        def m_body(m, c):
            qkv[m] = nn(n1[...], w_ref[m, :, 0:768]).astype(BF16)
            attend_group(qkv, m, bias, o_all, m, lse)
            h[...] += nt(o_all[m], wo[m])
            return c

        lax.fori_loop(0, bins, m_body, 0)
        hb = h[...]
        n2[...] = (hb * rms_rows(hb) * g2).astype(BF16)

    def ffn_out(b):
        acc[...] = h[...]

        def m_body(m, c):
            a = nn(n2[...], w_ref[m, :, 768:1280])
            up = nn(n2[...], w_ref[m, :, 1280:1792])
            u = (0.5 * a * (1.0 + gelu_parts(a)) * up).astype(BF16)
            acc[...] += nt(u, w_ref[m, :, 1792:2304])
            return c

        lax.fori_loop(0, bins, m_body, 0)
        source, _ = packed_source(place, b * CAP, (1, CAP), 1)
        drop = (lax.broadcasted_iota(jnp.int32, (seq, CAP), 0) == source).astype(BF16)
        out_ref[...] = (out_ref[...].astype(F32) + nn(drop, acc[...].astype(BF16))).astype(BF16)

    out_ref[...] = jnp.zeros_like(out_ref)

    def others(i, c):
        b = lax.rem(me + 1 + i, bins)
        forward(b)
        ffn_out(b)
        return c

    lax.fori_loop(0, bins, others, 0)

    n1t[...] = n1[...].T
    n2t[...] = n2[...].T
    dypt[...] = dyp[...].T
    lse_t[...] = lse[...].T
    acc[...] = jnp.zeros_like(acc)

    def ffn_back(m, c):
        a = nn(n2[...], w_ref[m, :, 768:1280])
        up = nn(n2[...], w_ref[m, :, 1280:1792])
        t = gelu_parts(a)
        gel = 0.5 * a * (1.0 + t)
        u = (gel * up).astype(BF16)
        du = nn(dyp[...], w_ref[m, :, 1792:2304])
        slope = 0.5 * (1.0 + t) + 0.5 * a * (1.0 - t * t) * (GELU_COEF * (1.0 + 3.0 * GELU_CUBE * a * a))
        da = (du * up * slope).astype(BF16)
        db = (du * gel).astype(BF16)
        g_ref[m, :, 1792:2304] = nn(dypt[...], u).astype(BF16)
        g_ref[m, :, 768:1280] = nn(n2t[...], da).astype(BF16)
        g_ref[m, :, 1280:1792] = nn(n2t[...], db).astype(BF16)
        acc[...] += nt(da, w_ref[m, :, 768:1280]) + nt(db, w_ref[m, :, 1280:1792])
        return c

    lax.fori_loop(0, bins, ffn_back, 0)
    hb = h[...]
    r2 = rms_rows(hb)
    dn2 = acc[...]
    gg_ffn = jnp.sum(dn2 * hb * r2, axis=0, keepdims=True)
    wg = dn2 * g2
    dh = dyp[...].astype(F32) + r2 * wg - hb * (r2 * r2 * r2) * jnp.mean(wg * hb, axis=1, keepdims=True)
    h[...] = dh
    dhb = dh.astype(BF16)
    dhbt[...] = dhb.T
    n2[...] = dhb
    acc[...] = jnp.zeros_like(acc)

    def attn_back(m, c):
        do[m] = nn(n2[...], wo[m]).astype(BF16)
        attend_group_back(qkv, m, bias, lse_t, do, m, dqkv)
        acc[...] += nt(dqkv[m], w_ref[m, :, 0:768])
        grad = nn(n1t[...], dqkv[m])
        go = nn(dhbt[...], o_all[m])
        lanes = low_lanes()
        for t in range(6):
            g = grad[:, 128 * t : 128 * (t + 1)]
            if t == 1:
                g = jnp.where(lanes, g, pltpu.roll(go[:, 0:128], 64, 1))
            elif t == 3:
                g = jnp.where(lanes, g, go[:, 0:128])
            elif t == 5:
                g = jnp.where(lanes, g, pltpu.roll(go[:, 128:256], 64, 1))
            g_ref[m, :, 128 * t : 128 * (t + 1)] = g.astype(BF16)
        return c

    lax.fori_loop(0, bins, attn_back, 0)
    xb = xp[...].astype(F32)
    r1 = rms_rows(xb)
    dn1 = acc[...]
    gg_attn = jnp.sum(dn1 * xb * r1, axis=0, keepdims=True)
    wa = dn1 * g1
    gt = h[...] + r1 * wa - xb * (r1 * r1 * r1) * jnp.mean(wa * xb, axis=1, keepdims=True)
    gt_ref[...] = gt.astype(BF16)
    gg_ref[0:1, :] = gg_attn
    gg_ref[1:2, :] = gg_ffn


def unpack_kernel(len_ref, gt_ref, out_ref):
    bins = gt_ref.shape[0]
    seq = out_ref.shape[0]
    place = placement(len_ref, bins)
    total = jnp.zeros(out_ref.shape, F32)
    for b in range(bins):
        source, _ = packed_source(place, b * CAP, (1, CAP), 1)
        drop = (lax.broadcasted_iota(jnp.int32, (seq, CAP), 0) == source).astype(BF16)
        total = total + nn(drop, gt_ref[b])
    out_ref[...] = total


def per_device(
    tokens, lengths, query_weight, key_weight, value_weight, out_weight, attn_gain, gate_weight, up_weight, down_weight,
    ffn_gain, cotangent,
):
    rows, seq, width = tokens.shape
    bins = lax.axis_size("mp")
    q, k, v, o = (w.astype(BF16) for w in (query_weight, key_weight, value_weight, out_weight.T))
    package = jnp.concatenate(
        [q, o[:, 0:64], k, o[:, 64:128], v, o[:, 128:192], gate_weight.astype(BF16), up_weight.astype(BF16),
         down_weight.T.astype(BF16)], axis=1)
    w = lax.all_gather(lax.all_gather(package, "dp", axis=0, tiled=True), "mp", axis=0)
    gains = jnp.stack([attn_gain, ffn_gain]).astype(BF16)
    gains = lax.all_gather(gains, "dp", axis=1, tiled=True).astype(F32)
    gains = jnp.concatenate([gains, jnp.zeros((6, width), F32)], axis=0)
    which = lax.axis_index("mp").astype(jnp.int32).reshape(1)
    vmem = pl.BlockSpec(memory_space=pltpu.VMEM)
    smem = pl.BlockSpec(memory_space=pltpu.SMEM)
    group = w.shape[2]
    x = tokens.reshape(seq, width)
    dy = cotangent.reshape(seq, width)
    out, gt, g, gg = pl.pallas_call(
        layer_kernel,
        out_shape=(
            jax.ShapeDtypeStruct((seq, width), BF16),
            jax.ShapeDtypeStruct((CAP, width), BF16),
            jax.ShapeDtypeStruct((bins, width, group), BF16),
            jax.ShapeDtypeStruct((8, width), F32),
        ),
        in_specs=[smem, vmem, vmem, vmem, vmem, smem],
        out_specs=[vmem] * 4,
        scratch_shapes=[
            pltpu.VMEM((CAP, CAP), F32),
            pltpu.VMEM((CAP, width), BF16),
            pltpu.VMEM((CAP, width), BF16),
            pltpu.VMEM((CAP, width), BF16),
            pltpu.VMEM((width, CAP), BF16),
            pltpu.VMEM((CAP, width), BF16),
            pltpu.VMEM((width, CAP), BF16),
            pltpu.VMEM((width, CAP), BF16),
            pltpu.VMEM((width, CAP), BF16),
            pltpu.VMEM((bins, CAP, width), BF16),
            pltpu.VMEM((bins, CAP, 256), BF16),
            pltpu.VMEM((bins, width, 256), BF16),
            pltpu.VMEM((CAP, 128), F32),
            pltpu.VMEM((128, CAP), F32),
            pltpu.VMEM((bins, CAP, 256), BF16),
            pltpu.VMEM((bins, CAP, width), BF16),
            pltpu.VMEM((CAP, width), F32),
            pltpu.VMEM((CAP, width), F32),
        ],
        compiler_params=pltpu.CompilerParams(vmem_limit_bytes=63 * 2**20+900000),
        name="layer",
    )(lengths, x, dy, w, gains, which)
    gt_all = lax.all_gather(gt, "mp", axis=0)
    grad_tokens = pl.pallas_call(
        unpack_kernel,
        out_shape=jax.ShapeDtypeStruct((seq, width), F32),
        in_specs=[smem, vmem],
        out_specs=vmem,
        compiler_params=pltpu.CompilerParams(vmem_limit_bytes=60 * 2**20),
        name="unpack",
    )(lengths, gt_all)
    g = lax.psum_scatter(g, "mp", scatter_dimension=0, tiled=False)
    g = lax.psum_scatter(g, "dp", scatter_dimension=0, tiled=True).astype(F32)
    gg = lax.psum_scatter(lax.psum(gg[0:2], "mp"), "dp", scatter_dimension=1, tiled=True)
    go = jnp.concatenate([g[:, 192:256], g[:, 448:512], g[:, 704:768]], axis=1).T
    return (
        out.reshape(rows, seq, width),
        grad_tokens.reshape(rows, seq, width),
        g[:, 0:192],
        g[:, 256:448],
        g[:, 512:704],
        go,
        gg[0],
        g[:, 768:1280],
        g[:, 1280:1792],
        g[:, 1792:2304].T,
        gg[1],
    )


MESH = pl.DeviceIdType.MESH
PARTS = ((0, 768), (768, 2304))


class Net:
    def __init__(self):
        self.dp = lax.axis_index("dp")
        self.z = lax.axis_index("mp")
        self.core = lax.rem(self.dp, 2)
        self.chip = lax.div(self.dp, 2)
        self.chip_x = self.chip + 1 - 2 * lax.rem(self.chip, 2)
        self.chip_y = lax.rem(self.chip + 2, 4)
        self.chip_d = 3 - self.chip
        self.sibling = (2 * self.chip + 1 - self.core, self.z)
        self.x = (2 * self.chip_x + self.core, self.z)
        self.y = (2 * self.chip_y + self.core, self.z)

    def up(self, k):
        return (self.dp, lax.rem(self.z + k, 4))

    def along(self, step):
        return (self.dp, lax.rem(self.z + 4 + step, 4))

    def group(self, i):
        z = self.z
        one = jnp.where(z == 0, 1, jnp.where(z == 1, 0, jnp.where(z == 2, 3, 2)))
        two = jnp.where(z < 2, 2, 1)
        return jnp.where(i == 0, z, jnp.where(i == 1, one, jnp.where(i == 2, two, 6 - z - one - two)))


class Gather:
    def __init__(self, net, w, send, recv):
        self.net, self.w, self.send, self.recv = net, w, send, recv

    def copy(self, part, m, chip, core, kind, to, rows=None):
        lo, hi = PARTS[part]
        first, last, mark = (0, 96, 0) if rows is None else (48 * rows, 48 * (rows + 1), 1 + rows)
        ref = self.w.at[m, chip, core, first:last, lo:hi]
        return pltpu.make_async_remote_copy(
            src_ref=ref, dst_ref=ref, send_sem=self.send.at[part, m, chip, kind],
            recv_sem=self.recv.at[part, m, chip, core, mark], device_id=to, device_id_type=MESH)

    def wait(self, part, m, chip, core, rows=None):
        self.copy(part, m, chip, core, 0, self.net.sibling, rows).wait_recv()

    def each_along_z(self, part, m, act):
        net = self.net

        @pl.when(jnp.logical_and(m <= net.z, net.z < 3))
        def _():
            act(self.copy(part, m, net.chip, net.core, 3, net.along(1)))

        @pl.when(jnp.logical_and(m >= net.z, net.z > 0))
        def _():
            act(self.copy(part, m, net.chip, net.core, 4, net.along(-1)))

    def own_copies(self, part, m):
        net = self.net
        return [self.copy(part, m, net.chip, net.core, k, to) for k, to in enumerate((net.x, net.y, net.sibling))]

    def relay_copies(self, part, m):
        net = self.net
        return [
            self.copy(part, m, net.chip_x, net.core, 0, net.y, 0), self.copy(part, m, net.chip_x, net.core, 2, net.sibling),
            self.copy(part, m, net.chip_y, net.core, 1, net.x, 1), self.copy(part, m, net.chip_y, net.core, 2, net.sibling)]

    def along_z(self, part, i):
        net = self.net
        m = net.group(i)
        if not isinstance(i, int) or i > 0:
            self.wait(part, m, net.chip, net.core)
        self.each_along_z(part, m, lambda copy: copy.start())

    def sideways(self, part, i):
        for copy in self.own_copies(part, self.net.group(i)):
            copy.start()

    def spread(self, part, i):
        self.along_z(part, i)
        self.sideways(part, i)

    def relay(self, part, i):
        net = self.net
        m = net.group(i)
        copies = self.relay_copies(part, m)
        for j, chip in enumerate((net.chip_x, net.chip_y)):
            self.wait(part, m, chip, net.core)
            copies[2 * j].start()
            copies[2 * j + 1].start()

    def across(self, part, i):
        net = self.net
        m = net.group(i)
        self.wait(part, m, net.chip_d, net.core, 0)
        self.wait(part, m, net.chip_d, net.core, 1)
        self.copy(part, m, net.chip_d, net.core, 2, net.sibling).start()

    def complete(self, part, i):
        net = self.net
        m = net.group(i)
        for chip in range(4):
            self.wait(part, m, chip, 1 - net.core)

    def drain(self):
        net = self.net
        for part in range(2):

            def body(m, c, part=part):
                self.each_along_z(part, m, lambda copy: copy.wait_send())
                for copy in self.own_copies(part, m) + self.relay_copies(part, m):
                    copy.wait_send()
                self.copy(part, m, net.chip_d, net.core, 2, net.sibling).wait_send()
                return c

            lax.fori_loop(0, 4, body, 0)


class Reduce:
    def __init__(self, net, g, slots, zbuf, sems, ok):
        self.net, self.g, self.slots, self.zbuf, self.sems, self.ok = net, g, slots, zbuf, sems, ok

    def lanes(self, part):
        return slice(*PARTS[part])

    def unit(self, part, m, chip, core, rows=slice(0, 96)):
        return self.g.at[m, chip, core, rows, self.lanes(part)]

    def copy(self, kind, part, key, src, dst, to):
        return pltpu.make_async_remote_copy(
            src_ref=src, dst_ref=dst, send_sem=self.sems.at[0, kind, part, key], recv_sem=self.sems.at[1, kind, part, key],
            device_id=to, device_id_type=MESH)

    def core_copy(self, part, i):
        m = self.net.group(i)
        lo, hi = PARTS[part]
        return self.copy(
            0, part, m, self.g.at[m, :, 1 - self.net.core, :, lo:hi],
            self.slots.at[lax.rem(i, 2), :, :, 0 : hi - lo], self.net.sibling)

    def to_core(self, part, i, credit):
        if credit:
            pl.semaphore_wait(self.ok.at[3, part, self.net.group(i)], 1)
        self.core_copy(part, i).start()

    def from_core(self, part, i, credit):
        net = self.net
        m = net.group(i)
        lo, hi = PARTS[part]
        copy = self.core_copy(part, i)
        copy.wait_recv()
        slot = lax.rem(i, 2)
        for chip in range(4):
            self.g[m, chip, net.core, :, lo:hi] = self.g[m, chip, net.core, :, lo:hi] + self.slots[slot, chip, :, 0 : hi - lo]
        if credit is not None:
            p, j = credit
            pl.semaphore_signal(self.ok.at[3, p, net.group(j)], inc=1, device_id=net.sibling, device_id_type=MESH)
        copy.wait_send()
        pl.semaphore_signal(self.ok.at[0, part, m], inc=1, device_id=net.x, device_id_type=MESH)
        pl.semaphore_signal(self.ok.at[1, part, m], inc=1, device_id=net.y, device_id_type=MESH)

        @pl.when(jnp.logical_and(m >= net.z, net.z > 0))
        def _():
            pl.semaphore_signal(self.ok.at[2, part, m], inc=1, device_id=net.along(-1), device_id_type=MESH)

        @pl.when(jnp.logical_and(m <= net.z, net.z < 3))
        def _():
            pl.semaphore_signal(self.ok.at[2, part, m], inc=1, device_id=net.along(1), device_id_type=MESH)

    def across_copies(self, part, m):
        net = self.net
        out = []
        for kind, rows, to in ((1, slice(0, 48), net.y), (2, slice(48, 96), net.x)):
            out.append(self.copy(
                kind, part, m, self.unit(part, m, net.chip_d, net.core, rows),
                self.unit(part, m, 0, 1 - net.core, rows), to))
        return out

    def side_copies(self, part, m):
        net = self.net
        return [
            self.copy(kind, part, m, self.unit(part, m, chip, net.core), self.unit(part, m, slot, 1 - net.core), to)
            for kind, chip, slot, to in ((3, net.chip_x, 1, net.x), (4, net.chip_y, 2, net.y))]

    def each_z(self, part, m, act):
        net = self.net
        z = net.z
        src = self.unit(part, m, net.chip, net.core)
        far = self.unit(part, m, 3, 1 - net.core)
        lo, hi = PARTS[part]
        near = self.zbuf.at[:, lo:hi]

        def copy(dst, kind, step):
            return pltpu.make_async_remote_copy(
                src_ref=src, dst_ref=dst, send_sem=self.sems.at[0, 5, part, m], recv_sem=self.sems.at[1, kind, part, m],
                device_id=net.along(step), device_id_type=MESH)

        for test, dst, kind, step in ((m > z, far, 5, 1), (m < z - 1, far, 5, -1), (m == z - 1, near, 6, -1)):

            @pl.when(test)
            def _(dst=dst, kind=kind, step=step):
                act(copy(dst, kind, step))

    def z_arrived(self, part, m, near):
        net = self.net
        lo, hi = PARTS[part]
        ref = self.zbuf.at[:, lo:hi] if near else self.unit(part, m, 3, 1 - net.core)
        pltpu.make_async_remote_copy(
            src_ref=ref, dst_ref=ref, send_sem=self.sems.at[0, 5, part, m],
            recv_sem=self.sems.at[1, 6 if near else 5, part, m], device_id=net.sibling, device_id_type=MESH).wait_recv()
        if near:
            mine = self.g[m, net.chip, net.core, :, lo:hi]
            self.g[m, net.chip, net.core, :, lo:hi] = mine + self.zbuf[:, lo:hi]
        else:
            self.add(part, m, net.chip, 3)

    def add(self, part, m, chip, slot, rows=slice(0, 96)):
        net = self.net
        lanes = self.lanes(part)
        self.g[m, chip, net.core, rows, lanes] = self.g[m, chip, net.core, rows, lanes] + self.g[m, slot, 1 - net.core, rows, lanes]

    def start_across(self, part, i):
        m = self.net.group(i)
        pl.semaphore_wait(self.ok.at[0, part, m], 1)
        pl.semaphore_wait(self.ok.at[1, part, m], 1)
        for copy in self.across_copies(part, m):
            copy.start()

    def start_sides(self, part, i):
        net = self.net
        m = net.group(i)
        by_y, by_x = self.across_copies(part, m)
        by_y.wait_recv()
        self.add(part, m, net.chip_x, 0, slice(0, 48))
        by_x.wait_recv()
        self.add(part, m, net.chip_y, 0, slice(48, 96))
        for copy in self.side_copies(part, m):
            copy.start()

    def gather_sides(self, part, i):
        net = self.net
        m = net.group(i)
        for slot, copy in zip((1, 2), self.side_copies(part, m)):
            copy.wait_recv()
            self.add(part, m, net.chip, slot)

    def send_z(self, part, m):
        pl.semaphore_wait(self.ok.at[2, part, m], 1)
        self.each_z(part, m, lambda copy: copy.start())

    def pass_z(self, part, m):
        self.z_arrived(part, m, False)
        self.send_z(part, m)

    def wave(self, part, n):
        z = self.net.z
        for at, groups, act in (
            ((0, (3, 2, 1), self.send_z), (3, (0, 1, 2), self.send_z)),
            ((1, (3, 2), self.pass_z), (2, (0, 1), self.pass_z)),
            ((1, (0,), self.pass_z), (2, (3,), self.pass_z)),
        )[n]:

            @pl.when(z == at)
            def _(groups=groups, act=act):
                for m in groups:
                    act(part, m)

    def step(self, n):
        if n > 0:
            self.start_sides(1 if n < 5 else 0, (n - 1) % 4)
        if n < 8:
            self.start_across(1 if n < 4 else 0, n % 4)

    def total(self, part):
        net = self.net

        @pl.when(net.z > 0)
        def _():
            self.z_arrived(part, net.z, False)

        @pl.when(net.z < 3)
        def _():
            self.z_arrived(part, net.z, True)

        return self.g[net.z, net.chip, net.core, :, self.lanes(part)].astype(F32)

    def drain(self):
        net = self.net
        for part in range(2):

            def body(m, c, part=part):
                for copy in self.across_copies(part, m) + self.side_copies(part, m):
                    copy.wait_send()
                self.each_z(part, m, lambda copy: copy.wait_send())
                return c

            lax.fori_loop(0, 4, body, 0)


def greet(net):
    barrier = pltpu.get_barrier_semaphore()
    for other in range(1, 8):
        pl.semaphore_signal(barrier, inc=1, device_id=(lax.rem(net.dp + other, 8), net.z), device_id_type=MESH)
    for k in range(1, 4):
        pl.semaphore_signal(barrier, inc=1, device_id=net.up(k), device_id_type=MESH)
    return barrier


def share_gains(net, parts, send, recv):
    copies = []
    for k in range(1, 8):
        copies.append(pltpu.make_async_remote_copy(
            src_ref=parts.at[net.dp], dst_ref=parts.at[net.dp], send_sem=send.at[k - 1], recv_sem=recv.at[net.dp],
            device_id=(lax.rem(net.dp + k, 8), net.z), device_id_type=MESH))
        copies[-1].start()
    return copies


def join_gains(net, parts, send, recv, gain):
    for k in range(1, 8):
        other = lax.rem(net.dp + k, 8)
        pltpu.make_async_remote_copy(
            src_ref=parts.at[other], dst_ref=parts.at[other], send_sem=send.at[k - 1], recv_sem=recv.at[other],
            device_id=net.sibling, device_id_type=MESH).wait_recv()
    total = jnp.zeros(gain.shape, F32)
    for d in range(8):
        piece = jnp.concatenate([parts[d], jnp.zeros((8, gain.shape[1] - 128), F32)], axis=1)
        total = total + pltpu.roll(piece, 96 * d, 1)
    gain[...] = total


def build_package(w, net, q_ref, k_ref, v_ref, o_ref, g_ref, u_ref, d_ref):
    lanes = low_lanes()
    ot = o_ref[...].T
    pad = jnp.zeros((96, 64), F32)
    at = (net.z, net.chip, net.core)

    def put(tile, value):
        w[at[0], at[1], at[2], :, 128 * tile : 128 * (tile + 1)] = value.astype(BF16)

    for j, ref in enumerate((q_ref, k_ref, v_ref)):
        put(2 * j, ref[:, 0:128])
        last = jnp.concatenate([ref[:, 128:192], pad], axis=1)
        extra = jnp.concatenate([ot[:, 64 * j : 64 * (j + 1)], pad], axis=1)
        put(2 * j + 1, jnp.where(lanes, last, pltpu.roll(extra, 64, 1)))
    w[at[0], at[1], at[2], :, 768:1280] = g_ref[...].astype(BF16)
    w[at[0], at[1], at[2], :, 1280:1792] = u_ref[...].astype(BF16)
    w[at[0], at[1], at[2], :, 1792:2304] = d_ref[...].astype(BF16)


def rows768(ref, m, lo, hi):
    return ref[m, :, :, :, lo:hi].reshape(768, hi - lo)


def put768(ref, m, lo, hi, value):
    ref[m, :, :, :, lo:hi] = value.reshape(4, 2, 96, hi - lo)


class RowGather:
    def __init__(self, net, pool, send, recv, ok):
        self.net, self.pool, self.send, self.recv, self.ok = net, pool, send, recv, ok

    def copy(self, m, way):
        net = self.net
        return pltpu.make_async_remote_copy(
            src_ref=self.pool.at[m], dst_ref=self.pool.at[m], send_sem=self.send.at[way, m], recv_sem=self.recv.at[m],
            device_id=net.along(1 - 2 * way), device_id_type=MESH)

    def each(self, m, act):
        net = self.net

        @pl.when(jnp.logical_and(m <= net.z, net.z < 3))
        def _():
            act(self.copy(m, 0))

        @pl.when(jnp.logical_and(m >= net.z, net.z > 0))
        def _():
            act(self.copy(m, 1))

    def start(self):
        net = self.net
        if self.ok is not None:
            for test, way in ((net.z < 3, 0), (net.z > 0, 1)):

                @pl.when(test)
                def _(way=way):
                    pl.semaphore_signal(self.ok.at[1 - way], inc=1, device_id=net.along(1 - 2 * way), device_id_type=MESH)

        for test, way in ((net.z < 3, 0), (net.z > 0, 1)):

            @pl.when(test)
            def _(way=way):
                if self.ok is not None:
                    pl.semaphore_wait(self.ok.at[way], 1)
                self.copy(net.z, way).start()

    def relay(self, i):
        z = self.net.z
        m = self.net.group(i)

        @pl.when(jnp.logical_and(z > 0, z < 3))
        def _():
            self.copy(m, 0).wait_recv()
            self.each(m, lambda copy: copy.start())

    def arrived(self, i):
        z = self.net.z
        m = self.net.group(i)

        @pl.when(jnp.logical_or(z == 0, z == 3))
        def _():
            self.copy(m, 0).wait_recv()

        return m

    def drain(self):
        def body(m, c):
            self.each(m, lambda copy: copy.wait_send())
            return c

        lax.fori_loop(0, 4, body, 0)


def mega_kernel(
    len_ref, x_ref, dy_ref, q_ref, k_ref, v_ref, o_ref, gate_ref, up_ref, down_ref, ga_ref, gf_ref,
    out_ref, gt_ref, gq_ref, gk_ref, gv_ref, go_ref, gate_grad_ref, up_grad_ref, down_grad_ref, gga_ref, ggf_ref,
    w, g, slots, pool, gain, gain_parts, gg_out, gg_in, gg_z, bias, n1t, n2t, dypt, spare, qkv, hx, o_own, wo, lse, lse_t,
    h, acc, res, zbuf,
    ag_send, ag_recv, gn_send, gn_recv, in_sem, rs_sems, ok, gt_send, gt_recv, gt_ok, hx_send, hx_recv, out_sem, gs_send,
    gs_recv, gz_send, gz_recv,
):
    net = Net()
    bins = 4
    seq = 1536
    me = net.z
    xp, dyp, n1, n2 = (pool.at[j] for j in range(4))
    n_b = spare.at[0]
    barrier = greet(net)
    halves = []
    for t, ref in enumerate((x_ref, dy_ref)):
        for j in range(2):
            halves.append(pltpu.make_async_copy(
                ref.at[j], g.at[t, :, :, :, 768 * j : 768 * (j + 1)], in_sem.at[2 * t + j]))
    for copy in halves:
        copy.start()
    ag = Gather(net, w, ag_send, ag_recv)
    rs = Reduce(net, g, slots, zbuf, rs_sems, ok)
    rows = RowGather(net, pool, gt_send, gt_recv, gt_ok)
    mids = RowGather(net, hx, hx_send, hx_recv, None)
    build_package(w, net, q_ref, k_ref, v_ref, o_ref, gate_ref, up_ref, down_ref)
    pad = jnp.zeros((1, 32), F32)
    mine = jnp.concatenate([
        jnp.concatenate([ga_ref[...], pad], axis=1), jnp.concatenate([gf_ref[...], pad], axis=1),
        jnp.zeros((6, 128), F32)], axis=0)
    gain_parts[net.dp] = mine.astype(BF16).astype(F32)
    pl.semaphore_wait(barrier, 10)
    gain_copies = share_gains(net, gain_parts, gn_send, gn_recv)
    ag.spread(0, 0)

    place = placement(len_ref, bins)
    lse[...] = jnp.zeros_like(lse)

    def set_bias(b):
        _, segment = packed_source(place, b * CAP, (CAP, 1), 0)
        _, segment_row = packed_source(place, b * CAP, (1, CAP), 1)
        bias[...] = jnp.where(segment == segment_row, 0.0, NEG)

    def pack(b, t, store):
        def body(j, c):
            source, _ = packed_source(place, b * CAP + j * 128, (128, 1), 0)
            pick = (source == lax.broadcasted_iota(jnp.int32, (128, seq), 1)).astype(BF16)
            value = nn(pick[:, 0:768], rows768(g, t, 0, 768)) + nn(pick[:, 768:1536], rows768(g, t, 768, 1536))
            store(pl.ds(pl.multiple_of(j * 128, 128), 128), value)
            return c

        lax.fori_loop(0, CAP // 128, body, 0)

    def drops(b, first, rows, count=1):
        source, _ = packed_source(place, b * CAP, (1, count * CAP), 1)
        return (lax.broadcasted_iota(jnp.int32, (rows, count * CAP), 0) + first == source).astype(BF16)

    def norm(src, dst, gain_row):
        def body(j, c):
            at = pl.ds(pl.multiple_of(j * 128, 128), 128)
            values = src[at, :]
            dst[at, :] = (values * rms_rows(values) * gain_row).astype(BF16)
            return c

        lax.fori_loop(0, CAP // 128, body, 0)

    for copy in halves:
        copy.wait()
    def store_x(at, value):
        xp[at, :] = value.astype(BF16)
        h[at, :] = value

    def store_dy(at, value):
        dyp[at, :] = value.astype(BF16)

    pack(me, 0, store_x)
    ag.spread(0, 1)
    ag.relay(0, 0)
    pack(me, 1, store_dy)
    join_gains(net, gain_parts, gn_send, gn_recv, gain)
    g1 = gain[0:1, :]
    g2 = gain[1:2, :]
    ag.spread(0, 2)
    ag.relay(0, 1)
    ag.across(0, 0)
    norm(h, n1, g1)
    n1t[...] = n1[...].T
    dypt[...] = dyp[...].T

    set_bias(me)
    ag.spread(0, 3)
    ag.relay(0, 2)
    ag.across(0, 1)
    ag.along_z(1, 0)
    ag.relay(0, 3)
    ag.across(0, 2)
    ag.sideways(1, 0)
    ag.across(0, 3)
    ag.along_z(1, 1)
    ag.sideways(1, 1)

    def own_forward(i, c):
        m = net.group(i)
        ag.complete(0, i)
        first, second = out_weight_tiles_at(w, m)
        wo[m, :, 0:128] = first
        wo[m, :, 128:256] = second
        qkv[m] = nn(n1[...], rows768(w, m, 0, 768)).astype(BF16)
        attend_group(qkv, m, bias, o_own, m, lse)
        h[...] += nt(o_own[m], wo[m])

        @pl.when(i == 0)
        def _():
            ag.along_z(1, 2)

        @pl.when(i == 1)
        def _():
            ag.relay(1, 0)
            ag.sideways(1, 2)

        @pl.when(i == 3)
        def _():
            ag.along_z(1, 3)
            ag.relay(1, 1)
            ag.across(1, 0)
            ag.sideways(1, 3)

        return c

    lax.fori_loop(0, 4, own_forward, 0)
    hx[me] = h[...].astype(BF16)
    mids.start()
    norm(h, n2, g2)
    n2t[...] = n2[...].T
    lse_t[...] = lse[...].T[0:16, :]
    acc[...] = jnp.zeros_like(acc)
    res[...] = h[...]

    def ffn_back(i, c):
        @pl.when(i == 1)
        def _():
            ag.relay(1, 2)
            ag.across(1, 1)

        @pl.when(i == 2)
        def _():
            ag.relay(1, 3)
            ag.across(1, 2)
            mids.relay(1)
            mids.relay(2)

        @pl.when(i == 3)
        def _():
            ag.across(1, 3)
            rs.step(0)

        m = net.group(i)
        ag.complete(1, i)

        @pl.when(i == 3)
        def _():
            rs.step(1)

        for lo in (0, 256):
            w_gate = rows768(w, m, 768 + lo, 1024 + lo)
            w_up = rows768(w, m, 1280 + lo, 1536 + lo)
            w_down = rows768(w, m, 1792 + lo, 2048 + lo)
            a = nn(n2[...], w_gate)
            up = nn(n2[...], w_up)
            t = gelu_parts(a)
            gel = 0.5 * a * (1.0 + t)
            u = (gel * up).astype(BF16)
            res[...] += nt(u, w_down)
            put768(g, m, 1792 + lo, 2048 + lo, nn(dypt[...], u).astype(BF16))
            du = nn(dyp[...], w_down)
            slope = 0.5 * (1.0 + t) + 0.5 * a * (1.0 - t * t) * (GELU_COEF * (1.0 + 3.0 * GELU_CUBE * a * a))
            da = (du * up * slope).astype(BF16)
            db = (du * gel).astype(BF16)
            put768(g, m, 768 + lo, 1024 + lo, nn(n2t[...], da).astype(BF16))
            put768(g, m, 1280 + lo, 1536 + lo, nn(n2t[...], db).astype(BF16))
            acc[...] += nt(da, w_gate) + nt(db, w_up)

        @pl.when(i < 2)
        def _():
            rs.to_core(1, i, False)

        @pl.when(i >= 2)
        def _():
            rs.to_core(1, i, True)

        @pl.when(jnp.logical_and(i >= 1, i < 3))
        def _():
            rs.from_core(1, i - 1, (1, i + 1))

        @pl.when(i == 3)
        def _():
            rs.from_core(1, 2, (0, 0))

        return c

    lax.fori_loop(0, 4, ffn_back, 0)

    def hidden_back(j, total):
        at = pl.ds(pl.multiple_of(j * 128, 128), 128)
        ho = h[at, :]
        r2 = rms_rows(ho)
        dn2 = acc[at, :]
        wg = dn2 * g2
        dh = dyp[at, :].astype(F32) + r2 * wg - ho * (r2 * r2 * r2) * jnp.mean(wg * ho, axis=1, keepdims=True)
        h[at, :] = dh
        n2[at, :] = dh.astype(BF16)
        acc[at, :] = jnp.zeros_like(dh)
        return total + jnp.sum(dn2 * ho * r2, axis=0, keepdims=True)

    gg_ffn = lax.fori_loop(0, CAP // 128, hidden_back, jnp.zeros((1, 768), F32))
    n2t[...] = n2[...].T
    rs.from_core(1, 3, (0, 1))

    def attn_back(i, c):
        m = net.group(i)
        spare[0, :, 0:256] = nn(n2[...], wo[m]).astype(BF16)
        attend_group_back(qkv, m, bias, lse_t, spare, 0, qkv)
        acc[...] += nt(qkv[m], rows768(w, m, 0, 768))

        @pl.when(i == 0)
        def _():
            mids.relay(3)

        @pl.when(i == 0)
        def _():
            rs.step(2)

        @pl.when(i == 3)
        def _():
            rs.step(3)

        @pl.when(i == 2)
        def _():
            rs.gather_sides(1, 0)

        return c

    lax.fori_loop(0, 4, attn_back, 0)

    def input_back(j, total):
        at = pl.ds(pl.multiple_of(j * 128, 128), 128)
        xb = xp[at, :].astype(F32)
        r1 = rms_rows(xb)
        dn1 = acc[at, :]
        wa = dn1 * g1
        gt = h[at, :] + r1 * wa - xb * (r1 * r1 * r1) * jnp.mean(wa * xb, axis=1, keepdims=True)
        n_b[at, :] = gt.astype(BF16)
        return total + jnp.sum(dn1 * xb * r1, axis=0, keepdims=True)

    gg_attn = lax.fori_loop(0, CAP // 128, input_back, jnp.zeros((1, 768), F32))
    pool[me] = n_b[...]
    rows.start()
    gg = jnp.concatenate([gg_attn, gg_ffn, jnp.zeros((6, 768), F32)], axis=0)
    for d in range(8):
        gg_out[d] = pltpu.roll(gg, (768 - 96 * d) % 768, 1)[:, 0:128] if d else gg[:, 0:128]

    def gg_copy(k):
        to = lax.rem(net.dp + k, 8)
        return pltpu.make_async_remote_copy(
            src_ref=gg_out.at[to], dst_ref=gg_in.at[net.dp], send_sem=gs_send.at[k - 1], recv_sem=gs_recv.at[net.dp],
            device_id=(to, net.z), device_id_type=MESH)

    for k in range(1, 8):
        gg_copy(k).start()

    def attn_grads(i, c):
        m = net.group(i)
        go = nn(n2t[...], o_own[m])
        lanes = low_lanes()
        for j in range(3):
            grad = nn(n1t[...], qkv[m, :, 256 * j : 256 * (j + 1)])
            put768(g, m, 256 * j, 256 * j + 128, grad[:, 0:128].astype(BF16))
            if j == 1:
                extra = go[:, 0:128]
            else:
                extra = pltpu.roll(go[:, 64 * j : 64 * j + 128], 64, 1)
            put768(g, m, 256 * j + 128, 256 * (j + 1), jnp.where(lanes, grad[:, 128:256], extra).astype(BF16))

        rs.to_core(0, i, True)

        @pl.when(jnp.logical_and(i >= 1, i < 3))
        def _():
            rs.from_core(0, i - 1, (0, i + 1))

        @pl.when(i == 3)
        def _():
            rs.from_core(0, 2, None)
            rs.gather_sides(1, 1)

        return c

    lax.fori_loop(0, 4, attn_grads, 0)
    rs.from_core(0, 3, None)
    rs.step(4)

    part = gg_out[net.dp]
    for k in range(1, 8):
        other = lax.rem(net.dp + k, 8)
        pltpu.make_async_remote_copy(
            src_ref=gg_out.at[other], dst_ref=gg_in.at[other], send_sem=gs_send.at[k - 1], recv_sem=gs_recv.at[other],
            device_id=net.sibling, device_id_type=MESH).wait_recv()
        part = part + gg_in[other]
    gg_z[me] = part
    gz_copies = [pltpu.make_async_remote_copy(
        src_ref=gg_z.at[me], dst_ref=gg_z.at[me], send_sem=gz_send.at[k - 1], recv_sem=gz_recv.at[me],
        device_id=net.up(k), device_id_type=MESH) for k in range(1, 4)]
    for copy in gz_copies:
        copy.start()

    mids.drain()
    hx[me] = res[...].astype(BF16)

    def ffn_out(j, c):
        b = mids.arrived(j)
        acc[...] = hx[b].astype(F32)
        norm(acc, n_b, g2)

        def ffn(m, c):
            a = nn(n_b[...], rows768(w, m, 768, 1280))
            up = nn(n_b[...], rows768(w, m, 1280, 1792))
            u = (0.5 * a * (1.0 + gelu_parts(a)) * up).astype(BF16)
            acc[...] += nt(u, rows768(w, m, 1792, 2304))

            @pl.when(jnp.logical_and(j == 2, m == 0))
            def _():
                rows.relay(1)
                rows.relay(2)

            @pl.when(jnp.logical_and(j == 1, m == 3))
            def _():
                rs.step(5)
                rs.gather_sides(1, 2)

            @pl.when(jnp.logical_and(j == 2, m == 1))
            def _():
                rs.step(6)
                rs.gather_sides(1, 3)

            @pl.when(jnp.logical_and(j == 3, m == 1))
            def _():
                rs.step(8)

            return c

        lax.fori_loop(0, 4, ffn, 0)
        hx[b] = acc[...].astype(BF16)

        @pl.when(j == 2)
        def _():
            rs.wave(1, 0)
            rs.step(7)

        @pl.when(j == 3)
        def _():
            rows.relay(3)

        return c

    lax.fori_loop(1, 4, ffn_out, 0)
    for i in range(4):
        rs.gather_sides(0, i)
    rs.wave(0, 0)

    def place_out(j, c):
        at = pl.ds(pl.multiple_of(j * 256, 256), 256)
        pick = drops(0, j * 256, 256, 4)
        out_ref[at, :] = nn(pick, hx[...].reshape(4 * CAP, 768)).astype(BF16)
        return c

    lax.fori_loop(0, seq // 256, place_out, 0)
    rs.wave(1, 1)

    def place_rows(bs, first):
        def body(j, c):
            value = nn(drops(bs[0], CAP * j, CAP), pool[bs[0]])
            for b in bs[1:]:
                value = value + nn(drops(b, CAP * j, CAP), pool[b])
            if not first:
                value = value + qkv[j].astype(F32)
            qkv[j] = value.astype(BF16)
            return c

        lax.fori_loop(0, 3, body, 0)

    place_rows([me, rows.arrived(1), rows.arrived(2)], True)
    rs.wave(1, 2)
    rs.wave(0, 1)
    ffn_sum = rs.total(1)
    gate_grad_ref[...] = ffn_sum[:, 0:512]
    up_grad_ref[...] = ffn_sum[:, 512:1024]
    down_grad_ref[...] = ffn_sum[:, 1024:1536]
    rs.wave(0, 2)
    place_rows([rows.arrived(3)], False)
    out = pltpu.make_async_copy(qkv.at[0:3], gt_ref, out_sem)
    out.start()

    for k in range(1, 4):
        other = lax.rem(me + k, 4)
        pltpu.make_async_remote_copy(
            src_ref=gg_z.at[other], dst_ref=gg_z.at[other], send_sem=gz_send.at[k - 1], recv_sem=gz_recv.at[other],
            device_id=net.up(k), device_id_type=MESH).wait_recv()
        part = part + gg_z[other]
    gga_ref[...] = part[0:1, 0:96]
    ggf_ref[...] = part[1:2, 0:96]
    attn_sum = rs.total(0)
    gq_ref[...] = attn_sum[:, 0:192]
    gk_ref[...] = attn_sum[:, 256:448]
    gv_ref[...] = attn_sum[:, 512:704]
    go_ref[...] = jnp.concatenate([attn_sum[:, 192:256], attn_sum[:, 448:512], attn_sum[:, 704:768]], axis=1).T
    out.wait()
    for copy in gain_copies + gz_copies:
        copy.wait_send()
    for k in range(1, 8):
        gg_copy(k).wait_send()
    rows.drain()
    rs.drain()
    ag.drain()


def finish_kernel(*refs):
    count = len(refs) // 2
    refs[count][...] = refs[0][...].astype(F32)
    refs[count + 1][...] = refs[1][...]

    @pl.when(pl.program_id(0) == 0)
    def _():
        for j in range(2, count):
            refs[count + j][...] = refs[j][...]


def out_weight_tiles_at(w, m):
    lanes = low_lanes()
    t1 = rows768(w, m, 128, 256).astype(F32)
    t3 = rows768(w, m, 384, 512).astype(F32)
    t5 = rows768(w, m, 640, 768).astype(F32)
    first = jnp.where(lanes, pltpu.roll(t1, 64, 1), t3)
    second = jnp.where(lanes, pltpu.roll(t5, 64, 1), 0.0)
    return first.astype(BF16), second.astype(BF16)


def on_this_slice(
    tokens, lengths, query_weight, key_weight, value_weight, out_weight, attn_gain, gate_weight, up_weight, down_weight,
    ffn_gain, cotangent,
):
    rows, seq, width = tokens.shape
    vmem = pl.BlockSpec(memory_space=pltpu.VMEM)
    smem = pl.BlockSpec(memory_space=pltpu.SMEM)
    dma = pltpu.SemaphoreType.DMA
    act = pltpu.VMEM((CAP, width), BF16)
    act_t = pltpu.VMEM((width, CAP), BF16)
    wide = pltpu.VMEM((CAP, width), F32)
    hbm = pl.BlockSpec(memory_space=pl.ANY)

    def f32(*shape):
        return jax.ShapeDtypeStruct(shape, F32)

    out, gt, gq, gk, gv, go, gate, up, down, gain_a, gain_f = pl.pallas_call(
        mega_kernel,
        out_shape=(
            jax.ShapeDtypeStruct((seq, width), BF16), jax.ShapeDtypeStruct((3, CAP, width), BF16),
            f32(96, 192), f32(96, 192), f32(96, 192), f32(192, 96), f32(96, 512), f32(96, 512), f32(96, 512), f32(1, 96), f32(1, 96),
        ),
        in_specs=[smem, hbm, hbm] + [vmem] * 9,
        out_specs=[vmem, hbm] + [vmem] * 9,
        scratch_shapes=[
            pltpu.VMEM((4, 4, 2, 96, 2304), BF16),
            pltpu.VMEM((4, 4, 2, 96, 2304), BF16),
            pltpu.VMEM((2, 4, 96, 1536), BF16),
            pltpu.VMEM((4, CAP, width), BF16),
            pltpu.VMEM((8, width), F32),
            pltpu.VMEM((8, 8, 128), F32), pltpu.VMEM((8, 8, 128), F32), pltpu.VMEM((8, 8, 128), F32),
            pltpu.VMEM((4, 8, 128), F32),
            pltpu.VMEM((CAP, CAP), F32),
            act_t, act_t, act_t, pltpu.VMEM((1, CAP, width), BF16),
            pltpu.VMEM((4, CAP, width), BF16),
            pltpu.VMEM((4, CAP, width), BF16),
            pltpu.VMEM((4, CAP, 256), BF16),
            pltpu.VMEM((4, width, 256), BF16),
            pltpu.VMEM((CAP, 128), F32),
            pltpu.VMEM((16, CAP), F32),
            wide, wide, wide,
            pltpu.VMEM((96, 2304), BF16),
            dma((2, 4, 4, 5)), dma((2, 4, 4, 2, 3)), dma((7,)), dma((8,)), dma((4,)),
            dma((2, 7, 2, 4)), pltpu.SemaphoreType.REGULAR((4, 2, 4)),
            dma((2, 4)), dma((4,)), pltpu.SemaphoreType.REGULAR((2,)), dma((2, 4)), dma((4,)), dma, dma((7,)), dma((8,)), dma((3,)), dma((4,)),
        ],
        compiler_params=pltpu.CompilerParams(
            vmem_limit_bytes=60 * 2**20, collective_id=0, has_side_effects=True),
        name="layer",
    )(lengths, tokens.reshape(2, 4, 2, 96, width), cotangent.reshape(2, 4, 2, 96, width), query_weight, key_weight,
      value_weight, out_weight, gate_weight, up_weight, down_weight.T, attn_gain.reshape(1, 96), ffn_gain.reshape(1, 96))
    rest = (out, gq, gk, gv, go, gate, up, down, gain_a, gain_f)
    block = pl.BlockSpec((512, width), lambda i: (i, 0))
    whole = [pl.BlockSpec(a.shape, lambda i: (0, 0)) for a in rest[1:]]
    gt, out, gq, gk, gv, go, gate, up, down, gain_a, gain_f = pl.pallas_call(
        finish_kernel,
        grid=(seq // 512,),
        out_shape=(f32(seq, width),) + tuple(jax.ShapeDtypeStruct(a.shape, a.dtype) for a in rest),
        in_specs=[block, block] + whole,
        out_specs=(block, block) + tuple(whole),
        name="finish",
    )(gt.reshape(seq, width), *rest)
    return (
        out.reshape(rows, seq, width), gt.reshape(rows, seq, width), gq, gk, gv, go, gain_a.reshape(96), gate, up, down.T,
        gain_f.reshape(96),
    )
def solution(mesh):
    body = on_this_slice if dict(mesh.shape) == {"dp": 8, "mp": 4} else per_device
    return jax.shard_map(
        body,
        mesh=mesh,
        in_specs=(
            P("dp", None, None), P("dp", None), P("dp", "mp"), P("dp", "mp"), P("dp", "mp"), P("mp", "dp"), P("dp"),
            P("dp", "mp"), P("dp", "mp"), P("mp", "dp"), P("dp"), P("dp", None, None),
        ),
        out_specs=(
            P("dp", None, None), P("dp", None, None), P("dp", "mp"), P("dp", "mp"), P("dp", "mp"), P("mp", "dp"),
            P("dp"), P("dp", "mp"), P("dp", "mp"), P("mp", "dp"), P("dp"),
        ),
        check_vma=False,
    )
```

```python
import functools
import jax
import jax.numpy as jnp
from jax import lax
from jax.experimental import pallas as pl
from jax.experimental.pallas import tpu as pltpu
from jax.sharding import PartitionSpec as P

EPSILON = 1e-06
GELU_COEF = 0.7978845608028654
GELU_CUBE = 0.044715
CAP = 512
NEG = -1e30
F32 = jnp.float32
BF16 = jnp.bfloat16


def nn(a, b):
    return lax.dot_general(a, b, (((1,), (0,)), ((), ())), preferred_element_type=F32)


def nt(a, b):
    return lax.dot_general(a, b, (((1,), (1,)), ((), ())), preferred_element_type=F32)


def tn(a, b):
    return lax.dot_general(a, b, (((0,), (0,)), ((), ())), preferred_element_type=F32)


def placement(len_ref, bins):
    count = len_ref.shape[1]
    sizes = [len_ref[0, i] for i in range(count)]
    starts = [jnp.int32(0)]
    for i in range(count - 1):
        starts.append(starts[-1] + sizes[i])
    ranks = []
    for i in range(count):
        rank = jnp.int32(0)
        for j in range(count):
            if j < i:
                rank = rank + jnp.where(sizes[j] >= sizes[i], 1, 0)
            elif j > i:
                rank = rank + jnp.where(sizes[j] > sizes[i], 1, 0)
        ranks.append(rank)
    fills = [jnp.int32(0)] * (bins - 1)
    spots = [jnp.int32(0)] * count
    for k in range(count):
        size = jnp.int32(0)
        for i in range(count):
            size = size + jnp.where(ranks[i] == k, sizes[i], 0)
        if k == 0:
            spot = jnp.int32((bins - 1) * CAP)
        else:
            free = jnp.int32(1)
            spot = jnp.int32(0)
            for b in range(bins - 1):
                fits = jnp.where(fills[b] + size <= CAP, free, 0) if b < bins - 2 else free
                spot = spot + fits * (b * CAP + fills[b])
                fills[b] = fills[b] + fits * size
                free = free - fits
        for i in range(count):
            spots[i] = spots[i] + jnp.where(ranks[i] == k, spot, 0)
    return starts, sizes, spots


def packed_source(place, first, shape, axis):
    spot = lax.broadcasted_iota(jnp.int32, shape, axis) + first
    source = jnp.full(shape, -1, jnp.int32)
    segment = jnp.full(shape, -1, jnp.int32)
    for i, (start, size, at) in enumerate(zip(*place)):
        here = (spot >= at) & (spot < at + size)
        source = jnp.where(here, spot + (start - at), source)
        segment = jnp.where(here, i, segment)
    return source, segment


def low_lanes():
    return lax.broadcasted_iota(jnp.int32, (1, 128), 1) < 64


def half(tile, low):
    lanes = low_lanes()
    return jnp.where(lanes if low else jnp.logical_not(lanes), tile, jnp.zeros_like(tile))


HEADS = ((0, 2, 4, True), (0, 2, 4, False), (1, 3, 5, True))


def tile_of(ref, m, t, rows=slice(None)):
    return ref[m, rows, 128 * t : 128 * (t + 1)]


def attend_group(qkv, m, bias, o_ref, at, lse_ref=None, qb=256):
    for i in range(CAP // qb):
        rows = slice(i * qb, (i + 1) * qb)
        scores = []
        for tq, tk, tv, low in HEADS:
            q = half(tile_of(qkv, m, tq, rows), low) * jnp.asarray(0.125, BF16)
            scores.append(nt(q, tile_of(qkv, m, tk)))
        shares, totals = [], []
        for head, s in enumerate(scores):
            s = s + bias[rows, :]
            top = jnp.max(s, axis=1, keepdims=True)
            e = jnp.exp(s - top)
            total = jnp.sum(e, axis=1, keepdims=True)
            shares.append(e.astype(BF16))
            totals.append(total)
            if lse_ref is not None:
                lane = lax.broadcasted_iota(jnp.int32, (1, 128), 1)
                lse_ref[rows, :] = jnp.where(lane == 3 * m + head, top + jnp.log(total), lse_ref[rows, :])
        parts = []
        for (tq, tk, tv, low), e, total in zip(HEADS, shares, totals):
            parts.append(nn(e, half(tile_of(qkv, m, tv), low)) * (1.0 / total))
        o_ref[at, rows, 0:128] = (parts[0] + parts[1]).astype(BF16)
        o_ref[at, rows, 128:256] = parts[2].astype(BF16)


def attend_group_back(qkv, m, bias, lse_t, do_ref, at, dqkv):
    dk = [None, None]
    dv = [None, None]
    dq = [None, None]
    scale = jnp.asarray(0.125, BF16)
    for head, (tq, tk, tv, low) in enumerate(HEADS):
        j = 0 if head < 2 else 1
        k = half(tile_of(qkv, m, tk), low) * scale
        s = nt(k, tile_of(qkv, m, tq))
        do = do_ref[at, :, 128 * j : 128 * (j + 1)]
        dp = nt(half(tile_of(qkv, m, tv), low), do)
        p = jnp.exp(s + bias[...] - lse_t[pl.ds(3 * m + head, 1), :])
        delta = jnp.sum(p * dp, axis=0, keepdims=True)
        ds = (p * (dp - delta)).astype(BF16)
        parts = (
            nn(p.astype(BF16), half(do, low)), nn(ds, half(tile_of(qkv, m, tq), low) * scale), tn(ds, k))
        for total, part in zip((dv, dk, dq), parts):
            total[j] = part if total[j] is None else total[j] + part
    for j in range(2):
        for t, total in ((0, dq), (2, dk), (4, dv)):
            dqkv[m, :, 128 * (t + j) : 128 * (t + j + 1)] = total[j].astype(BF16)


def out_weight_tiles(w, m):
    lanes = low_lanes()
    t1 = tile_of(w, m, 1).astype(F32)
    t3 = tile_of(w, m, 3).astype(F32)
    t5 = tile_of(w, m, 5).astype(F32)
    first = jnp.where(lanes, pltpu.roll(t1, 64, 1), t3)
    second = jnp.where(lanes, pltpu.roll(t5, 64, 1), 0.0)
    return first.astype(BF16), second.astype(BF16)


def gelu_parts(a):
    inner = GELU_COEF * (a + GELU_CUBE * a * a * a)
    t = jnp.tanh(inner)
    return t


def rms_rows(values):
    return lax.rsqrt(jnp.mean(values * values, axis=1, keepdims=True) + EPSILON)


def layer_kernel(
    len_ref, x_ref, dy_ref, w_ref, gain_ref, which_ref,
    out_ref, gt_ref, g_ref, gg_ref,
    bias, xp, dyp, n1, n1t, n2, n2t, dypt, dhbt, qkv, o_all, wo, lse, lse_t, do, dqkv, h, acc,
):
    bins = w_ref.shape[0]
    seq = x_ref.shape[0]
    place = placement(len_ref, bins)
    me = which_ref[0]
    g1 = gain_ref[0:1, :]
    g2 = gain_ref[1:2, :]

    def wo_body(m, c):
        first, second = out_weight_tiles(w_ref, m)
        wo[m, :, 0:128] = first
        wo[m, :, 128:256] = second
        return c

    lax.fori_loop(0, bins, wo_body, 0)
    lse[...] = jnp.zeros_like(lse)

    def forward(b):
        source, segment = packed_source(place, b * CAP, (CAP, 1), 0)
        _, segment_row = packed_source(place, b * CAP, (1, CAP), 1)
        bias[...] = jnp.where(segment == segment_row, 0.0, NEG)
        pick = (source == lax.broadcasted_iota(jnp.int32, (CAP, seq), 1)).astype(BF16)
        xb = nn(pick, x_ref[...])
        xp[...] = xb.astype(BF16)
        dyp[...] = nn(pick, dy_ref[...]).astype(BF16)
        n1[...] = (xb * rms_rows(xb) * g1).astype(BF16)
        h[...] = xb

        def m_body(m, c):
            qkv[m] = nn(n1[...], w_ref[m, :, 0:768]).astype(BF16)
            attend_group(qkv, m, bias, o_all, m, lse)
            h[...] += nt(o_all[m], wo[m])
            return c

        lax.fori_loop(0, bins, m_body, 0)
        hb = h[...]
        n2[...] = (hb * rms_rows(hb) * g2).astype(BF16)

    def ffn_out(b):
        acc[...] = h[...]

        def m_body(m, c):
            a = nn(n2[...], w_ref[m, :, 768:1280])
            up = nn(n2[...], w_ref[m, :, 1280:1792])
            u = (0.5 * a * (1.0 + gelu_parts(a)) * up).astype(BF16)
            acc[...] += nt(u, w_ref[m, :, 1792:2304])
            return c

        lax.fori_loop(0, bins, m_body, 0)
        source, _ = packed_source(place, b * CAP, (1, CAP), 1)
        drop = (lax.broadcasted_iota(jnp.int32, (seq, CAP), 0) == source).astype(BF16)
        out_ref[...] = (out_ref[...].astype(F32) + nn(drop, acc[...].astype(BF16))).astype(BF16)

    out_ref[...] = jnp.zeros_like(out_ref)

    def others(i, c):
        b = lax.rem(me + 1 + i, bins)
        forward(b)
        ffn_out(b)
        return c

    lax.fori_loop(0, bins, others, 0)

    n1t[...] = n1[...].T
    n2t[...] = n2[...].T
    dypt[...] = dyp[...].T
    lse_t[...] = lse[...].T
    acc[...] = jnp.zeros_like(acc)

    def ffn_back(m, c):
        a = nn(n2[...], w_ref[m, :, 768:1280])
        up = nn(n2[...], w_ref[m, :, 1280:1792])
        t = gelu_parts(a)
        gel = 0.5 * a * (1.0 + t)
        u = (gel * up).astype(BF16)
        du = nn(dyp[...], w_ref[m, :, 1792:2304])
        slope = 0.5 * (1.0 + t) + 0.5 * a * (1.0 - t * t) * (GELU_COEF * (1.0 + 3.0 * GELU_CUBE * a * a))
        da = (du * up * slope).astype(BF16)
        db = (du * gel).astype(BF16)
        g_ref[m, :, 1792:2304] = nn(dypt[...], u).astype(BF16)
        g_ref[m, :, 768:1280] = nn(n2t[...], da).astype(BF16)
        g_ref[m, :, 1280:1792] = nn(n2t[...], db).astype(BF16)
        acc[...] += nt(da, w_ref[m, :, 768:1280]) + nt(db, w_ref[m, :, 1280:1792])
        return c

    lax.fori_loop(0, bins, ffn_back, 0)
    hb = h[...]
    r2 = rms_rows(hb)
    dn2 = acc[...]
    gg_ffn = jnp.sum(dn2 * hb * r2, axis=0, keepdims=True)
    wg = dn2 * g2
    dh = dyp[...].astype(F32) + r2 * wg - hb * (r2 * r2 * r2) * jnp.mean(wg * hb, axis=1, keepdims=True)
    h[...] = dh
    dhb = dh.astype(BF16)
    dhbt[...] = dhb.T
    n2[...] = dhb
    acc[...] = jnp.zeros_like(acc)

    def attn_back(m, c):
        do[m] = nn(n2[...], wo[m]).astype(BF16)
        attend_group_back(qkv, m, bias, lse_t, do, m, dqkv)
        acc[...] += nt(dqkv[m], w_ref[m, :, 0:768])
        grad = nn(n1t[...], dqkv[m])
        go = nn(dhbt[...], o_all[m])
        lanes = low_lanes()
        for t in range(6):
            g = grad[:, 128 * t : 128 * (t + 1)]
            if t == 1:
                g = jnp.where(lanes, g, pltpu.roll(go[:, 0:128], 64, 1))
            elif t == 3:
                g = jnp.where(lanes, g, go[:, 0:128])
            elif t == 5:
                g = jnp.where(lanes, g, pltpu.roll(go[:, 128:256], 64, 1))
            g_ref[m, :, 128 * t : 128 * (t + 1)] = g.astype(BF16)
        return c

    lax.fori_loop(0, bins, attn_back, 0)
    xb = xp[...].astype(F32)
    r1 = rms_rows(xb)
    dn1 = acc[...]
    gg_attn = jnp.sum(dn1 * xb * r1, axis=0, keepdims=True)
    wa = dn1 * g1
    gt = h[...] + r1 * wa - xb * (r1 * r1 * r1) * jnp.mean(wa * xb, axis=1, keepdims=True)
    gt_ref[...] = gt.astype(BF16)
    gg_ref[0:1, :] = gg_attn
    gg_ref[1:2, :] = gg_ffn


def unpack_kernel(len_ref, gt_ref, out_ref):
    bins = gt_ref.shape[0]
    seq = out_ref.shape[0]
    place = placement(len_ref, bins)
    total = jnp.zeros(out_ref.shape, F32)
    for b in range(bins):
        source, _ = packed_source(place, b * CAP, (1, CAP), 1)
        drop = (lax.broadcasted_iota(jnp.int32, (seq, CAP), 0) == source).astype(BF16)
        total = total + nn(drop, gt_ref[b])
    out_ref[...] = total


def per_device(
    tokens, lengths, query_weight, key_weight, value_weight, out_weight, attn_gain, gate_weight, up_weight, down_weight,
    ffn_gain, cotangent,
):
    rows, seq, width = tokens.shape
    bins = lax.axis_size("mp")
    q, k, v, o = (w.astype(BF16) for w in (query_weight, key_weight, value_weight, out_weight.T))
    package = jnp.concatenate(
        [q, o[:, 0:64], k, o[:, 64:128], v, o[:, 128:192], gate_weight.astype(BF16), up_weight.astype(BF16),
         down_weight.T.astype(BF16)], axis=1)
    w = lax.all_gather(lax.all_gather(package, "dp", axis=0, tiled=True), "mp", axis=0)
    gains = jnp.stack([attn_gain, ffn_gain]).astype(BF16)
    gains = lax.all_gather(gains, "dp", axis=1, tiled=True).astype(F32)
    gains = jnp.concatenate([gains, jnp.zeros((6, width), F32)], axis=0)
    which = lax.axis_index("mp").astype(jnp.int32).reshape(1)
    vmem = pl.BlockSpec(memory_space=pltpu.VMEM)
    smem = pl.BlockSpec(memory_space=pltpu.SMEM)
    group = w.shape[2]
    x = tokens.reshape(seq, width)
    dy = cotangent.reshape(seq, width)
    out, gt, g, gg = pl.pallas_call(
        layer_kernel,
        out_shape=(
            jax.ShapeDtypeStruct((seq, width), BF16),
            jax.ShapeDtypeStruct((CAP, width), BF16),
            jax.ShapeDtypeStruct((bins, width, group), BF16),
            jax.ShapeDtypeStruct((8, width), F32),
        ),
        in_specs=[smem, vmem, vmem, vmem, vmem, smem],
        out_specs=[vmem] * 4,
        scratch_shapes=[
            pltpu.VMEM((CAP, CAP), F32),
            pltpu.VMEM((CAP, width), BF16),
            pltpu.VMEM((CAP, width), BF16),
            pltpu.VMEM((CAP, width), BF16),
            pltpu.VMEM((width, CAP), BF16),
            pltpu.VMEM((CAP, width), BF16),
            pltpu.VMEM((width, CAP), BF16),
            pltpu.VMEM((width, CAP), BF16),
            pltpu.VMEM((width, CAP), BF16),
            pltpu.VMEM((bins, CAP, width), BF16),
            pltpu.VMEM((bins, CAP, 256), BF16),
            pltpu.VMEM((bins, width, 256), BF16),
            pltpu.VMEM((CAP, 128), F32),
            pltpu.VMEM((128, CAP), F32),
            pltpu.VMEM((bins, CAP, 256), BF16),
            pltpu.VMEM((bins, CAP, width), BF16),
            pltpu.VMEM((CAP, width), F32),
            pltpu.VMEM((CAP, width), F32),
        ],
        compiler_params=pltpu.CompilerParams(vmem_limit_bytes=63 * 2**20+900000),
        name="layer",
    )(lengths, x, dy, w, gains, which)
    gt_all = lax.all_gather(gt, "mp", axis=0)
    grad_tokens = pl.pallas_call(
        unpack_kernel,
        out_shape=jax.ShapeDtypeStruct((seq, width), F32),
        in_specs=[smem, vmem],
        out_specs=vmem,
        compiler_params=pltpu.CompilerParams(vmem_limit_bytes=60 * 2**20),
        name="unpack",
    )(lengths, gt_all)
    g = lax.psum_scatter(g, "mp", scatter_dimension=0, tiled=False)
    g = lax.psum_scatter(g, "dp", scatter_dimension=0, tiled=True).astype(F32)
    gg = lax.psum_scatter(lax.psum(gg[0:2], "mp"), "dp", scatter_dimension=1, tiled=True)
    go = jnp.concatenate([g[:, 192:256], g[:, 448:512], g[:, 704:768]], axis=1).T
    return (
        out.reshape(rows, seq, width),
        grad_tokens.reshape(rows, seq, width),
        g[:, 0:192],
        g[:, 256:448],
        g[:, 512:704],
        go,
        gg[0],
        g[:, 768:1280],
        g[:, 1280:1792],
        g[:, 1792:2304].T,
        gg[1],
    )


MESH = pl.DeviceIdType.MESH
PARTS = ((0, 768), (768, 2304))


class Net:
    def __init__(self):
        self.dp = lax.axis_index("dp")
        self.z = lax.axis_index("mp")
        self.core = lax.rem(self.dp, 2)
        self.chip = lax.div(self.dp, 2)
        self.chip_x = self.chip + 1 - 2 * lax.rem(self.chip, 2)
        self.chip_y = lax.rem(self.chip + 2, 4)
        self.chip_d = 3 - self.chip
        self.sibling = (2 * self.chip + 1 - self.core, self.z)
        self.x = (2 * self.chip_x + self.core, self.z)
        self.y = (2 * self.chip_y + self.core, self.z)

    def up(self, k):
        return (self.dp, lax.rem(self.z + k, 4))

    def along(self, step):
        return (self.dp, lax.rem(self.z + 4 + step, 4))

    def group(self, i):
        z = self.z
        one = jnp.where(z == 0, 1, jnp.where(z == 1, 0, jnp.where(z == 2, 3, 2)))
        two = jnp.where(z < 2, 2, 1)
        return jnp.where(i == 0, z, jnp.where(i == 1, one, jnp.where(i == 2, two, 6 - z - one - two)))


class Gather:
    def __init__(self, net, w, send, recv):
        self.net, self.w, self.send, self.recv = net, w, send, recv

    def copy(self, part, m, chip, core, kind, to, rows=None):
        lo, hi = PARTS[part]
        first, last, mark = (0, 96, 0) if rows is None else (48 * rows, 48 * (rows + 1), 1 + rows)
        ref = self.w.at[m, chip, core, first:last, lo:hi]
        return pltpu.make_async_remote_copy(
            src_ref=ref, dst_ref=ref, send_sem=self.send.at[part, m, chip, kind],
            recv_sem=self.recv.at[part, m, chip, core, mark], device_id=to, device_id_type=MESH)

    def wait(self, part, m, chip, core, rows=None):
        self.copy(part, m, chip, core, 0, self.net.sibling, rows).wait_recv()

    def each_along_z(self, part, m, act):
        net = self.net

        @pl.when(jnp.logical_and(m <= net.z, net.z < 3))
        def _():
            act(self.copy(part, m, net.chip, net.core, 3, net.along(1)))

        @pl.when(jnp.logical_and(m >= net.z, net.z > 0))
        def _():
            act(self.copy(part, m, net.chip, net.core, 4, net.along(-1)))

    def own_copies(self, part, m):
        net = self.net
        return [self.copy(part, m, net.chip, net.core, k, to) for k, to in enumerate((net.x, net.y, net.sibling))]

    def relay_copies(self, part, m):
        net = self.net
        return [
            self.copy(part, m, net.chip_x, net.core, 0, net.y, 0), self.copy(part, m, net.chip_x, net.core, 2, net.sibling),
            self.copy(part, m, net.chip_y, net.core, 1, net.x, 1), self.copy(part, m, net.chip_y, net.core, 2, net.sibling)]

    def along_z(self, part, i):
        net = self.net
        m = net.group(i)
        if not isinstance(i, int) or i > 0:
            self.wait(part, m, net.chip, net.core)
        self.each_along_z(part, m, lambda copy: copy.start())

    def sideways(self, part, i):
        for copy in self.own_copies(part, self.net.group(i)):
            copy.start()

    def spread(self, part, i):
        self.along_z(part, i)
        self.sideways(part, i)

    def relay(self, part, i):
        net = self.net
        m = net.group(i)
        copies = self.relay_copies(part, m)
        for j, chip in enumerate((net.chip_x, net.chip_y)):
            self.wait(part, m, chip, net.core)
            copies[2 * j].start()
            copies[2 * j + 1].start()

    def across(self, part, i):
        net = self.net
        m = net.group(i)
        self.wait(part, m, net.chip_d, net.core, 0)
        self.wait(part, m, net.chip_d, net.core, 1)
        self.copy(part, m, net.chip_d, net.core, 2, net.sibling).start()

    def complete(self, part, i):
        net = self.net
        m = net.group(i)
        for chip in range(4):
            self.wait(part, m, chip, 1 - net.core)

    def drain(self):
        net = self.net
        for part in range(2):

            def body(m, c, part=part):
                self.each_along_z(part, m, lambda copy: copy.wait_send())
                for copy in self.own_copies(part, m) + self.relay_copies(part, m):
                    copy.wait_send()
                self.copy(part, m, net.chip_d, net.core, 2, net.sibling).wait_send()
                return c

            lax.fori_loop(0, 4, body, 0)


class Reduce:
    def __init__(self, net, g, slots, zbuf, sems, ok):
        self.net, self.g, self.slots, self.zbuf, self.sems, self.ok = net, g, slots, zbuf, sems, ok

    def lanes(self, part):
        return slice(*PARTS[part])

    def unit(self, part, m, chip, core, rows=slice(0, 96)):
        return self.g.at[m, chip, core, rows, self.lanes(part)]

    def copy(self, kind, part, key, src, dst, to):
        return pltpu.make_async_remote_copy(
            src_ref=src, dst_ref=dst, send_sem=self.sems.at[0, kind, part, key], recv_sem=self.sems.at[1, kind, part, key],
            device_id=to, device_id_type=MESH)

    def core_copy(self, part, i):
        m = self.net.group(i)
        lo, hi = PARTS[part]
        return self.copy(
            0, part, m, self.g.at[m, :, 1 - self.net.core, :, lo:hi],
            self.slots.at[lax.rem(i, 2), :, :, 0 : hi - lo], self.net.sibling)

    def to_core(self, part, i, credit):
        if credit:
            pl.semaphore_wait(self.ok.at[3, part, self.net.group(i)], 1)
        self.core_copy(part, i).start()

    def from_core(self, part, i, credit):
        net = self.net
        m = net.group(i)
        lo, hi = PARTS[part]
        copy = self.core_copy(part, i)
        copy.wait_recv()
        slot = lax.rem(i, 2)
        for chip in range(4):
            self.g[m, chip, net.core, :, lo:hi] = self.g[m, chip, net.core, :, lo:hi] + self.slots[slot, chip, :, 0 : hi - lo]
        if credit is not None:
            p, j = credit
            pl.semaphore_signal(self.ok.at[3, p, net.group(j)], inc=1, device_id=net.sibling, device_id_type=MESH)
        copy.wait_send()
        pl.semaphore_signal(self.ok.at[0, part, m], inc=1, device_id=net.x, device_id_type=MESH)
        pl.semaphore_signal(self.ok.at[1, part, m], inc=1, device_id=net.y, device_id_type=MESH)

        @pl.when(jnp.logical_and(m >= net.z, net.z > 0))
        def _():
            pl.semaphore_signal(self.ok.at[2, part, m], inc=1, device_id=net.along(-1), device_id_type=MESH)

        @pl.when(jnp.logical_and(m <= net.z, net.z < 3))
        def _():
            pl.semaphore_signal(self.ok.at[2, part, m], inc=1, device_id=net.along(1), device_id_type=MESH)

    def across_copies(self, part, m):
        net = self.net
        out = []
        for kind, rows, to in ((1, slice(0, 48), net.y), (2, slice(48, 96), net.x)):
            out.append(self.copy(
                kind, part, m, self.unit(part, m, net.chip_d, net.core, rows),
                self.unit(part, m, 0, 1 - net.core, rows), to))
        return out

    def side_copies(self, part, m):
        net = self.net
        return [
            self.copy(kind, part, m, self.unit(part, m, chip, net.core), self.unit(part, m, slot, 1 - net.core), to)
            for kind, chip, slot, to in ((3, net.chip_x, 1, net.x), (4, net.chip_y, 2, net.y))]

    def each_z(self, part, m, act):
        net = self.net
        z = net.z
        src = self.unit(part, m, net.chip, net.core)
        far = self.unit(part, m, 3, 1 - net.core)
        lo, hi = PARTS[part]
        near = self.zbuf.at[:, lo:hi]

        def copy(dst, kind, step):
            return pltpu.make_async_remote_copy(
                src_ref=src, dst_ref=dst, send_sem=self.sems.at[0, 5, part, m], recv_sem=self.sems.at[1, kind, part, m],
                device_id=net.along(step), device_id_type=MESH)

        for test, dst, kind, step in ((m > z, far, 5, 1), (m < z - 1, far, 5, -1), (m == z - 1, near, 6, -1)):

            @pl.when(test)
            def _(dst=dst, kind=kind, step=step):
                act(copy(dst, kind, step))

    def z_arrived(self, part, m, near):
        net = self.net
        lo, hi = PARTS[part]
        ref = self.zbuf.at[:, lo:hi] if near else self.unit(part, m, 3, 1 - net.core)
        pltpu.make_async_remote_copy(
            src_ref=ref, dst_ref=ref, send_sem=self.sems.at[0, 5, part, m],
            recv_sem=self.sems.at[1, 6 if near else 5, part, m], device_id=net.sibling, device_id_type=MESH).wait_recv()
        if near:
            mine = self.g[m, net.chip, net.core, :, lo:hi]
            self.g[m, net.chip, net.core, :, lo:hi] = mine + self.zbuf[:, lo:hi]
        else:
            self.add(part, m, net.chip, 3)

    def add(self, part, m, chip, slot, rows=slice(0, 96)):
        net = self.net
        lanes = self.lanes(part)
        self.g[m, chip, net.core, rows, lanes] = self.g[m, chip, net.core, rows, lanes] + self.g[m, slot, 1 - net.core, rows, lanes]

    def start_across(self, part, i):
        m = self.net.group(i)
        pl.semaphore_wait(self.ok.at[0, part, m], 1)
        pl.semaphore_wait(self.ok.at[1, part, m], 1)
        for copy in self.across_copies(part, m):
            copy.start()

    def start_sides(self, part, i):
        net = self.net
        m = net.group(i)
        by_y, by_x = self.across_copies(part, m)
        by_y.wait_recv()
        self.add(part, m, net.chip_x, 0, slice(0, 48))
        by_x.wait_recv()
        self.add(part, m, net.chip_y, 0, slice(48, 96))
        for copy in self.side_copies(part, m):
            copy.start()

    def gather_sides(self, part, i):
        net = self.net
        m = net.group(i)
        for slot, copy in zip((1, 2), self.side_copies(part, m)):
            copy.wait_recv()
            self.add(part, m, net.chip, slot)

    def send_z(self, part, m):
        pl.semaphore_wait(self.ok.at[2, part, m], 1)
        self.each_z(part, m, lambda copy: copy.start())

    def pass_z(self, part, m):
        self.z_arrived(part, m, False)
        self.send_z(part, m)

    def wave(self, part, n):
        z = self.net.z
        for at, groups, act in (
            ((0, (3, 2, 1), self.send_z), (3, (0, 1, 2), self.send_z)),
            ((1, (3, 2), self.pass_z), (2, (0, 1), self.pass_z)),
            ((1, (0,), self.pass_z), (2, (3,), self.pass_z)),
        )[n]:

            @pl.when(z == at)
            def _(groups=groups, act=act):
                for m in groups:
                    act(part, m)

    def step(self, n):
        if n > 0:
            self.start_sides(1 if n < 5 else 0, (n - 1) % 4)
        if n < 8:
            self.start_across(1 if n < 4 else 0, n % 4)

    def total(self, part):
        net = self.net

        @pl.when(net.z > 0)
        def _():
            self.z_arrived(part, net.z, False)

        @pl.when(net.z < 3)
        def _():
            self.z_arrived(part, net.z, True)

        return self.g[net.z, net.chip, net.core, :, self.lanes(part)].astype(F32)

    def drain(self):
        net = self.net
        for part in range(2):

            def body(m, c, part=part):
                for copy in self.across_copies(part, m) + self.side_copies(part, m):
                    copy.wait_send()
                self.each_z(part, m, lambda copy: copy.wait_send())
                return c

            lax.fori_loop(0, 4, body, 0)


def greet(net):
    barrier = pltpu.get_barrier_semaphore()
    for other in range(1, 8):
        pl.semaphore_signal(barrier, inc=1, device_id=(lax.rem(net.dp + other, 8), net.z), device_id_type=MESH)
    for k in range(1, 4):
        pl.semaphore_signal(barrier, inc=1, device_id=net.up(k), device_id_type=MESH)
    return barrier


def share_gains(net, parts, send, recv):
    copies = []
    for k in range(1, 8):
        copies.append(pltpu.make_async_remote_copy(
            src_ref=parts.at[net.dp], dst_ref=parts.at[net.dp], send_sem=send.at[k - 1], recv_sem=recv.at[net.dp],
            device_id=(lax.rem(net.dp + k, 8), net.z), device_id_type=MESH))
        copies[-1].start()
    return copies


def join_gains(net, parts, send, recv, gain):
    for k in range(1, 8):
        other = lax.rem(net.dp + k, 8)
        pltpu.make_async_remote_copy(
            src_ref=parts.at[other], dst_ref=parts.at[other], send_sem=send.at[k - 1], recv_sem=recv.at[other],
            device_id=net.sibling, device_id_type=MESH).wait_recv()
    total = jnp.zeros(gain.shape, F32)
    for d in range(8):
        piece = jnp.concatenate([parts[d], jnp.zeros((8, gain.shape[1] - 128), F32)], axis=1)
        total = total + pltpu.roll(piece, 96 * d, 1)
    gain[...] = total


def build_attn_package(w, net, q_ref, k_ref, v_ref, o_ref):
    lanes = low_lanes()
    ot = o_ref[...].T
    pad = jnp.zeros((96, 64), F32)
    at = (net.z, net.chip, net.core)

    def put(tile, value):
        w[at[0], at[1], at[2], :, 128 * tile : 128 * (tile + 1)] = value.astype(BF16)

    for j, ref in enumerate((q_ref, k_ref, v_ref)):
        put(2 * j, ref[:, 0:128])
        last = jnp.concatenate([ref[:, 128:192], pad], axis=1)
        extra = jnp.concatenate([ot[:, 64 * j : 64 * (j + 1)], pad], axis=1)
        put(2 * j + 1, jnp.where(lanes, last, pltpu.roll(extra, 64, 1)))


def build_ffn_package(w, net, g_ref, u_ref, d_ref):
    at = (net.z, net.chip, net.core)
    w[at[0], at[1], at[2], :, 768:1280] = g_ref[...].astype(BF16)
    w[at[0], at[1], at[2], :, 1280:1792] = u_ref[...].astype(BF16)
    w[at[0], at[1], at[2], :, 1792:2304] = d_ref[...].astype(BF16)


def rows768(ref, m, lo, hi):
    return ref[m, :, :, :, lo:hi].reshape(768, hi - lo)


def put768(ref, m, lo, hi, value):
    ref[m, :, :, :, lo:hi] = value.reshape(4, 2, 96, hi - lo)


class RowGather:
    def __init__(self, net, pool, send, recv, ok):
        self.net, self.pool, self.send, self.recv, self.ok = net, pool, send, recv, ok

    def copy(self, m, way):
        net = self.net
        return pltpu.make_async_remote_copy(
            src_ref=self.pool.at[m], dst_ref=self.pool.at[m], send_sem=self.send.at[way, m], recv_sem=self.recv.at[m],
            device_id=net.along(1 - 2 * way), device_id_type=MESH)

    def each(self, m, act):
        net = self.net

        @pl.when(jnp.logical_and(m <= net.z, net.z < 3))
        def _():
            act(self.copy(m, 0))

        @pl.when(jnp.logical_and(m >= net.z, net.z > 0))
        def _():
            act(self.copy(m, 1))

    def start(self):
        net = self.net
        if self.ok is not None:
            for test, way in ((net.z < 3, 0), (net.z > 0, 1)):

                @pl.when(test)
                def _(way=way):
                    pl.semaphore_signal(self.ok.at[1 - way], inc=1, device_id=net.along(1 - 2 * way), device_id_type=MESH)

        for test, way in ((net.z < 3, 0), (net.z > 0, 1)):

            @pl.when(test)
            def _(way=way):
                if self.ok is not None:
                    pl.semaphore_wait(self.ok.at[way], 1)
                self.copy(net.z, way).start()

    def relay(self, i):
        z = self.net.z
        m = self.net.group(i)

        @pl.when(jnp.logical_and(z > 0, z < 3))
        def _():
            self.copy(m, 0).wait_recv()
            self.each(m, lambda copy: copy.start())

    def arrived(self, i):
        z = self.net.z
        m = self.net.group(i)

        @pl.when(jnp.logical_or(z == 0, z == 3))
        def _():
            self.copy(m, 0).wait_recv()

        return m

    def drain(self):
        def body(m, c):
            self.each(m, lambda copy: copy.wait_send())
            return c

        lax.fori_loop(0, 4, body, 0)


def mega_kernel(
    len_ref, x_ref, dy_ref, q_ref, k_ref, v_ref, o_ref, gate_ref, up_ref, down_ref, ga_ref, gf_ref,
    out_ref, gt_ref, gq_ref, gk_ref, gv_ref, go_ref, gate_grad_ref, up_grad_ref, down_grad_ref, gga_ref, ggf_ref,
    w, g, slots, pool, gain, gain_parts, gg_out, gg_in, gg_z, bias, n1t, n2t, dypt, spare, qkv, hx, o_own, wo, lse, lse_t,
    h, acc, res, zbuf,
    ag_send, ag_recv, gn_send, gn_recv, in_sem, rs_sems, ok, gt_send, gt_recv, gt_ok, hx_send, hx_recv, out_sem, gs_send,
    gs_recv, gz_send, gz_recv,
):
    net = Net()
    bins = 4
    seq = 1536
    me = net.z
    xp, dyp, n1, n2 = (pool.at[j] for j in range(4))
    n_b = spare.at[0]
    barrier = greet(net)
    halves = []
    for t, ref in enumerate((x_ref, dy_ref)):
        for j in range(2):
            halves.append(pltpu.make_async_copy(
                ref.at[j], g.at[t, :, :, :, 768 * j : 768 * (j + 1)], in_sem.at[2 * t + j]))
    for copy in halves:
        copy.start()
    ag = Gather(net, w, ag_send, ag_recv)
    rs = Reduce(net, g, slots, zbuf, rs_sems, ok)
    rows = RowGather(net, pool, gt_send, gt_recv, gt_ok)
    mids = RowGather(net, hx, hx_send, hx_recv, None)
    build_attn_package(w, net, q_ref, k_ref, v_ref, o_ref)
    pl.semaphore_wait(barrier, 10)
    ag.spread(0, 0)
    build_ffn_package(w, net, gate_ref, up_ref, down_ref)
    pad = jnp.zeros((1, 32), F32)
    mine = jnp.concatenate([
        jnp.concatenate([ga_ref[...], pad], axis=1), jnp.concatenate([gf_ref[...], pad], axis=1),
        jnp.zeros((6, 128), F32)], axis=0)
    gain_parts[net.dp] = mine.astype(BF16).astype(F32)
    gain_copies = share_gains(net, gain_parts, gn_send, gn_recv)

    place = placement(len_ref, bins)
    lse[...] = jnp.zeros_like(lse)

    def set_bias(b):
        _, segment = packed_source(place, b * CAP, (CAP, 1), 0)
        _, segment_row = packed_source(place, b * CAP, (1, CAP), 1)
        bias[...] = jnp.where(segment == segment_row, 0.0, NEG)

    def pack(b, t, store):
        def body(j, c):
            source, _ = packed_source(place, b * CAP + j * 128, (128, 1), 0)
            pick = (source == lax.broadcasted_iota(jnp.int32, (128, seq), 1)).astype(BF16)
            value = nn(pick[:, 0:768], rows768(g, t, 0, 768)) + nn(pick[:, 768:1536], rows768(g, t, 768, 1536))
            store(pl.ds(pl.multiple_of(j * 128, 128), 128), value)
            return c

        lax.fori_loop(0, CAP // 128, body, 0)

    def drops(b, first, rows, count=1):
        source, _ = packed_source(place, b * CAP, (1, count * CAP), 1)
        return (lax.broadcasted_iota(jnp.int32, (rows, count * CAP), 0) + first == source).astype(BF16)

    def norm(src, dst, gain_row):
        def body(j, c):
            at = pl.ds(pl.multiple_of(j * 128, 128), 128)
            values = src[at, :]
            dst[at, :] = (values * rms_rows(values) * gain_row).astype(BF16)
            return c

        lax.fori_loop(0, CAP // 128, body, 0)

    for copy in halves:
        copy.wait()
    def store_x(at, value):
        xp[at, :] = value.astype(BF16)
        h[at, :] = value

    def store_dy(at, value):
        dyp[at, :] = value.astype(BF16)

    pack(me, 0, store_x)
    ag.spread(0, 1)
    ag.relay(0, 0)
    pack(me, 1, store_dy)
    join_gains(net, gain_parts, gn_send, gn_recv, gain)
    g1 = gain[0:1, :]
    g2 = gain[1:2, :]
    ag.spread(0, 2)
    ag.relay(0, 1)
    ag.across(0, 0)
    norm(h, n1, g1)
    n1t[...] = n1[...].T
    dypt[...] = dyp[...].T

    set_bias(me)
    ag.spread(0, 3)
    ag.relay(0, 2)
    ag.across(0, 1)
    ag.along_z(1, 0)
    ag.relay(0, 3)
    ag.across(0, 2)
    ag.sideways(1, 0)
    ag.across(0, 3)
    ag.along_z(1, 1)
    ag.sideways(1, 1)

    def own_forward(i, c):
        m = net.group(i)
        ag.complete(0, i)
        first, second = out_weight_tiles_at(w, m)
        wo[m, :, 0:128] = first
        wo[m, :, 128:256] = second
        qkv[m] = nn(n1[...], rows768(w, m, 0, 768)).astype(BF16)
        attend_group(qkv, m, bias, o_own, m, lse)
        h[...] += nt(o_own[m], wo[m])

        @pl.when(i == 0)
        def _():
            ag.along_z(1, 2)

        @pl.when(i == 1)
        def _():
            ag.relay(1, 0)
            ag.sideways(1, 2)

        @pl.when(i == 3)
        def _():
            ag.along_z(1, 3)
            ag.relay(1, 1)
            ag.across(1, 0)
            ag.sideways(1, 3)

        return c

    lax.fori_loop(0, 4, own_forward, 0)
    hx[me] = h[...].astype(BF16)
    mids.start()
    norm(h, n2, g2)
    n2t[...] = n2[...].T
    lse_t[...] = lse[...].T[0:16, :]
    acc[...] = jnp.zeros_like(acc)
    res[...] = h[...]

    def ffn_back(i, c):
        @pl.when(i == 1)
        def _():
            ag.relay(1, 2)
            ag.across(1, 1)

        @pl.when(i == 2)
        def _():
            ag.relay(1, 3)
            ag.across(1, 2)
            mids.relay(1)
            mids.relay(2)

        @pl.when(i == 3)
        def _():
            ag.across(1, 3)
            rs.step(0)

        m = net.group(i)
        ag.complete(1, i)

        @pl.when(i == 3)
        def _():
            rs.step(1)

        for lo in (0, 256):
            w_gate = rows768(w, m, 768 + lo, 1024 + lo)
            w_up = rows768(w, m, 1280 + lo, 1536 + lo)
            w_down = rows768(w, m, 1792 + lo, 2048 + lo)
            a = nn(n2[...], w_gate)
            up = nn(n2[...], w_up)
            t = gelu_parts(a)
            gel = 0.5 * a * (1.0 + t)
            u = (gel * up).astype(BF16)
            res[...] += nt(u, w_down)
            put768(g, m, 1792 + lo, 2048 + lo, nn(dypt[...], u).astype(BF16))
            du = nn(dyp[...], w_down)
            slope = 0.5 * (1.0 + t) + 0.5 * a * (1.0 - t * t) * (GELU_COEF * (1.0 + 3.0 * GELU_CUBE * a * a))
            da = (du * up * slope).astype(BF16)
            db = (du * gel).astype(BF16)
            put768(g, m, 768 + lo, 1024 + lo, nn(n2t[...], da).astype(BF16))
            put768(g, m, 1280 + lo, 1536 + lo, nn(n2t[...], db).astype(BF16))
            acc[...] += nt(da, w_gate) + nt(db, w_up)

        @pl.when(i < 2)
        def _():
            rs.to_core(1, i, False)

        @pl.when(i >= 2)
        def _():
            rs.to_core(1, i, True)

        @pl.when(jnp.logical_and(i >= 1, i < 3))
        def _():
            rs.from_core(1, i - 1, (1, i + 1))

        @pl.when(i == 3)
        def _():
            rs.from_core(1, 2, (0, 0))

        return c

    lax.fori_loop(0, 4, ffn_back, 0)

    def hidden_back(j, total):
        at = pl.ds(pl.multiple_of(j * 128, 128), 128)
        ho = h[at, :]
        r2 = rms_rows(ho)
        dn2 = acc[at, :]
        wg = dn2 * g2
        dh = dyp[at, :].astype(F32) + r2 * wg - ho * (r2 * r2 * r2) * jnp.mean(wg * ho, axis=1, keepdims=True)
        h[at, :] = dh
        n2[at, :] = dh.astype(BF16)
        acc[at, :] = jnp.zeros_like(dh)
        return total + jnp.sum(dn2 * ho * r2, axis=0, keepdims=True)

    gg_ffn = lax.fori_loop(0, CAP // 128, hidden_back, jnp.zeros((1, 768), F32))
    n2t[...] = n2[...].T
    rs.from_core(1, 3, (0, 1))

    def attn_back(i, c):
        m = net.group(i)
        spare[0, :, 0:256] = nn(n2[...], wo[m]).astype(BF16)
        attend_group_back(qkv, m, bias, lse_t, spare, 0, qkv)
        acc[...] += nt(qkv[m], rows768(w, m, 0, 768))

        @pl.when(i == 0)
        def _():
            mids.relay(3)

        @pl.when(i == 0)
        def _():
            rs.step(2)

        @pl.when(i == 3)
        def _():
            rs.step(3)

        @pl.when(i == 2)
        def _():
            rs.gather_sides(1, 0)

        return c

    lax.fori_loop(0, 4, attn_back, 0)

    def input_back(j, total):
        at = pl.ds(pl.multiple_of(j * 128, 128), 128)
        xb = xp[at, :].astype(F32)
        r1 = rms_rows(xb)
        dn1 = acc[at, :]
        wa = dn1 * g1
        gt = h[at, :] + r1 * wa - xb * (r1 * r1 * r1) * jnp.mean(wa * xb, axis=1, keepdims=True)
        n_b[at, :] = gt.astype(BF16)
        return total + jnp.sum(dn1 * xb * r1, axis=0, keepdims=True)

    gg_attn = lax.fori_loop(0, CAP // 128, input_back, jnp.zeros((1, 768), F32))
    pool[me] = n_b[...]
    rows.start()
    gg = jnp.concatenate([gg_attn, gg_ffn, jnp.zeros((6, 768), F32)], axis=0)
    for d in range(8):
        gg_out[d] = pltpu.roll(gg, (768 - 96 * d) % 768, 1)[:, 0:128] if d else gg[:, 0:128]

    def gg_copy(k):
        to = lax.rem(net.dp + k, 8)
        return pltpu.make_async_remote_copy(
            src_ref=gg_out.at[to], dst_ref=gg_in.at[net.dp], send_sem=gs_send.at[k - 1], recv_sem=gs_recv.at[net.dp],
            device_id=(to, net.z), device_id_type=MESH)

    for k in range(1, 8):
        gg_copy(k).start()

    def attn_grads(i, c):
        m = net.group(i)
        go = nn(n2t[...], o_own[m])
        lanes = low_lanes()
        for j in range(3):
            grad = nn(n1t[...], qkv[m, :, 256 * j : 256 * (j + 1)])
            put768(g, m, 256 * j, 256 * j + 128, grad[:, 0:128].astype(BF16))
            if j == 1:
                extra = go[:, 0:128]
            else:
                extra = pltpu.roll(go[:, 64 * j : 64 * j + 128], 64, 1)
            put768(g, m, 256 * j + 128, 256 * (j + 1), jnp.where(lanes, grad[:, 128:256], extra).astype(BF16))

        rs.to_core(0, i, True)

        @pl.when(jnp.logical_and(i >= 1, i < 3))
        def _():
            rs.from_core(0, i - 1, (0, i + 1))

        @pl.when(i == 3)
        def _():
            rs.from_core(0, 2, None)
            rs.gather_sides(1, 1)

        return c

    lax.fori_loop(0, 4, attn_grads, 0)
    rs.from_core(0, 3, None)
    rs.step(4)

    part = gg_out[net.dp]
    for k in range(1, 8):
        other = lax.rem(net.dp + k, 8)
        pltpu.make_async_remote_copy(
            src_ref=gg_out.at[other], dst_ref=gg_in.at[other], send_sem=gs_send.at[k - 1], recv_sem=gs_recv.at[other],
            device_id=net.sibling, device_id_type=MESH).wait_recv()
        part = part + gg_in[other]
    gg_z[me] = part
    gz_copies = [pltpu.make_async_remote_copy(
        src_ref=gg_z.at[me], dst_ref=gg_z.at[me], send_sem=gz_send.at[k - 1], recv_sem=gz_recv.at[me],
        device_id=net.up(k), device_id_type=MESH) for k in range(1, 4)]
    for copy in gz_copies:
        copy.start()

    mids.drain()
    hx[me] = res[...].astype(BF16)

    def ffn_out(j, c):
        b = mids.arrived(j)
        acc[...] = hx[b].astype(F32)
        norm(acc, n_b, g2)

        def ffn(m, c):
            a = nn(n_b[...], rows768(w, m, 768, 1280))
            up = nn(n_b[...], rows768(w, m, 1280, 1792))
            u = (0.5 * a * (1.0 + gelu_parts(a)) * up).astype(BF16)
            acc[...] += nt(u, rows768(w, m, 1792, 2304))

            @pl.when(jnp.logical_and(j == 2, m == 0))
            def _():
                rows.relay(1)
                rows.relay(2)

            @pl.when(jnp.logical_and(j == 1, m == 3))
            def _():
                rs.step(5)
                rs.gather_sides(1, 2)

            @pl.when(jnp.logical_and(j == 2, m == 1))
            def _():
                rs.step(6)
                rs.gather_sides(1, 3)

            @pl.when(jnp.logical_and(j == 3, m == 1))
            def _():
                rs.step(8)

            return c

        lax.fori_loop(0, 4, ffn, 0)
        hx[b] = acc[...].astype(BF16)

        @pl.when(j == 2)
        def _():
            rs.wave(1, 0)
            rs.step(7)

        @pl.when(j == 3)
        def _():
            rows.relay(3)

        return c

    lax.fori_loop(1, 4, ffn_out, 0)
    for i in range(4):
        rs.gather_sides(0, i)
    rs.wave(0, 0)
    rs.wave(1, 1)

    def place_out(j, c):
        at = pl.ds(pl.multiple_of(j * 256, 256), 256)
        pick = drops(0, j * 256, 256, 4)
        out_ref[at, :] = nn(pick, hx[...].reshape(4 * CAP, 768)).astype(BF16)
        return c

    lax.fori_loop(0, seq // 256, place_out, 0)

    def place_rows(bs, first):
        def body(j, c):
            value = nn(drops(bs[0], CAP * j, CAP), pool[bs[0]])
            for b in bs[1:]:
                value = value + nn(drops(b, CAP * j, CAP), pool[b])
            if not first:
                value = value + qkv[j].astype(F32)
            qkv[j] = value.astype(BF16)
            return c

        lax.fori_loop(0, 3, body, 0)

    place_rows([me, rows.arrived(1), rows.arrived(2)], True)
    rs.wave(1, 2)
    rs.wave(0, 1)
    ffn_sum = rs.total(1)
    gate_grad_ref[...] = ffn_sum[:, 0:512]
    up_grad_ref[...] = ffn_sum[:, 512:1024]
    down_grad_ref[...] = ffn_sum[:, 1024:1536]
    rs.wave(0, 2)
    place_rows([rows.arrived(3)], False)
    out = pltpu.make_async_copy(qkv.at[0:3], gt_ref, out_sem)
    out.start()

    for k in range(1, 4):
        other = lax.rem(me + k, 4)
        pltpu.make_async_remote_copy(
            src_ref=gg_z.at[other], dst_ref=gg_z.at[other], send_sem=gz_send.at[k - 1], recv_sem=gz_recv.at[other],
            device_id=net.up(k), device_id_type=MESH).wait_recv()
        part = part + gg_z[other]
    gga_ref[...] = part[0:1, 0:96]
    ggf_ref[...] = part[1:2, 0:96]
    attn_sum = rs.total(0)
    gq_ref[...] = attn_sum[:, 0:192]
    gk_ref[...] = attn_sum[:, 256:448]
    gv_ref[...] = attn_sum[:, 512:704]
    go_ref[...] = jnp.concatenate([attn_sum[:, 192:256], attn_sum[:, 448:512], attn_sum[:, 704:768]], axis=1).T
    out.wait()
    for copy in gain_copies + gz_copies:
        copy.wait_send()
    for k in range(1, 8):
        gg_copy(k).wait_send()
    rows.drain()
    rs.drain()
    ag.drain()


def finish_kernel(*refs):
    count = len(refs) // 2
    refs[count][...] = refs[0][...].astype(F32)
    refs[count + 1][...] = refs[1][...]

    @pl.when(pl.program_id(0) == 0)
    def _():
        for j in range(2, count):
            refs[count + j][...] = refs[j][...]


def out_weight_tiles_at(w, m):
    lanes = low_lanes()
    t1 = rows768(w, m, 128, 256).astype(F32)
    t3 = rows768(w, m, 384, 512).astype(F32)
    t5 = rows768(w, m, 640, 768).astype(F32)
    first = jnp.where(lanes, pltpu.roll(t1, 64, 1), t3)
    second = jnp.where(lanes, pltpu.roll(t5, 64, 1), 0.0)
    return first.astype(BF16), second.astype(BF16)


def on_this_slice(
    tokens, lengths, query_weight, key_weight, value_weight, out_weight, attn_gain, gate_weight, up_weight, down_weight,
    ffn_gain, cotangent,
):
    rows, seq, width = tokens.shape
    vmem = pl.BlockSpec(memory_space=pltpu.VMEM)
    smem = pl.BlockSpec(memory_space=pltpu.SMEM)
    dma = pltpu.SemaphoreType.DMA
    act = pltpu.VMEM((CAP, width), BF16)
    act_t = pltpu.VMEM((width, CAP), BF16)
    wide = pltpu.VMEM((CAP, width), F32)
    hbm = pl.BlockSpec(memory_space=pl.ANY)

    def f32(*shape):
        return jax.ShapeDtypeStruct(shape, F32)

    out, gt, gq, gk, gv, go, gate, up, down, gain_a, gain_f = pl.pallas_call(
        mega_kernel,
        out_shape=(
            jax.ShapeDtypeStruct((seq, width), BF16), jax.ShapeDtypeStruct((3, CAP, width), BF16),
            f32(96, 192), f32(96, 192), f32(96, 192), f32(192, 96), f32(96, 512), f32(96, 512), f32(96, 512), f32(1, 96), f32(1, 96),
        ),
        in_specs=[smem, hbm, hbm] + [vmem] * 9,
        out_specs=[vmem, hbm] + [vmem] * 9,
        scratch_shapes=[
            pltpu.VMEM((4, 4, 2, 96, 2304), BF16),
            pltpu.VMEM((4, 4, 2, 96, 2304), BF16),
            pltpu.VMEM((2, 4, 96, 1536), BF16),
            pltpu.VMEM((4, CAP, width), BF16),
            pltpu.VMEM((8, width), F32),
            pltpu.VMEM((8, 8, 128), F32), pltpu.VMEM((8, 8, 128), F32), pltpu.VMEM((8, 8, 128), F32),
            pltpu.VMEM((4, 8, 128), F32),
            pltpu.VMEM((CAP, CAP), F32),
            act_t, act_t, act_t, pltpu.VMEM((1, CAP, width), BF16),
            pltpu.VMEM((4, CAP, width), BF16),
            pltpu.VMEM((4, CAP, width), BF16),
            pltpu.VMEM((4, CAP, 256), BF16),
            pltpu.VMEM((4, width, 256), BF16),
            pltpu.VMEM((CAP, 128), F32),
            pltpu.VMEM((16, CAP), F32),
            wide, wide, wide,
            pltpu.VMEM((96, 2304), BF16),
            dma((2, 4, 4, 5)), dma((2, 4, 4, 2, 3)), dma((7,)), dma((8,)), dma((4,)),
            dma((2, 7, 2, 4)), pltpu.SemaphoreType.REGULAR((4, 2, 4)),
            dma((2, 4)), dma((4,)), pltpu.SemaphoreType.REGULAR((2,)), dma((2, 4)), dma((4,)), dma, dma((7,)), dma((8,)), dma((3,)), dma((4,)),
        ],
        compiler_params=pltpu.CompilerParams(
            vmem_limit_bytes=60 * 2**20, collective_id=0, has_side_effects=True),
        name="layer",
    )(lengths, tokens.reshape(2, 4, 2, 96, width), cotangent.reshape(2, 4, 2, 96, width), query_weight, key_weight,
      value_weight, out_weight, gate_weight, up_weight, down_weight.T, attn_gain.reshape(1, 96), ffn_gain.reshape(1, 96))
    rest = (out, gq, gk, gv, go, gate, up, down, gain_a, gain_f)
    block = pl.BlockSpec((512, width), lambda i: (i, 0))
    whole = [pl.BlockSpec(a.shape, lambda i: (0, 0)) for a in rest[1:]]
    gt, out, gq, gk, gv, go, gate, up, down, gain_a, gain_f = pl.pallas_call(
        finish_kernel,
        grid=(seq // 512,),
        out_shape=(f32(seq, width),) + tuple(jax.ShapeDtypeStruct(a.shape, a.dtype) for a in rest),
        in_specs=[block, block] + whole,
        out_specs=(block, block) + tuple(whole),
        name="finish",
    )(gt.reshape(seq, width), *rest)
    return (
        out.reshape(rows, seq, width), gt.reshape(rows, seq, width), gq, gk, gv, go, gain_a.reshape(96), gate, up, down.T,
        gain_f.reshape(96),
    )
def solution(mesh):
    body = on_this_slice if dict(mesh.shape) == {"dp": 8, "mp": 4} else per_device
    return jax.shard_map(
        body,
        mesh=mesh,
        in_specs=(
            P("dp", None, None), P("dp", None), P("dp", "mp"), P("dp", "mp"), P("dp", "mp"), P("mp", "dp"), P("dp"),
            P("dp", "mp"), P("dp", "mp"), P("mp", "dp"), P("dp"), P("dp", None, None),
        ),
        out_specs=(
            P("dp", None, None), P("dp", None, None), P("dp", "mp"), P("dp", "mp"), P("dp", "mp"), P("mp", "dp"),
            P("dp"), P("dp", "mp"), P("dp", "mp"), P("mp", "dp"), P("dp"),
        ),
        check_vma=False,
    )
```
